256 devices in a mesh: row: 4 (over z_hi), col: 64 (over x, y, z_lo, core).
Axes of the slice: x: 4, y: 4, z: 8 (z_hi: 4, z_lo: 2; z = z_hi * 2 + z_lo), core: 2. Of those that a mesh axis runs over, the one named last changes fastest.
Arguments:
- object_field: float32 [2, 2048, 32768], P(None, 'row', 'col'), may hold values from -6 to 6
- probe_modes: float32 [2, 2, 128, 128], replicated, may hold values from -5 to 5
- photons: bfloat16 [4, 64, 64, 128, 128], P('row', 'col'), may hold values from 0.099609375 to 10
- positions: int32 [4, 64, 64, 2], P('row', 'col'), may hold values from 0 to 511, as said below
- counts: int32 [4, 64], P('row', 'col'), may hold values from 8 to 64, as said below
Outputs:
- object_gradient: float32 [2, 2048, 32768], P(None, 'row', 'col')
- probe_gradient: float32 [2, 2, 128, 128], replicated
The draws below stay inside these ranges and needn't reach their ends.
Inputs may be any that keep to these rules, and one draw needn't show every extreme that they name: `positions`: each tile's offsets lie inside that tile; slots at or beyond the tile's count hold offsets that are ignored. `counts`: some tile has all 64 slots valid and some has 8; most tiles have few.
All inputs are finite; a program needn't handle non-finite values.
Results may differ from the reference program's by a relative error of at most 0.0012.
The reference program's roundings to bfloat16 on the way count: a program that leaves them out, or rounds other values in their place, can miss the bound.
Values sent between devices are 32-bit elements; how exact they have to be, the bound alone decides.
No kernel may reach another device: no remote copies, remote signals or barrier semaphores. Data moves between devices by JAX's collectives and lax.ppermute only.
A program may use at most 64 MiB of HBM per device.

```python
import math
import jax
import jax.numpy as jnp
from jax import lax

PATCH = 128
MODES = 2
TILE_R = 512
TILE_C = 512
SLOTS = 64
ROWS = 2048
COLS = 32768
N_ROW = 4
N_COL = 64


def draw_positions(key, part):
    key = jax.random.fold_in(key, 11)
    key_row, key_col = jax.random.split(key)
    row_offset = jax.random.randint(key_row, (N_ROW, N_COL, SLOTS, 1), 0, TILE_R, dtype=jnp.int32)
    col_offset = jax.random.randint(key_col, (N_ROW, N_COL, SLOTS, 1), 0, TILE_C, dtype=jnp.int32)
    placed = jnp.concatenate([row_offset, col_offset], axis=-1)
    placed = placed.at[0, 0, 0].set(jnp.array([TILE_R - 1, TILE_C - 1], jnp.int32))
    placed = placed.at[0, 0, 1].set(jnp.array([0, 0], jnp.int32))
    return placed


def draw_counts(key, part):
    key = jax.random.fold_in(key, 23)
    key_raw, key_top, key_low = jax.random.split(key, 3)
    tiles = N_ROW * N_COL
    spread = SLOTS - 8
    raw = jax.random.randint(key_raw, (tiles,), 0, spread + 1, dtype=jnp.int32)
    filled = 8 + raw * raw * raw // (spread * spread)
    busiest = jax.random.randint(key_top, (), 0, tiles, dtype=jnp.int32)
    lightest = (busiest + 1 + jax.random.randint(key_low, (), 0, tiles - 1, dtype=jnp.int32)) % tiles
    filled = filled.at[busiest].set(SLOTS)
    filled = filled.at[lightest].set(8)
    return filled.reshape(N_ROW, N_COL)


def level_of(rng, extent, cuts, low, largest):
    loudness = 1.0
    for dim, shards_of in cuts:
        heights = jax.random.uniform(jax.random.fold_in(jax.random.fold_in(rng, 6), dim), (shards_of,), jnp.float32, low / len(cuts), largest / len(cuts))
        loudness = loudness * jnp.repeat(jnp.exp(heights), extent[dim] // shards_of).reshape((-1,) + (1,) * (len(extent) - 1 - dim))
    return loudness


def noise(rng, dims, deviation, bound, pieces=(), kind=jnp.bfloat16):
    loudness = level_of(rng, dims, pieces, -0.22, 0.18) if pieces else 1.0
    values = jax.random.normal(rng, dims, jnp.float32) * deviation * loudness
    return jnp.minimum(jnp.maximum(values, -bound), bound).astype(kind)


def setup_inputs(seed: int = 0) -> dict:
    splits = jax.random.split(jax.random.key(seed), 6)
    return {
        "object_field": noise(splits[0], (2, ROWS, COLS), 1.0, 6.0, ((1, 4), (2, 64)), jnp.float32),
        "probe_modes": noise(splits[1], (2, MODES, PATCH, PATCH), 0.7, 5.0, (), jnp.float32),
        "photons": jnp.clip(jnp.exp(math.log(10.0) - 4.609084 * jax.random.uniform(splits[2], (N_ROW, N_COL, SLOTS, PATCH, PATCH), jnp.float32) ** level_of(splits[2], (N_ROW, N_COL, SLOTS, PATCH, PATCH), ((0, 4), (1, 64)), -0.2, 0.2)), 0.099609375, 10.0).astype(jnp.bfloat16),
        "positions": draw_positions(jax.random.fold_in(splits[5], 71), 0),
        "counts": draw_counts(jax.random.fold_in(splits[5], 71), 0),
    }


def fourier_tables(patch_len):
    index_range = jnp.arange(patch_len, dtype=jnp.int32)
    product = index_range[:, None] * index_range[None, :] % patch_len
    angle = product.astype(jnp.float32) * (2.0 * math.pi / patch_len)
    cosine = jnp.cos(angle) / math.sqrt(patch_len)
    sine_part = jnp.sin(angle) / math.sqrt(patch_len)
    plus_table = jnp.concatenate([jnp.concatenate([cosine, sine_part], 1), jnp.concatenate([-sine_part, cosine], 1)], 0)
    minus_table = jnp.concatenate([jnp.concatenate([cosine, -sine_part], 1), jnp.concatenate([sine_part, cosine], 1)], 0)
    return (plus_table.astype(jnp.bfloat16), minus_table.astype(jnp.bfloat16))

def wave_gradient(patches, photon_block, valid, probe_modes, plus_table, minus_table):
    batch, _, patch_len, _ = patches.shape
    modes = probe_modes.shape[1]
    object_real = patches[:, 0][:, None]
    object_imaginary = patches[:, 1][:, None]
    probe_real = probe_modes[0][None]
    probe_imaginary = probe_modes[1][None]
    wave_real = probe_real * object_real - probe_imaginary * object_imaginary
    wave_imaginary = probe_real * object_imaginary + probe_imaginary * object_real
    stacked = jnp.concatenate([wave_real, wave_imaginary], axis=2).astype(jnp.bfloat16)
    first_pass = jnp.einsum('ik,bmkj->bmij', plus_table.astype(jnp.float32), stacked.astype(jnp.float32)).astype(jnp.bfloat16)
    turned = first_pass.reshape(batch, modes, 2, patch_len, patch_len).transpose(0, 1, 3, 2, 4).reshape(batch, modes, patch_len, 2 * patch_len)
    far_field = jnp.einsum('bmik,kj->bmij', turned.astype(jnp.float32), minus_table.astype(jnp.float32))
    power = lax.optimization_barrier(jnp.sum(far_field * far_field, axis=1))
    intensity = power[..., :patch_len] + power[..., patch_len:]
    factor = (1.0 - photon_block.astype(jnp.float32) / (intensity + 1.0)) * valid[:, None, None]
    scaled = (far_field * jnp.concatenate([factor, factor], -1)[:, None]).astype(jnp.bfloat16)
    back_pass = jnp.einsum('bmik,kj->bmij', scaled.astype(jnp.float32), plus_table.astype(jnp.float32)).astype(jnp.bfloat16)
    unturned = back_pass.reshape(batch, modes, patch_len, 2, patch_len).transpose(0, 1, 3, 2, 4).reshape(batch, modes, 2 * patch_len, patch_len)
    exit_grad = jnp.einsum('ik,bmkj->bmij', minus_table.astype(jnp.float32), unturned.astype(jnp.float32))
    exit_real = exit_grad[:, :, :patch_len]
    exit_imaginary = exit_grad[:, :, patch_len:]
    patch_real = lax.optimization_barrier(jnp.sum(probe_real * exit_real + probe_imaginary * exit_imaginary, axis=1))
    patch_imaginary = lax.optimization_barrier(jnp.sum(probe_real * exit_imaginary - probe_imaginary * exit_real, axis=1))
    patch_gradient = jnp.stack([patch_real, patch_imaginary], axis=1)
    mode_real = lax.optimization_barrier(jnp.sum(object_real * exit_real + object_imaginary * exit_imaginary, axis=0))
    mode_imaginary = lax.optimization_barrier(jnp.sum(object_real * exit_imaginary - object_imaginary * exit_real, axis=0))
    return (patch_gradient, jnp.stack([mode_real, mode_imaginary], axis=0))

def take_patches(field, row_start, col_start, patch_len):
    zero_index = jnp.zeros((), jnp.int32)
    return jax.vmap(lambda r, c: lax.dynamic_slice(field, (zero_index, r, c), (2, patch_len, patch_len)))(row_start, col_start)

def add_patches(gradient, patch_gradient, row_start, col_start):
    patch_len = patch_gradient.shape[-1]
    zero_index = jnp.zeros((), jnp.int32)
    for k in range(patch_gradient.shape[0]):
        corner_at = (zero_index, row_start[k], col_start[k])
        present = lax.dynamic_slice(gradient, corner_at, (2, patch_len, patch_len))
        gradient = lax.dynamic_update_slice(gradient, present + patch_gradient[k], corner_at)
    return gradient

def own_slots(gradient, probe_sum, field, photon_rows, row_start, col_start, low_slot, high_slot, probe_modes, plus_table, minus_table):
    patch_len = probe_modes.shape[-1]

    def block_step(k, carry):
        grad_now, probe_now = carry
        start = (k * 8).astype(jnp.int32)
        row_block = lax.dynamic_slice_in_dim(row_start, start, 8)
        col_block = lax.dynamic_slice_in_dim(col_start, start, 8)
        slot_ids = start + jnp.arange(8, dtype=jnp.int32)
        valid = ((slot_ids >= low_slot) & (slot_ids < high_slot)).astype(jnp.float32)
        patches = take_patches(field, row_block, col_block, patch_len)
        photon_block = lax.dynamic_slice_in_dim(photon_rows, start, 8)
        patch_gradient, probe_part = wave_gradient(patches, photon_block, valid, probe_modes, plus_table, minus_table)
        return (add_patches(grad_now, patch_gradient, row_block, col_block), probe_now + probe_part)
    return lax.fori_loop(low_slot // 8, (high_slot + 7) // 8, block_step, (gradient, probe_sum))

def reference(object_field, probe_modes, photons, positions, counts):
    patch_len = probe_modes.shape[-1]
    total_rows = object_field.shape[1]
    total_cols = object_field.shape[2]
    tile_rows = total_rows // N_ROW
    tile_cols = total_cols // N_COL
    plus_table, minus_table = fourier_tables(patch_len)
    padded = jnp.pad(object_field, ((0, 0), (0, patch_len), (0, patch_len)))

    def device_step(carry, index):
        gradient, probe_sum = carry
        tile_row = index // N_COL
        tile_col = index % N_COL
        offsets = positions[tile_row, tile_col]
        row_start = (tile_row * tile_rows + offsets[:, 0]).astype(jnp.int32)
        col_start = (tile_col * tile_cols + offsets[:, 1]).astype(jnp.int32)
        count_here = counts[tile_row, tile_col].astype(jnp.int32)
        photon_rows = photons[tile_row, tile_col]
        gradient, probe_sum = own_slots(gradient, probe_sum, padded, photon_rows, row_start, col_start, jnp.zeros((), jnp.int32), count_here, probe_modes, plus_table, minus_table)
        return ((gradient, probe_sum), None)
    start_carry = (jnp.zeros(padded.shape, jnp.float32), jnp.zeros(probe_modes.shape, jnp.float32))
    (gradient, probe_sum), _ = lax.scan(device_step, start_carry, jnp.arange(N_ROW * N_COL, dtype=jnp.int32))
    object_gradient = gradient[:, :total_rows, :total_cols]
    probe_gradient = probe_sum / math.sqrt(N_ROW * N_COL * SLOTS)
    return (object_gradient, probe_gradient)
```

```python
import math

import jax
import jax.numpy as jnp
import numpy as np
from jax import lax
from jax.experimental import pallas as pl
from jax.experimental.pallas import tpu as pltpu
from jax.sharding import PartitionSpec as P

F32 = jnp.float32
BF16 = jnp.bfloat16
PATCH = 128
BLOCK = 4
BOTH = ("row", "col")


def fourier_tables(patch_len):
    index_range = np.arange(patch_len)
    product = (index_range[:, None] * index_range[None, :]) % patch_len
    angle = product.astype(np.float32) * np.float32(2.0 * math.pi / patch_len)
    cosine = (np.cos(angle) / np.float32(math.sqrt(patch_len))).astype(np.float32)
    sine = (np.sin(angle) / np.float32(math.sqrt(patch_len))).astype(np.float32)
    plus_table = np.block([[cosine, sine], [-sine, cosine]])
    minus_table = np.block([[cosine, -sine], [sine, cosine]])
    return jnp.asarray(plus_table, BF16), jnp.asarray(minus_table, BF16)


def dot(a, b):
    return jnp.dot(a, b, preferred_element_type=F32)


def slot_block(slots, valids, pos, field, grad, photons, probe, probe_sum, plus_ref, minus_ref):
    n = len(slots)
    lane = lax.broadcasted_iota(jnp.int32, (PATCH, PATCH), 1)
    plus = plus_ref[...]
    minus = minus_ref[...]
    places, patches, waves = [], [], []
    for s in slots:
        top = pos[0, s]
        left = pos[1, s]
        tile = left // PATCH
        shift = left % PATCH
        back = (PATCH - shift) % PATCH
        keep = lane >= shift
        patch = []
        for k in range(2):
            a = field[tile, k, pl.ds(top, PATCH), :]
            b = field[tile + 1, k, pl.ds(top, PATCH), :]
            patch.append(pltpu.roll(jnp.where(keep, a, b), back, 1))
        places.append((top, tile, shift, keep))
        patches.append(patch)
        for m in range(2):
            pr = probe[0, m]
            pi = probe[1, m]
            wr = (pr * patch[0] - pi * patch[1]).astype(BF16)
            wi = (pr * patch[1] + pi * patch[0]).astype(BF16)
            waves.append(jnp.concatenate([wr, wi], axis=0))
    first = dot(plus, jnp.concatenate(waves, axis=1)).astype(BF16)
    cols = [slice(q * PATCH, (q + 1) * PATCH) for q in range(2 * n)]
    turned = [jnp.concatenate([first[:PATCH, q], first[PATCH:, q]], axis=1) for q in cols]
    far = dot(jnp.concatenate(turned, axis=0), minus)
    scaled = []
    for i in range(n):
        f0 = far[2 * i * PATCH:(2 * i + 1) * PATCH]
        f1 = far[(2 * i + 1) * PATCH:(2 * i + 2) * PATCH]
        power = f0 * f0 + f1 * f1
        intensity = power[:, :PATCH] + power[:, PATCH:]
        factor = (1.0 - photons[slots[i]].astype(F32) / (intensity + 1.0)) * valids[i]
        for f in (f0, f1):
            re = (f[:, :PATCH] * factor).astype(BF16)
            im = (f[:, PATCH:] * factor).astype(BF16)
            scaled.append(jnp.concatenate([re, im], axis=1))
    back_pass = dot(jnp.concatenate(scaled, axis=0), plus).astype(BF16)
    unturned = [jnp.concatenate([back_pass[q, :PATCH], back_pass[q, PATCH:]], axis=0) for q in cols]
    exit_grad = dot(minus, jnp.concatenate(unturned, axis=1))
    for m in range(2):
        sum_re = sum_im = None
        for i in range(n):
            er = exit_grad[:PATCH, cols[2 * i + m]]
            ei = exit_grad[PATCH:, cols[2 * i + m]]
            o_re, o_im = patches[i]
            t_re = o_re * er + o_im * ei
            t_im = o_re * ei - o_im * er
            sum_re = t_re if sum_re is None else sum_re + t_re
            sum_im = t_im if sum_im is None else sum_im + t_im
        probe_sum[0, m] += sum_re
        probe_sum[1, m] += sum_im
    for i in range(n):
        g_re = g_im = None
        for m in range(2):
            er = exit_grad[:PATCH, cols[2 * i + m]]
            ei = exit_grad[PATCH:, cols[2 * i + m]]
            pr = probe[0, m]
            pi = probe[1, m]
            t_re = pr * er + pi * ei
            t_im = pr * ei - pi * er
            g_re = t_re if g_re is None else g_re + t_re
            g_im = t_im if g_im is None else g_im + t_im
        top, tile, shift, keep = places[i]
        for k, g in ((0, g_re), (1, g_im)):
            g = pltpu.roll(g, shift, 1)
            grad[tile, k, pl.ds(top, PATCH), :] += jnp.where(keep, g, 0.0)
            grad[tile + 1, k, pl.ds(top, PATCH), :] += jnp.where(keep, 0.0, g)


def run_slots(inner, rows, cols, pos, count, listed, field, grad, photons, probe, probe_sum, plus_ref, minus_ref):
    def list_step(s, found):
        listed[found] = s
        inside = (pos[0, s] <= rows - PATCH) & (pos[1, s] <= cols - PATCH)
        wanted = inside if inner else jnp.logical_not(inside)
        return found + wanted.astype(jnp.int32)

    found = lax.fori_loop(0, count, list_step, jnp.int32(0))

    def step(k, carry):
        at = [k * BLOCK + i for i in range(BLOCK)]
        slots = [listed[jnp.minimum(a, found - 1)] for a in at]
        valids = [jnp.where(a < found, 1.0, 0.0).astype(F32) for a in at]
        slot_block(slots, valids, pos, field, grad, photons, probe, probe_sum, plus_ref, minus_ref)
        return carry

    lax.fori_loop(0, (found + BLOCK - 1) // BLOCK, step, 0)


def tile_copies(hbm, vmem, rows, tiles, row_at, sems, first, out=False):
    copies = []
    for t in range(tiles):
        a = hbm.at[:, :, pl.ds(t * PATCH, PATCH)]
        b = vmem.at[t, :, pl.ds(row_at, rows), :]
        copies.append(pltpu.make_async_copy(b, a, sems.at[first + t]) if out else
                      pltpu.make_async_copy(a, b, sems.at[first + t]))
    return copies


def inner_kernel(pos, count, own, photons, probe, plus_ref, minus_ref, grad_out, probe_out,
                 field, grad, photon_buf, listed, sems):
    rows, cols = own.shape[1], own.shape[2]
    tiles = cols // PATCH
    loads = tile_copies(own, field, rows, tiles, 0, sems, 0)
    loads.append(pltpu.make_async_copy(photons, photon_buf, sems.at[tiles]))
    for c in loads:
        c.start()
    for t in range(tiles + 1):
        grad[t] = jnp.zeros(grad.shape[1:], F32)
    probe_out[...] = jnp.zeros(probe_out.shape, F32)
    field[tiles] = jnp.zeros(field.shape[1:], F32)
    for c in loads:
        c.wait()
    run_slots(True, rows, cols, pos, count[0], listed, field, grad, photon_buf, probe, probe_out,
              plus_ref, minus_ref)
    for t in range(tiles):
        pltpu.make_async_copy(grad.at[t], grad_out.at[t], sems.at[t]).start()
    for t in range(tiles):
        pltpu.make_async_copy(grad.at[t], grad_out.at[t], sems.at[t]).wait()


def border_kernel(pos, count, own, right, below, corner, photons, probe, plus_ref, minus_ref, grad_in, probe_in,
                  g_own, g_right, g_below, g_corner, probe_out, field, grad, photon_buf, listed, sems):
    rows, cols = own.shape[1], own.shape[2]
    tiles = cols // PATCH
    loads = tile_copies(own, field, rows, tiles, 0, sems, 0)
    loads += tile_copies(below, field, PATCH, tiles, rows, sems, tiles)
    n = 2 * tiles
    loads.append(pltpu.make_async_copy(right, field.at[tiles, :, pl.ds(0, rows), :], sems.at[n]))
    loads.append(pltpu.make_async_copy(corner, field.at[tiles, :, pl.ds(rows, PATCH), :], sems.at[n + 1]))
    loads.append(pltpu.make_async_copy(photons, photon_buf, sems.at[n + 2]))
    for t in range(tiles):
        loads.append(pltpu.make_async_copy(grad_in.at[t], grad.at[t, :, pl.ds(0, rows), :], sems.at[n + 3 + t]))
    for c in loads:
        c.start()
    grad[tiles] = jnp.zeros(grad.shape[1:], F32)
    for t in range(tiles):
        grad[t, :, pl.ds(rows, PATCH), :] = jnp.zeros((2, PATCH, PATCH), F32)
    probe_out[...] = probe_in[...]
    for c in loads:
        c.wait()
    run_slots(False, rows, cols, pos, count[0], listed, field, grad, photon_buf, probe, probe_out,
              plus_ref, minus_ref)
    stores = tile_copies(g_own, grad, rows, tiles, 0, sems, 0, out=True)
    stores += tile_copies(g_below, grad, PATCH, tiles, rows, sems, tiles, out=True)
    stores.append(pltpu.make_async_copy(grad.at[tiles, :, pl.ds(0, rows), :], g_right, sems.at[n]))
    stores.append(pltpu.make_async_copy(grad.at[tiles, :, pl.ds(rows, PATCH), :], g_corner, sems.at[n + 1]))
    for c in stores:
        c.start()
    for c in stores:
        c.wait()


def shape(*dims):
    return jax.ShapeDtypeStruct(dims, F32)


def bit_exchange(value, bit):
    size = lax.axis_size(BOTH)
    return lax.ppermute(value, BOTH, [(i, i ^ bit) for i in range(size)])


def total_over_devices(value):
    me = lax.axis_index(BOTH)
    x_low, x_high = (me // 16) % 2, (me // 32) % 2
    halving = ((1, me % 2), (16, (x_low + x_high) % 2), (48, x_high))
    whole = (4, 12, 2, 64, 128)
    lows = []
    for mask, label in halving:
        half = value.shape[0] // 2
        upper = label != 0
        keep = jnp.where(upper, value[half:], value[:half])
        send = jnp.where(upper, value[:half], value[half:])
        value = keep + bit_exchange(send, mask)
        lows.append(upper)
    for mask in whole:
        value = value + bit_exchange(value, mask)
    for (mask, _), upper in zip(halving[::-1], lows[::-1]):
        other = bit_exchange(value, mask)
        value = jnp.concatenate([jnp.where(upper, other, value), jnp.where(upper, value, other)], axis=0)
    return value


def body(object_field, probe_modes, photons, positions, counts):
    rows, cols = object_field.shape[1], object_field.shape[2]
    slot_count = photons.shape[2]
    tiles = cols // PATCH
    n_row, n_col = lax.axis_size("row"), lax.axis_size("col")
    plus_table, minus_table = fourier_tables(PATCH)
    pos = positions[0, 0].T
    count = counts[0]
    photon_rows = photons[0, 0]
    right = lax.ppermute(object_field[:, :, :PATCH], "col", [(i, i - 1) for i in range(1, n_col)])
    below = lax.ppermute(object_field[:, :PATCH, :], "row", [(i, i - 1) for i in range(1, n_row)])
    corner = lax.ppermute(below[:, :, :PATCH], "col", [(i, i - 1) for i in range(1, n_col)])

    smem = pl.BlockSpec(memory_space=pltpu.SMEM)
    vmem = pl.BlockSpec(memory_space=pltpu.VMEM)
    hbm = pl.BlockSpec(memory_space=pl.ANY)
    scratch = [
        pltpu.VMEM((tiles + 1, 2, rows + PATCH, PATCH), F32),
        pltpu.VMEM((tiles + 1, 2, rows + PATCH, PATCH), F32),
        pltpu.VMEM(photon_rows.shape, BF16),
        pltpu.SMEM((slot_count,), jnp.int32),
        pltpu.SemaphoreType.DMA((3 * tiles + 3,)),
    ]
    inner_scratch = [
        pltpu.VMEM((tiles + 1, 2, rows, PATCH), F32),
        pltpu.VMEM((tiles + 1, 2, rows, PATCH), F32),
    ] + scratch[2:]
    params = pltpu.CompilerParams(vmem_limit_bytes=40 * 2**20)
    work = 4 * 2 * 256 * 256 * 256 * slot_count // 2
    cost = pl.CostEstimate(flops=work, bytes_accessed=8 * 2**20, transcendentals=0)
    grad_1, probe_1 = pl.pallas_call(
        inner_kernel,
        out_shape=(shape(tiles, 2, rows, PATCH), shape(*probe_modes.shape)),
        in_specs=[smem, smem, hbm, hbm, vmem, vmem, vmem],
        out_specs=(hbm, vmem),
        scratch_shapes=inner_scratch,
        compiler_params=params,
        cost_estimate=cost,
        name="inner_slots",
    )(pos, count, object_field, photon_rows, probe_modes, plus_table, minus_table)
    g_own, g_right, g_below, g_corner, probe_2 = pl.pallas_call(
        border_kernel,
        out_shape=(
            shape(2, rows, cols), shape(2, rows, PATCH), shape(2, PATCH, cols), shape(2, PATCH, PATCH),
            shape(*probe_modes.shape),
        ),
        in_specs=[smem, smem, hbm, hbm, hbm, hbm, hbm, vmem, vmem, vmem, hbm, vmem],
        out_specs=(hbm, hbm, hbm, hbm, vmem),
        scratch_shapes=scratch,
        compiler_params=params,
        cost_estimate=cost,
        name="border_slots",
    )(pos, count, object_field, right, below, corner, photon_rows, probe_modes, plus_table, minus_table,
      grad_1, probe_1)

    down = [(i, i + 1) for i in range(n_row - 1)]
    along = [(i, i + 1) for i in range(n_col - 1)]
    diagonal = [
        (a * n_col + b, (a + 1) * n_col + b + 1) for a in range(n_row - 1) for b in range(n_col - 1)
    ]
    from_above = lax.ppermute(g_below, "row", down)
    from_left = lax.ppermute(g_right, "col", along)
    from_corner = lax.ppermute(g_corner, BOTH, diagonal)
    total_probe = total_over_devices(probe_2.reshape(-1, PATCH)).reshape(probe_modes.shape)
    probe_gradient = total_probe / math.sqrt(n_row * n_col * slot_count)
    object_gradient = g_own.at[:, :PATCH, :].add(from_above)
    object_gradient = object_gradient.at[:, :, :PATCH].add(from_left)
    object_gradient = object_gradient.at[:, :PATCH, :PATCH].add(from_corner)
    return (object_gradient, probe_gradient)


def solution(mesh):
    in_specs = (
        P(None, "row", "col"),
        P(),
        P("row", "col", None, None, None),
        P("row", "col", None, None),
        P("row", "col"),
    )
    out_specs = (P(None, "row", "col"), P())
    return jax.shard_map(body, mesh=mesh, in_specs=in_specs, out_specs=out_specs, check_vma=False)
```

```python
import math

import jax
import jax.numpy as jnp
import numpy as np
from jax import lax
from jax.experimental import pallas as pl
from jax.experimental.pallas import tpu as pltpu
from jax.sharding import Mesh
from jax.sharding import PartitionSpec as P

F32 = jnp.float32
BF16 = jnp.bfloat16
PATCH = 128
BLOCK = 8
VMEM_LIMIT = 63 * 2**20
ROW = "z_hi"
COL = ("x", "y", "z_lo", "core")
BOTH = (ROW,) + COL
PLANE = ("x", "y")
DEPTH = ("z_hi", "z_lo")


def fourier_tables(patch_len):
    index_range = np.arange(patch_len)
    product = (index_range[:, None] * index_range[None, :]) % patch_len
    angle = product.astype(np.float32) * np.float32(2.0 * math.pi / patch_len)
    cosine = (np.cos(angle) / np.float32(math.sqrt(patch_len))).astype(np.float32)
    sine = (np.sin(angle) / np.float32(math.sqrt(patch_len))).astype(np.float32)
    plus_table = np.block([[cosine, sine], [-sine, cosine]])
    minus_table = np.block([[cosine, -sine], [sine, cosine]])
    return jnp.asarray(plus_table, BF16), jnp.asarray(minus_table, BF16)


def dot(a, b):
    return jnp.dot(a, b, preferred_element_type=F32)


def slot_block(slots, valids, pos, field, grad, photons, probe, probe_sum, plus_ref, minus_ref):
    n = len(slots)
    lane = lax.broadcasted_iota(jnp.int32, (PATCH, PATCH), 1)
    plus = plus_ref[...]
    minus = minus_ref[...]
    places, patches, waves = [], [], []
    for s in slots:
        top = pos[0, s]
        left = pos[1, s]
        tile = left // PATCH
        shift = left % PATCH
        back = (PATCH - shift) % PATCH
        keep = lane >= shift
        patch = []
        for k in range(2):
            a = field[tile, k, pl.ds(top, PATCH), :]
            b = field[tile + 1, k, pl.ds(top, PATCH), :]
            patch.append(pltpu.roll(jnp.where(keep, a, b), back, 1))
        places.append((top, tile, shift, keep))
        patches.append(patch)
        for m in range(2):
            pr = probe[0, m]
            pi = probe[1, m]
            wr = (pr * patch[0] - pi * patch[1]).astype(BF16)
            wi = (pr * patch[1] + pi * patch[0]).astype(BF16)
            waves.append(jnp.concatenate([wr, wi], axis=0))
    first = dot(plus, jnp.concatenate(waves, axis=1)).astype(BF16)
    cols = [slice(q * PATCH, (q + 1) * PATCH) for q in range(2 * n)]
    turned = [jnp.concatenate([first[:PATCH, q], first[PATCH:, q]], axis=1) for q in cols]
    far = dot(jnp.concatenate(turned, axis=0), minus)
    scaled = []
    for i in range(n):
        f0 = far[2 * i * PATCH:(2 * i + 1) * PATCH]
        f1 = far[(2 * i + 1) * PATCH:(2 * i + 2) * PATCH]
        power = f0 * f0 + f1 * f1
        intensity = power[:, :PATCH] + power[:, PATCH:]
        factor = (1.0 - photons[slots[i]].astype(F32) / (intensity + 1.0)) * valids[i]
        for f in (f0, f1):
            re = (f[:, :PATCH] * factor).astype(BF16)
            im = (f[:, PATCH:] * factor).astype(BF16)
            scaled.append(jnp.concatenate([re, im], axis=1))
    back_pass = dot(jnp.concatenate(scaled, axis=0), plus).astype(BF16)
    unturned = [jnp.concatenate([back_pass[q, :PATCH], back_pass[q, PATCH:]], axis=0) for q in cols]
    exit_grad = dot(minus, jnp.concatenate(unturned, axis=1))
    for m in range(2):
        sum_re = sum_im = None
        for i in range(n):
            er = exit_grad[:PATCH, cols[2 * i + m]]
            ei = exit_grad[PATCH:, cols[2 * i + m]]
            o_re, o_im = patches[i]
            t_re = o_re * er + o_im * ei
            t_im = o_re * ei - o_im * er
            sum_re = t_re if sum_re is None else sum_re + t_re
            sum_im = t_im if sum_im is None else sum_im + t_im
        probe_sum[0, m] += sum_re
        probe_sum[1, m] += sum_im
    for i in range(n):
        g_re = g_im = None
        for m in range(2):
            er = exit_grad[:PATCH, cols[2 * i + m]]
            ei = exit_grad[PATCH:, cols[2 * i + m]]
            pr = probe[0, m]
            pi = probe[1, m]
            t_re = pr * er + pi * ei
            t_im = pr * ei - pi * er
            g_re = t_re if g_re is None else g_re + t_re
            g_im = t_im if g_im is None else g_im + t_im
        top, tile, shift, keep = places[i]
        for k, g in ((0, g_re), (1, g_im)):
            g = pltpu.roll(g, shift, 1)
            grad[tile, k, pl.ds(top, PATCH), :] += jnp.where(keep, g, 0.0)
            grad[tile + 1, k, pl.ds(top, PATCH), :] += jnp.where(keep, 0.0, g)


def run_slots(inner, rows, cols, pos, count, listed, field, grad, photons, probe, probe_sum, plus_ref, minus_ref):
    def list_step(s, found):
        listed[found] = s
        inside = (pos[0, s] <= rows - PATCH) & (pos[1, s] <= cols - PATCH)
        wanted = inside if inner else jnp.logical_not(inside)
        return found + wanted.astype(jnp.int32)

    found = lax.fori_loop(0, count, list_step, jnp.int32(0))

    def step(k, carry, first=0, width=BLOCK):
        at = [first + k * width + i for i in range(width)]
        slots = [listed[jnp.minimum(a, found - 1)] for a in at]
        valids = [jnp.where(a < found, 1.0, 0.0).astype(F32) for a in at]
        slot_block(slots, valids, pos, field, grad, photons, probe, probe_sum, plus_ref, minus_ref)
        return carry

    rest = found % BLOCK
    small = (rest > 0) & (rest <= BLOCK // 2)
    blocks = found // BLOCK + ((rest > 0) & jnp.logical_not(small)).astype(jnp.int32)
    lax.fori_loop(0, blocks, step, 0)

    @pl.when(small)
    def _():
        step(0, 0, blocks * BLOCK, BLOCK // 2)


def tile_copies(hbm, vmem, rows, tiles, row_at, sems, first, out=False):
    copies = []
    for t in range(tiles):
        a = hbm.at[:, :, pl.ds(t * PATCH, PATCH)]
        b = vmem.at[t, :, pl.ds(row_at, rows), :]
        copies.append(pltpu.make_async_copy(b, a, sems.at[first + t]) if out else
                      pltpu.make_async_copy(a, b, sems.at[first + t]))
    return copies


def rim_kernel(own, below, right, corner, sems):
    copies = [
        pltpu.make_async_copy(own.at[:, pl.ds(0, PATCH), :], below, sems.at[0]),
        pltpu.make_async_copy(own.at[:, :, pl.ds(0, PATCH)], right, sems.at[1]),
        pltpu.make_async_copy(own.at[:, pl.ds(0, PATCH), pl.ds(0, PATCH)], corner, sems.at[2]),
    ]
    for c in copies:
        c.start()
    for c in copies:
        c.wait()


def inner_kernel(pos, count, own, photons, probe, plus_ref, minus_ref, grad_out, probe_out,
                 field, grad, photon_buf, listed, sems):
    rows, cols = own.shape[1], own.shape[2]
    tiles = cols // PATCH
    loads = tile_copies(own, field, rows, tiles, 0, sems, 0)
    loads.append(pltpu.make_async_copy(photons, photon_buf, sems.at[tiles]))
    for c in loads:
        c.start()
    for t in range(tiles + 1):
        grad[t] = jnp.zeros(grad.shape[1:], F32)
    probe_out[...] = jnp.zeros(probe_out.shape, F32)
    field[tiles] = jnp.zeros(field.shape[1:], F32)
    for c in loads:
        c.wait()
    run_slots(True, rows, cols, pos, count[0], listed, field, grad, photon_buf, probe, probe_out,
              plus_ref, minus_ref)
    for t in range(tiles):
        pltpu.make_async_copy(grad.at[t], grad_out.at[t], sems.at[t]).start()
    for t in range(tiles):
        pltpu.make_async_copy(grad.at[t], grad_out.at[t], sems.at[t]).wait()


def border_kernel(pos, count, own, right, below, corner, photons, probe, plus_ref, minus_ref, grad_in, probe_in,
                  g_own, g_right, g_below, g_corner, probe_out, field, grad, photon_buf, listed, sems):
    rows, cols = own.shape[1], own.shape[2]
    tiles = cols // PATCH
    loads = tile_copies(own, field, rows, tiles, 0, sems, 0)
    loads += tile_copies(below, field, PATCH, tiles, rows, sems, tiles)
    n = 2 * tiles
    loads.append(pltpu.make_async_copy(right, field.at[tiles, :, pl.ds(0, rows), :], sems.at[n]))
    loads.append(pltpu.make_async_copy(corner, field.at[tiles, :, pl.ds(rows, PATCH), :], sems.at[n + 1]))
    loads.append(pltpu.make_async_copy(photons, photon_buf, sems.at[n + 2]))
    for t in range(tiles):
        loads.append(pltpu.make_async_copy(grad_in.at[t], grad.at[t, :, pl.ds(0, rows), :], sems.at[n + 3 + t]))
    for c in loads:
        c.start()
    grad[tiles] = jnp.zeros(grad.shape[1:], F32)
    for t in range(tiles):
        grad[t, :, pl.ds(rows, PATCH), :] = jnp.zeros((2, PATCH, PATCH), F32)
    probe_out[...] = probe_in[...]
    for c in loads:
        c.wait()
    run_slots(False, rows, cols, pos, count[0], listed, field, grad, photon_buf, probe, probe_out,
              plus_ref, minus_ref)
    stores = tile_copies(g_own, grad, rows, tiles, 0, sems, 0, out=True)
    stores += tile_copies(g_below, grad, PATCH, tiles, rows, sems, tiles, out=True)
    stores.append(pltpu.make_async_copy(grad.at[tiles, :, pl.ds(0, rows), :], g_right, sems.at[n]))
    stores.append(pltpu.make_async_copy(grad.at[tiles, :, pl.ds(rows, PATCH), :], g_corner, sems.at[n + 1]))
    for c in stores:
        c.start()
    for c in stores:
        c.wait()


def seam_kernel(grad_in, above, left, corner, grad, top_buf, left_buf, above_buf, beside_buf, corner_buf, sems):
    rows, cols = grad.shape[1], grad.shape[2]
    rest = rows - PATCH
    top_rim = grad.at[:, pl.ds(0, PATCH), :]
    left_rim = grad.at[:, pl.ds(PATCH, rest), pl.ds(0, PATCH)]
    loads = [
        pltpu.make_async_copy(top_rim, top_buf, sems.at[0]),
        pltpu.make_async_copy(left_rim, left_buf, sems.at[1]),
        pltpu.make_async_copy(above, above_buf, sems.at[2]),
        pltpu.make_async_copy(left, beside_buf, sems.at[3]),
        pltpu.make_async_copy(corner, corner_buf, sems.at[4]),
    ]
    for c in loads:
        c.start()
    for c in loads:
        c.wait()
    top_buf[:, :, PATCH:] += above_buf[:, :, PATCH:]
    top_buf[:, :, :PATCH] += above_buf[:, :, :PATCH] + (beside_buf[:, :PATCH, :] + corner_buf[...])
    left_buf[...] += beside_buf[:, PATCH:, :]
    stores = [
        pltpu.make_async_copy(top_buf, top_rim, sems.at[0]),
        pltpu.make_async_copy(left_buf, left_rim, sems.at[1]),
    ]
    for c in stores:
        c.start()
    for c in stores:
        c.wait()


def shape(*dims):
    return jax.ShapeDtypeStruct(dims, F32)


def everyone(value, axes, count):
    sent = jnp.broadcast_to(value[None], (count,) + value.shape)
    return lax.all_to_all(sent, axes, 0, 0, tiled=True)


def total_over_devices(value, halos):
    core = lax.axis_index("core")
    plane = lax.axis_size(PLANE)
    depth = lax.axis_size(DEPTH)
    swap = [(0, 1), (1, 0)]
    half = value.shape[0] // 2
    upper = core != 0
    keep = jnp.where(upper, value[half:], value[:half])
    send = jnp.where(upper, value[:half], value[half:])
    value = keep + lax.ppermute(send, "core", swap)
    shares = lax.all_to_all(value.reshape(plane, -1, PATCH), PLANE, 0, 0, tiled=True)
    share = jnp.sum(shares, axis=0)
    share, _ = lax.optimization_barrier((share, halos))
    share = jnp.sum(everyone(share, DEPTH, depth), axis=0)
    value = everyone(share, PLANE, plane).reshape(half, PATCH)
    other = lax.ppermute(value, "core", swap)
    return jnp.concatenate([jnp.where(upper, other, value), jnp.where(upper, value, other)], axis=0)


def body(object_field, probe_modes, photons, positions, counts):
    rows, cols = object_field.shape[1], object_field.shape[2]
    slot_count = photons.shape[2]
    tiles = cols // PATCH
    n_row, n_col = lax.axis_size(ROW), lax.axis_size(COL)
    plus_table, minus_table = fourier_tables(PATCH)
    pos = positions[0, 0].T
    count = counts[0]
    photon_rows = photons[0, 0]
    down = [(i, i + 1) for i in range(n_row - 1)]
    along = [(i, i + 1) for i in range(n_col - 1)]
    diagonal = [
        (a * n_col + b, (a + 1) * n_col + b + 1) for a in range(n_row - 1) for b in range(n_col - 1)
    ]
    up, back, diagonal_back = ([(j, i) for i, j in pairs] for pairs in (down, along, diagonal))

    smem = pl.BlockSpec(memory_space=pltpu.SMEM)
    vmem = pl.BlockSpec(memory_space=pltpu.VMEM)
    hbm = pl.BlockSpec(memory_space=pl.ANY)
    scratch = [
        pltpu.VMEM((tiles + 1, 2, rows + PATCH, PATCH), F32),
        pltpu.VMEM((tiles + 1, 2, rows + PATCH, PATCH), F32),
        pltpu.VMEM(photon_rows.shape, BF16),
        pltpu.SMEM((slot_count,), jnp.int32),
        pltpu.SemaphoreType.DMA((3 * tiles + 3,)),
    ]
    inner_scratch = [
        pltpu.VMEM((tiles + 1, 2, rows, PATCH), F32),
        pltpu.VMEM((tiles + 1, 2, rows, PATCH), F32),
    ] + scratch[2:]
    params = pltpu.CompilerParams(vmem_limit_bytes=VMEM_LIMIT)
    rims = (shape(2, PATCH, cols), shape(2, rows, PATCH), shape(2, PATCH, PATCH))
    below, right, corner = pl.pallas_call(
        rim_kernel,
        out_shape=rims,
        in_specs=[hbm],
        out_specs=(hbm, hbm, hbm),
        scratch_shapes=[pltpu.SemaphoreType.DMA((3,))],
        compiler_params=params,
        name="rims",
    )(object_field)
    below = lax.ppermute(below, ROW, up)
    right = lax.ppermute(right, COL, back)
    corner = lax.ppermute(corner, BOTH, diagonal_back)
    work = 24 * 10**9
    cost = pl.CostEstimate(flops=work, bytes_accessed=8 * 2**20, transcendentals=0)
    grad_1, probe_1 = pl.pallas_call(
        inner_kernel,
        out_shape=(shape(tiles, 2, rows, PATCH), shape(*probe_modes.shape)),
        in_specs=[smem, smem, hbm, hbm, vmem, vmem, vmem],
        out_specs=(hbm, vmem),
        scratch_shapes=inner_scratch,
        compiler_params=params,
        cost_estimate=cost,
        name="inner_slots",
    )(pos, count, object_field, photon_rows, probe_modes, plus_table, minus_table)
    g_own, g_right, g_below, g_corner, probe_2 = pl.pallas_call(
        border_kernel,
        out_shape=(
            shape(2, rows, cols), shape(2, rows, PATCH), shape(2, PATCH, cols), shape(2, PATCH, PATCH),
            shape(*probe_modes.shape),
        ),
        in_specs=[smem, smem, hbm, hbm, hbm, hbm, hbm, vmem, vmem, vmem, hbm, vmem],
        out_specs=(hbm, hbm, hbm, hbm, vmem),
        scratch_shapes=scratch,
        compiler_params=params,
        cost_estimate=cost,
        name="border_slots",
    )(pos, count, object_field, right, below, corner, photon_rows, probe_modes, plus_table, minus_table,
      grad_1, probe_1)

    from_above = lax.ppermute(g_below, ROW, down)
    from_left = lax.ppermute(g_right, COL, along)
    from_corner = lax.ppermute(g_corner, BOTH, diagonal)
    total_probe = total_over_devices(probe_2.reshape(-1, PATCH), (from_above, from_left, from_corner))
    probe_gradient = total_probe.reshape(probe_modes.shape) / math.sqrt(n_row * n_col * slot_count)
    object_gradient = pl.pallas_call(
        seam_kernel,
        out_shape=shape(2, rows, cols),
        in_specs=[hbm] * 4,
        out_specs=hbm,
        scratch_shapes=[
            pltpu.VMEM((2, PATCH, cols), F32),
            pltpu.VMEM((2, rows - PATCH, PATCH), F32),
            pltpu.VMEM((2, PATCH, cols), F32),
            pltpu.VMEM((2, rows, PATCH), F32),
            pltpu.VMEM((2, PATCH, PATCH), F32),
            pltpu.SemaphoreType.DMA((5,)),
        ],
        input_output_aliases={0: 0},
        compiler_params=params,
        name="seams",
    )(g_own, from_above, from_left, from_corner)
    return (object_gradient, probe_gradient)


def solution(mesh):
    fine = Mesh(mesh.devices.reshape(4, 4, 4, 2, 2), BOTH)
    in_specs = (
        P(None, ROW, COL),
        P(),
        P(ROW, COL, None, None, None),
        P(ROW, COL, None, None),
        P(ROW, COL),
    )
    out_specs = (P(None, ROW, COL), P())
    return jax.shard_map(body, mesh=fine, in_specs=in_specs, out_specs=out_specs, check_vma=False)
```

```python
import functools
import math

import jax
import jax.numpy as jnp
import numpy as np
from jax import lax
from jax.experimental import pallas as pl
from jax.experimental.pallas import tpu as pltpu
from jax.sharding import Mesh
from jax.sharding import PartitionSpec as P

F32 = jnp.float32
BF16 = jnp.bfloat16
PATCH = 128
BLOCK = 8
VMEM_LIMIT = 63 * 2**20
ROW = "z_hi"
COL = ("x", "y", "z_lo", "core")
BOTH = (ROW,) + COL
PLANE = ("x", "y")
DEPTH = ("z_hi", "z_lo")


def waves_of(patch_len):
    index_range = np.arange(patch_len)
    product = (index_range[:, None] * index_range[None, :]) % patch_len
    angle = product.astype(np.float32) * np.float32(2.0 * math.pi / patch_len)
    pair = np.stack([np.cos(angle), np.sin(angle)]) / np.float32(math.sqrt(patch_len))
    return jnp.asarray(pair, F32)


def dot(a, b):
    return jnp.dot(a, b, preferred_element_type=F32)


def slot_block(at, slots, valids, pos, row_base, field, grad, photons, probe, probe_sum, plus_ref, minus_ref):
    n = len(slots)
    lane = lax.broadcasted_iota(jnp.int32, (PATCH, PATCH), 1)
    plus = plus_ref[...]
    minus = minus_ref[...]
    places, patches, waves = [], [], []
    for s in slots:
        top = pos[0, s] - row_base
        left = pos[1, s]
        tile = left // PATCH
        shift = left % PATCH
        back = (PATCH - shift) % PATCH
        keep = lane >= shift
        patch = []
        for k in range(2):
            a = field[tile, k, pl.ds(top, PATCH), :]
            b = field[tile + 1, k, pl.ds(top, PATCH), :]
            patch.append(pltpu.roll(jnp.where(keep, a, b), back, 1))
        places.append((top, tile, shift, keep))
        patches.append(patch)
        for m in range(2):
            pr = probe[0, m]
            pi = probe[1, m]
            wr = (pr * patch[0] - pi * patch[1]).astype(BF16)
            wi = (pr * patch[1] + pi * patch[0]).astype(BF16)
            waves.append(jnp.concatenate([wr, wi], axis=0))
    first = dot(plus, jnp.concatenate(waves, axis=1)).astype(BF16)
    cols = [slice(q * PATCH, (q + 1) * PATCH) for q in range(2 * n)]
    turned = [jnp.concatenate([first[:PATCH, q], first[PATCH:, q]], axis=1) for q in cols]
    far = dot(jnp.concatenate(turned, axis=0), minus)
    scaled = []
    for i in range(n):
        f0 = far[2 * i * PATCH:(2 * i + 1) * PATCH]
        f1 = far[(2 * i + 1) * PATCH:(2 * i + 2) * PATCH]
        power = f0 * f0 + f1 * f1
        intensity = power[:, :PATCH] + power[:, PATCH:]
        factor = (1.0 - photons[at[i]].astype(F32) / (intensity + 1.0)) * valids[i]
        for f in (f0, f1):
            re = (f[:, :PATCH] * factor).astype(BF16)
            im = (f[:, PATCH:] * factor).astype(BF16)
            scaled.append(jnp.concatenate([re, im], axis=1))
    back_pass = dot(jnp.concatenate(scaled, axis=0), plus).astype(BF16)
    unturned = [jnp.concatenate([back_pass[q, :PATCH], back_pass[q, PATCH:]], axis=0) for q in cols]
    exit_grad = dot(minus, jnp.concatenate(unturned, axis=1))
    for m in range(2):
        sum_re = sum_im = None
        for i in range(n):
            er = exit_grad[:PATCH, cols[2 * i + m]]
            ei = exit_grad[PATCH:, cols[2 * i + m]]
            o_re, o_im = patches[i]
            t_re = o_re * er + o_im * ei
            t_im = o_re * ei - o_im * er
            sum_re = t_re if sum_re is None else sum_re + t_re
            sum_im = t_im if sum_im is None else sum_im + t_im
        probe_sum[0, m] += sum_re
        probe_sum[1, m] += sum_im
    for i in range(n):
        g_re = g_im = None
        for m in range(2):
            er = exit_grad[:PATCH, cols[2 * i + m]]
            ei = exit_grad[PATCH:, cols[2 * i + m]]
            pr = probe[0, m]
            pi = probe[1, m]
            t_re = pr * er + pi * ei
            t_im = pr * ei - pi * er
            g_re = t_re if g_re is None else g_re + t_re
            g_im = t_im if g_im is None else g_im + t_im
        top, tile, shift, keep = places[i]
        for k, g in ((0, g_re), (1, g_im)):
            g = pltpu.roll(g, shift, 1)
            grad[tile, k, pl.ds(top, PATCH), :] += jnp.where(keep, g, 0.0)
            grad[tile + 1, k, pl.ds(top, PATCH), :] += jnp.where(keep, 0.0, g)


def fill_tables(waves, plus_ref, minus_ref):
    c = waves[0].astype(BF16)
    s = waves[1].astype(BF16)
    plus_ref[:PATCH, :PATCH] = c
    plus_ref[:PATCH, PATCH:] = s
    plus_ref[PATCH:, :PATCH] = -s
    plus_ref[PATCH:, PATCH:] = c
    minus_ref[:PATCH, :PATCH] = c
    minus_ref[:PATCH, PATCH:] = -s
    minus_ref[PATCH:, :PATCH] = s
    minus_ref[PATCH:, PATCH:] = c


def list_slots(wanted, pos, count, listed, photons, photon_buf, photon_sems):
    def list_step(s, found):
        chosen = wanted(pos[0, s])

        @pl.when(chosen)
        def _():
            listed[found] = s
            pltpu.make_async_copy(photons.at[s], photon_buf.at[found], photon_sems.at[found]).start()

        return found + chosen.astype(jnp.int32)

    return lax.fori_loop(0, count, list_step, jnp.int32(0))


def run_slots(found, pos, row_base, listed, field, grad, photons, photon_buf, photon_sems, probe, probe_sum,
              plus_ref, minus_ref):
    def step(k, carry, first=0, width=BLOCK):
        places = [first + k * width + i for i in range(width)]
        at = [jnp.minimum(p, found - 1) for p in places]
        slots = [listed[a] for a in at]
        valids = [jnp.where(p < found, 1.0, 0.0).astype(F32) for p in places]
        for p, a, s in zip(places, at, slots):
            @pl.when(p < found)
            def _(a=a, s=s):
                pltpu.make_async_copy(photons.at[s], photon_buf.at[a], photon_sems.at[a]).wait()

        slot_block(at, slots, valids, pos, row_base, field, grad, photon_buf, probe, probe_sum, plus_ref, minus_ref)
        return carry

    rest = found % BLOCK
    small = (rest > 0) & (rest <= BLOCK // 2)
    blocks = found // BLOCK + ((rest > 0) & jnp.logical_not(small)).astype(jnp.int32)
    lax.fori_loop(0, blocks, step, 0)

    @pl.when(small)
    def _():
        step(0, 0, blocks * BLOCK, BLOCK // 2)


def copies_of(pairs, sems):
    return [pltpu.make_async_copy(a, b, sems.at[i]) for i, (a, b) in enumerate(pairs)]


def start_all(copies):
    for c in copies:
        c.start()


def wait_all(copies):
    for c in copies:
        c.wait()


def by_tiles(array, tiles):
    return [array.at[:, :, pl.ds(t * PATCH, PATCH)] for t in range(tiles)]


def rim_kernel(own, below, right, corner, below_buf, right_buf, sems):
    rim = pl.ds(0, PATCH)
    loads = copies_of([(own.at[:, rim, :], below_buf), (own.at[:, :, rim], right_buf)], sems)
    stores = copies_of(
        [(below_buf, below), (right_buf, right), (below_buf.at[:, :, rim], corner)], sems
    )
    start_all(loads)
    wait_all(loads)
    start_all(stores)
    wait_all(stores)


def upper_kernel(pos, count, own, right, photons, probe_in, waves_in, g_own, g_right, probe_out,
                 field, grad, photon_buf, probe, waves, plus_ref, minus_ref, probe_sum, listed, sems, photon_sems):
    rows, cols = own.shape[1], own.shape[2]
    tiles = cols // PATCH
    loads = copies_of(
        [(waves_in, waves), (probe_in, probe)]
        + [(a, field.at[t]) for t, a in enumerate(by_tiles(own, tiles))]
        + [(right, field.at[tiles])],
        sems,
    )
    start_all(loads)
    found = list_slots(lambda top: top <= rows - PATCH, pos, count[0], listed, photons, photon_buf, photon_sems)
    grad[...] = jnp.zeros(grad.shape, F32)
    probe_sum[...] = jnp.zeros(probe_sum.shape, F32)
    loads[0].wait()
    fill_tables(waves, plus_ref, minus_ref)
    wait_all(loads[1:])
    run_slots(found, pos, 0, listed, field, grad, photons, photon_buf, photon_sems, probe, probe_sum,
              plus_ref, minus_ref)
    stores = copies_of(
        [(probe_sum, probe_out)]
        + [(grad.at[t], a) for t, a in enumerate(by_tiles(g_own, tiles))]
        + [(grad.at[tiles], g_right)],
        sems,
    )
    start_all(stores)
    wait_all(stores)


def lower_kernel(scale, pos, count, own, right, below, corner, photons, probe_in, waves_in, own_in, right_in, sum_in,
                 g_own, g_right, g_below, probe_out,
                 field, grad, photon_buf, probe, waves, plus_ref, minus_ref, probe_sum, listed, sems, photon_sems):
    rows, cols = own.shape[1], own.shape[2]
    tiles = cols // PATCH
    base = rows - PATCH
    last, upper, lower = pl.ds(base, PATCH), pl.ds(0, PATCH), pl.ds(PATCH, PATCH)

    def last_rows(array):
        return [array.at[:, last, pl.ds(t * PATCH, PATCH)] for t in range(tiles)]

    loads = copies_of(
        [(waves_in, waves), (probe_in, probe), (sum_in, probe_sum)]
        + [(a, field.at[t, :, upper, :]) for t, a in enumerate(last_rows(own) + [right.at[:, last, :]])]
        + [(a, field.at[t, :, lower, :]) for t, a in enumerate(by_tiles(below, tiles) + [corner])]
        + [(a, grad.at[t, :, upper, :]) for t, a in enumerate(last_rows(own_in) + [right_in.at[:, last, :]])],
        sems,
    )
    start_all(loads)
    found = list_slots(lambda top: top > base, pos, count[0], listed, photons, photon_buf, photon_sems)
    for t in range(tiles + 1):
        grad[t, :, lower, :] = jnp.zeros((2, PATCH, PATCH), F32)
    loads[0].wait()
    fill_tables(waves, plus_ref, minus_ref)
    wait_all(loads[1:])
    run_slots(found, pos, base, listed, field, grad, photons, photon_buf, photon_sems, probe, probe_sum,
              plus_ref, minus_ref)
    probe_sum[...] = probe_sum[...] * scale
    stores = copies_of(
        [(probe_sum, probe_out)]
        + [(grad.at[t, :, lower, :], a) for t, a in enumerate(by_tiles(g_below, tiles + 1))]
        + [(grad.at[t, :, upper, :], a) for t, a in enumerate(last_rows(g_own) + [g_right.at[:, last, :]])],
        sems,
    )
    start_all(stores)
    wait_all(stores)


def seam_kernel(grad_in, above, left, grad, top_buf, left_buf, above_buf, beside_buf, sems):
    rows, cols = grad.shape[1], grad.shape[2]
    rest = rows - PATCH
    top_rim = grad.at[:, pl.ds(0, PATCH), :]
    left_rim = grad.at[:, pl.ds(PATCH, rest), pl.ds(0, PATCH)]
    loads = copies_of(
        [(top_rim, top_buf), (left_rim, left_buf), (above.at[:, :, pl.ds(0, cols)], above_buf), (left, beside_buf)],
        sems,
    )
    start_all(loads)
    wait_all(loads)
    top_buf[:, :, PATCH:] += above_buf[:, :, PATCH:]
    top_buf[:, :, :PATCH] += above_buf[:, :, :PATCH] + beside_buf[:, :PATCH, :]
    left_buf[...] += beside_buf[:, PATCH:, :]
    stores = copies_of([(top_buf, top_rim), (left_buf, left_rim)], sems)
    start_all(stores)
    wait_all(stores)


def shape(*dims):
    return jax.ShapeDtypeStruct(dims, F32)


def everyone(value, axes, count):
    sent = jnp.broadcast_to(value[None], (count,) + value.shape)
    return lax.all_to_all(sent, axes, 0, 0, tiled=True)


def body(object_field, probe_modes, photons, positions, counts):
    rows, cols = object_field.shape[1], object_field.shape[2]
    slot_count = photons.shape[2]
    tiles = cols // PATCH
    n_row, n_col = lax.axis_size(ROW), lax.axis_size(COL)
    pos = positions[0, 0].T
    count = counts[0]
    photon_rows = photons[0, 0]
    waves = waves_of(PATCH)
    scale = 1.0 / math.sqrt(n_row * n_col * slot_count)
    down = [(i, i + 1) for i in range(n_row - 1)]
    along = [(i, i + 1) for i in range(n_col - 1)]
    up, back = ([(j, i) for i, j in pairs] for pairs in (down, along))
    diagonal_back = [
        ((a + 1) * n_col + b + 1, a * n_col + b) for a in range(n_row - 1) for b in range(n_col - 1)
    ]
    smem = pl.BlockSpec(memory_space=pltpu.SMEM)
    hbm = pl.BlockSpec(memory_space=pl.ANY)
    params = pltpu.CompilerParams(vmem_limit_bytes=VMEM_LIMIT)

    below, right, corner = pl.pallas_call(
        rim_kernel,
        out_shape=(shape(2, PATCH, cols), shape(2, rows, PATCH), shape(2, PATCH, PATCH)),
        in_specs=[hbm],
        out_specs=(hbm,) * 3,
        scratch_shapes=[
            pltpu.VMEM((2, PATCH, cols), F32),
            pltpu.VMEM((2, rows, PATCH), F32),
            pltpu.SemaphoreType.DMA((3,)),
        ],
        compiler_params=params,
        name="rims",
    )(object_field)
    below = lax.ppermute(below, ROW, up)
    right = lax.ppermute(right, COL, back)
    corner = lax.ppermute(corner, BOTH, diagonal_back)

    def scratch(height):
        return [
            pltpu.VMEM((tiles + 1, 2, height, PATCH), F32),
            pltpu.VMEM((tiles + 1, 2, height, PATCH), F32),
            pltpu.VMEM(photon_rows.shape, BF16),
            pltpu.VMEM(probe_modes.shape, F32),
            pltpu.VMEM(waves.shape, F32),
            pltpu.VMEM((2 * PATCH, 2 * PATCH), BF16),
            pltpu.VMEM((2 * PATCH, 2 * PATCH), BF16),
            pltpu.VMEM(probe_modes.shape, F32),
            pltpu.SMEM((slot_count,), jnp.int32),
            pltpu.SemaphoreType.DMA((3 * tiles + 6,)),
            pltpu.SemaphoreType.DMA((slot_count,)),
        ]

    own_shape, right_shape, probe_shape = shape(2, rows, cols), shape(2, rows, PATCH), shape(*probe_modes.shape)
    g_own, g_right, probe_1 = pl.pallas_call(
        upper_kernel,
        out_shape=(own_shape, right_shape, probe_shape),
        in_specs=[smem, smem] + [hbm] * 5,
        out_specs=(hbm,) * 3,
        scratch_shapes=scratch(rows),
        compiler_params=params,
        cost_estimate=pl.CostEstimate(flops=24 * 10**9, bytes_accessed=8 * 2**20, transcendentals=0),
        name="upper_slots",
    )(pos, count, object_field, right, photon_rows, probe_modes, waves)
    g_own, g_right, g_below, probe_2 = pl.pallas_call(
        functools.partial(lower_kernel, scale),
        out_shape=(own_shape, right_shape, shape(2, PATCH, cols + PATCH), probe_shape),
        in_specs=[smem, smem] + [hbm] * 10,
        out_specs=(hbm,) * 4,
        scratch_shapes=scratch(2 * PATCH),
        input_output_aliases={9: 0, 10: 1},
        compiler_params=params,
        cost_estimate=pl.CostEstimate(flops=8 * 10**9, bytes_accessed=4 * 2**20, transcendentals=0),
        name="lower_slots",
    )(pos, count, object_field, right, below, corner, photon_rows, probe_modes, waves, g_own, g_right, probe_1)

    core, plane, depth = lax.axis_index("core"), lax.axis_size(PLANE), lax.axis_size(DEPTH)
    swap = [(0, 1), (1, 0)]
    above = lax.ppermute(g_below, ROW, down)
    value = probe_2.reshape(-1, PATCH)
    half = value.shape[0] // 2
    upper = core != 0
    keep = jnp.where(upper, value[half:], value[:half])
    send = jnp.where(upper, value[:half], value[half:])
    value = keep + lax.ppermute(send, "core", swap)
    shares = lax.all_to_all(value.reshape(plane, -1, PATCH), PLANE, 0, 0, tiled=True)
    share = jnp.sum(shares, axis=0)
    share, above = lax.optimization_barrier((share, above))
    g_right = g_right.at[:, :PATCH, :].add(above[:, :, cols:])
    left = lax.ppermute(g_right, COL, along)
    share = jnp.sum(everyone(share, DEPTH, depth), axis=0)
    value = everyone(share, PLANE, plane).reshape(half, PATCH)
    other = lax.ppermute(value, "core", swap)
    value = jnp.concatenate([jnp.where(upper, other, value), jnp.where(upper, value, other)], axis=0)
    probe_gradient = value.reshape(probe_modes.shape)

    object_gradient = pl.pallas_call(
        seam_kernel,
        out_shape=own_shape,
        in_specs=[hbm] * 3,
        out_specs=hbm,
        scratch_shapes=[
            pltpu.VMEM((2, PATCH, cols), F32),
            pltpu.VMEM((2, rows - PATCH, PATCH), F32),
            pltpu.VMEM((2, PATCH, cols), F32),
            pltpu.VMEM((2, rows, PATCH), F32),
            pltpu.SemaphoreType.DMA((4,)),
        ],
        input_output_aliases={0: 0},
        compiler_params=params,
        name="seams",
    )(g_own, above, left)
    return (object_gradient, probe_gradient)


def solution(mesh):
    fine = Mesh(mesh.devices.reshape(4, 4, 4, 2, 2), BOTH)
    in_specs = (
        P(None, ROW, COL),
        P(),
        P(ROW, COL, None, None, None),
        P(ROW, COL, None, None),
        P(ROW, COL),
    )
    out_specs = (P(None, ROW, COL), P())
    return jax.shard_map(body, mesh=fine, in_specs=in_specs, out_specs=out_specs, check_vma=False)
```

```python
import functools
import math

import jax
import jax.numpy as jnp
import numpy as np
from jax import lax
from jax.experimental import pallas as pl
from jax.experimental.pallas import tpu as pltpu
from jax.sharding import Mesh
from jax.sharding import PartitionSpec as P

F32 = jnp.float32
BF16 = jnp.bfloat16
PATCH = 128
BLOCK = 8
VMEM_LIMIT = 63 * 2**20
ROW = "z_hi"
COL = ("x", "y", "z_lo", "core")
BOTH = (ROW,) + COL
PLANE = ("x", "y")
DEPTH = ("z_hi", "z_lo")


def waves_of(patch_len):
    index_range = np.arange(patch_len)
    product = (index_range[:, None] * index_range[None, :]) % patch_len
    angle = product.astype(np.float32) * np.float32(2.0 * math.pi / patch_len)
    pair = np.stack([np.cos(angle), np.sin(angle)]) / np.float32(math.sqrt(patch_len))
    return jnp.asarray(pair, F32)


def dot(a, b):
    return jnp.dot(a, b, preferred_element_type=F32)


def slot_block(at, slots, valids, pos, row_base, field, grad, photons, probe, probe_sum, plus_ref, minus_ref):
    n = len(slots)
    lane = lax.broadcasted_iota(jnp.int32, (PATCH, PATCH), 1)
    plus = plus_ref[...]
    minus = minus_ref[...]
    places, patches, waves = [], [], []
    for s in slots:
        top = pos[0, s] - row_base
        left = pos[1, s]
        tile = left // PATCH
        shift = left % PATCH
        back = (PATCH - shift) % PATCH
        keep = lane >= shift
        patch = []
        for k in range(2):
            a = field[tile, k, pl.ds(top, PATCH), :]
            b = field[tile + 1, k, pl.ds(top, PATCH), :]
            patch.append(pltpu.roll(jnp.where(keep, a, b), back, 1))
        places.append((top, tile, shift, keep))
        patches.append(patch)
        for m in range(2):
            pr = probe[0, m]
            pi = probe[1, m]
            wr = (pr * patch[0] - pi * patch[1]).astype(BF16)
            wi = (pr * patch[1] + pi * patch[0]).astype(BF16)
            waves.append(jnp.concatenate([wr, wi], axis=0))
    first = dot(plus, jnp.concatenate(waves, axis=1)).astype(BF16)
    cols = [slice(q * PATCH, (q + 1) * PATCH) for q in range(2 * n)]
    turned = [jnp.concatenate([first[:PATCH, q], first[PATCH:, q]], axis=1) for q in cols]
    far = dot(jnp.concatenate(turned, axis=0), minus)
    scaled = []
    for i in range(n):
        f0 = far[2 * i * PATCH:(2 * i + 1) * PATCH]
        f1 = far[(2 * i + 1) * PATCH:(2 * i + 2) * PATCH]
        power = f0 * f0 + f1 * f1
        intensity = power[:, :PATCH] + power[:, PATCH:]
        factor = (1.0 - photons[at[i]].astype(F32) / (intensity + 1.0)) * valids[i]
        for f in (f0, f1):
            re = (f[:, :PATCH] * factor).astype(BF16)
            im = (f[:, PATCH:] * factor).astype(BF16)
            scaled.append(jnp.concatenate([re, im], axis=1))
    back_pass = dot(jnp.concatenate(scaled, axis=0), plus).astype(BF16)
    unturned = [jnp.concatenate([back_pass[q, :PATCH], back_pass[q, PATCH:]], axis=0) for q in cols]
    exit_grad = dot(minus, jnp.concatenate(unturned, axis=1))
    for m in range(2):
        sum_re = sum_im = None
        for i in range(n):
            er = exit_grad[:PATCH, cols[2 * i + m]]
            ei = exit_grad[PATCH:, cols[2 * i + m]]
            o_re, o_im = patches[i]
            t_re = o_re * er + o_im * ei
            t_im = o_re * ei - o_im * er
            sum_re = t_re if sum_re is None else sum_re + t_re
            sum_im = t_im if sum_im is None else sum_im + t_im
        probe_sum[0, m] += sum_re
        probe_sum[1, m] += sum_im
    for i in range(n):
        g_re = g_im = None
        for m in range(2):
            er = exit_grad[:PATCH, cols[2 * i + m]]
            ei = exit_grad[PATCH:, cols[2 * i + m]]
            pr = probe[0, m]
            pi = probe[1, m]
            t_re = pr * er + pi * ei
            t_im = pr * ei - pi * er
            g_re = t_re if g_re is None else g_re + t_re
            g_im = t_im if g_im is None else g_im + t_im
        top, tile, shift, keep = places[i]
        for k, g in ((0, g_re), (1, g_im)):
            g = pltpu.roll(g, shift, 1)
            grad[tile, k, pl.ds(top, PATCH), :] += jnp.where(keep, g, 0.0)
            grad[tile + 1, k, pl.ds(top, PATCH), :] += jnp.where(keep, 0.0, g)


def fill_tables(waves, plus_ref, minus_ref):
    c = waves[0].astype(BF16)
    s = waves[1].astype(BF16)
    plus_ref[:PATCH, :PATCH] = c
    plus_ref[:PATCH, PATCH:] = s
    plus_ref[PATCH:, :PATCH] = -s
    plus_ref[PATCH:, PATCH:] = c
    minus_ref[:PATCH, :PATCH] = c
    minus_ref[:PATCH, PATCH:] = -s
    minus_ref[PATCH:, :PATCH] = s
    minus_ref[PATCH:, PATCH:] = c


def list_slots(wanted, pos, count, listed, photons, photon_buf, photon_sems):
    def list_step(s, found):
        chosen = wanted(pos[0, s])

        @pl.when(chosen)
        def _():
            listed[found] = s
            pltpu.make_async_copy(photons.at[s], photon_buf.at[found], photon_sems.at[found]).start()

        return found + chosen.astype(jnp.int32)

    return lax.fori_loop(0, count, list_step, jnp.int32(0))


def run_slots(found, pos, row_base, listed, field, grad, photons, photon_buf, photon_sems, probe, probe_sum,
              plus_ref, minus_ref):
    def step(k, carry, first=0, width=BLOCK):
        places = [first + k * width + i for i in range(width)]
        at = [jnp.minimum(p, found - 1) for p in places]
        slots = [listed[a] for a in at]
        valids = [jnp.where(p < found, 1.0, 0.0).astype(F32) for p in places]
        for p, a, s in zip(places, at, slots):
            @pl.when(p < found)
            def _(a=a, s=s):
                pltpu.make_async_copy(photons.at[s], photon_buf.at[a], photon_sems.at[a]).wait()

        slot_block(at, slots, valids, pos, row_base, field, grad, photon_buf, probe, probe_sum, plus_ref, minus_ref)
        return carry

    rest = found % BLOCK
    small = (rest > 0) & (rest <= BLOCK // 2)
    blocks = found // BLOCK + ((rest > 0) & jnp.logical_not(small)).astype(jnp.int32)
    lax.fori_loop(0, blocks, step, 0)

    @pl.when(small)
    def _():
        step(0, 0, blocks * BLOCK, BLOCK // 2)


def copies_of(pairs, sems):
    return [pltpu.make_async_copy(a, b, sems.at[i]) for i, (a, b) in enumerate(pairs)]


def start_all(copies):
    for c in copies:
        c.start()


def wait_all(copies):
    for c in copies:
        c.wait()


def by_tiles(array, tiles):
    return [array.at[:, :, pl.ds(t * PATCH, PATCH)] for t in range(tiles)]


def rim_kernel(own, below, right, corner, below_buf, right_buf, sems):
    rim = pl.ds(0, PATCH)
    loads = copies_of([(own.at[:, rim, :], below_buf), (own.at[:, :, rim], right_buf)], sems)
    stores = copies_of(
        [(below_buf, below), (right_buf, right), (below_buf.at[:, :, rim], corner)], sems
    )
    start_all(loads)
    wait_all(loads)
    start_all(stores)
    wait_all(stores)


def upper_kernel(pos, count, own, right, photons, probe_in, waves_in, g_own, g_right, probe_out,
                 field, grad, photon_buf, probe, waves, plus_ref, minus_ref, probe_sum, listed, sems, photon_sems):
    rows, cols = own.shape[1], own.shape[2]
    tiles = cols // PATCH
    loads = copies_of(
        [(waves_in, waves), (probe_in, probe)]
        + [(a, field.at[t]) for t, a in enumerate(by_tiles(own, tiles))]
        + [(right, field.at[tiles])],
        sems,
    )
    start_all(loads)
    found = list_slots(lambda top: top <= rows - PATCH, pos, count[0], listed, photons, photon_buf, photon_sems)
    grad[...] = jnp.zeros(grad.shape, F32)
    probe_sum[...] = jnp.zeros(probe_sum.shape, F32)
    loads[0].wait()
    fill_tables(waves, plus_ref, minus_ref)
    wait_all(loads[1:])
    run_slots(found, pos, 0, listed, field, grad, photons, photon_buf, photon_sems, probe, probe_sum,
              plus_ref, minus_ref)
    stores = copies_of(
        [(probe_sum, probe_out)]
        + [(grad.at[t], a) for t, a in enumerate(by_tiles(g_own, tiles))]
        + [(grad.at[tiles], g_right)],
        sems,
    )
    start_all(stores)
    wait_all(stores)


def lower_kernel(scale, pos, count, core, own, right, below, corner, photons, probe_in, waves_in, own_in, right_in, sum_in,
                 g_own, g_right, g_below, g_corner, kept, sent,
                 field, grad, photon_buf, probe, waves, plus_ref, minus_ref, probe_sum, listed, sems, photon_sems):
    rows, cols = own.shape[1], own.shape[2]
    tiles = cols // PATCH
    base = rows - PATCH
    last, upper, lower = pl.ds(base, PATCH), pl.ds(0, PATCH), pl.ds(PATCH, PATCH)

    def last_rows(array):
        return [array.at[:, last, pl.ds(t * PATCH, PATCH)] for t in range(tiles)]

    loads = copies_of(
        [(waves_in, waves), (probe_in, probe), (sum_in, probe_sum)]
        + [(a, field.at[t, :, upper, :]) for t, a in enumerate(last_rows(own) + [right.at[:, last, :]])]
        + [(a, field.at[t, :, lower, :]) for t, a in enumerate(by_tiles(below, tiles) + [corner])]
        + [(a, grad.at[t, :, upper, :]) for t, a in enumerate(last_rows(own_in) + [right_in.at[:, last, :]])],
        sems,
    )
    start_all(loads)
    found = list_slots(lambda top: top > base, pos, count[0], listed, photons, photon_buf, photon_sems)
    for t in range(tiles + 1):
        grad[t, :, lower, :] = jnp.zeros((2, PATCH, PATCH), F32)
    loads[0].wait()
    fill_tables(waves, plus_ref, minus_ref)
    wait_all(loads[1:])
    run_slots(found, pos, base, listed, field, grad, photons, photon_buf, photon_sems, probe, probe_sum,
              plus_ref, minus_ref)
    probe_sum[...] = probe_sum[...] * scale
    stores = copies_of(
        [(probe_sum.at[core[0]], kept), (probe_sum.at[1 - core[0]], sent)]
        + [(grad.at[t, :, lower, :], a) for t, a in enumerate(by_tiles(g_below, tiles) + [g_corner])]
        + [(grad.at[t, :, upper, :], a) for t, a in enumerate(last_rows(g_own) + [g_right.at[:, last, :]])],
        sems,
    )
    start_all(stores)
    wait_all(stores)


def seam_kernel(core, grad_in, above, left, corner, value, other, grad, probe,
                top_buf, left_buf, above_buf, beside_buf, corner_buf, probe_buf, sems):
    rows, cols = grad.shape[1], grad.shape[2]
    rest = rows - PATCH
    top_rim = grad.at[:, pl.ds(0, PATCH), :]
    left_rim = grad.at[:, pl.ds(PATCH, rest), pl.ds(0, PATCH)]
    loads = copies_of(
        [(top_rim, top_buf), (left_rim, left_buf), (above, above_buf), (left, beside_buf), (corner, corner_buf),
         (value, probe_buf.at[core[0]]), (other, probe_buf.at[1 - core[0]])],
        sems,
    )
    start_all(loads)
    wait_all(loads)
    join = pltpu.make_async_copy(probe_buf, probe, sems.at[2])
    join.start()
    top_buf[:, :, PATCH:] += above_buf[:, :, PATCH:]
    top_buf[:, :, :PATCH] += above_buf[:, :, :PATCH] + (beside_buf[:, :PATCH, :] + corner_buf[...])
    left_buf[...] += beside_buf[:, PATCH:, :]
    stores = copies_of([(top_buf, top_rim), (left_buf, left_rim)], sems)
    start_all(stores)
    wait_all(stores)
    join.wait()


def shape(*dims):
    return jax.ShapeDtypeStruct(dims, F32)


def everyone(value, axes, count):
    sent = jnp.broadcast_to(value[None], (count,) + value.shape)
    return lax.all_to_all(sent, axes, 0, 0, tiled=True)


def body(object_field, probe_modes, photons, positions, counts):
    rows, cols = object_field.shape[1], object_field.shape[2]
    slot_count = photons.shape[2]
    tiles = cols // PATCH
    n_row, n_col = lax.axis_size(ROW), lax.axis_size(COL)
    pos = positions[0, 0].T
    count = counts[0]
    photon_rows = photons[0, 0]
    waves = waves_of(PATCH)
    scale = 1.0 / math.sqrt(n_row * n_col * slot_count)
    down = [(i, i + 1) for i in range(n_row - 1)]
    along = [(i, i + 1) for i in range(n_col - 1)]
    up, back = ([(j, i) for i, j in pairs] for pairs in (down, along))
    diagonal = [
        (a * n_col + b, (a + 1) * n_col + b + 1) for a in range(n_row - 1) for b in range(n_col - 1)
    ]
    diagonal_back = [(j, i) for i, j in diagonal]
    core = lax.axis_index("core")[None]
    smem = pl.BlockSpec(memory_space=pltpu.SMEM)
    hbm = pl.BlockSpec(memory_space=pl.ANY)
    params = pltpu.CompilerParams(vmem_limit_bytes=VMEM_LIMIT)

    rim_shape = shape(2, PATCH, PATCH)
    below, right, corner = pl.pallas_call(
        rim_kernel,
        out_shape=(shape(2, PATCH, cols), shape(2, rows, PATCH), rim_shape),
        in_specs=[hbm],
        out_specs=(hbm,) * 3,
        scratch_shapes=[
            pltpu.VMEM((2, PATCH, cols), F32),
            pltpu.VMEM((2, rows, PATCH), F32),
            pltpu.SemaphoreType.DMA((3,)),
        ],
        compiler_params=params,
        name="rims",
    )(object_field)
    below = lax.ppermute(below, ROW, up)
    right = lax.ppermute(right, COL, back)
    corner = lax.ppermute(corner, BOTH, diagonal_back)

    def scratch(height):
        return [
            pltpu.VMEM((tiles + 1, 2, height, PATCH), F32),
            pltpu.VMEM((tiles + 1, 2, height, PATCH), F32),
            pltpu.VMEM(photon_rows.shape, BF16),
            pltpu.VMEM(probe_modes.shape, F32),
            pltpu.VMEM(waves.shape, F32),
            pltpu.VMEM((2 * PATCH, 2 * PATCH), BF16),
            pltpu.VMEM((2 * PATCH, 2 * PATCH), BF16),
            pltpu.VMEM(probe_modes.shape, F32),
            pltpu.SMEM((slot_count,), jnp.int32),
            pltpu.SemaphoreType.DMA((3 * tiles + 6,)),
            pltpu.SemaphoreType.DMA((slot_count,)),
        ]

    own_shape, right_shape, probe_shape = shape(2, rows, cols), shape(2, rows, PATCH), shape(*probe_modes.shape)
    g_own, g_right, probe_1 = pl.pallas_call(
        upper_kernel,
        out_shape=(own_shape, right_shape, probe_shape),
        in_specs=[smem, smem] + [hbm] * 5,
        out_specs=(hbm,) * 3,
        scratch_shapes=scratch(rows),
        compiler_params=params,
        cost_estimate=pl.CostEstimate(flops=24 * 10**9, bytes_accessed=8 * 2**20, transcendentals=0),
        name="upper_slots",
    )(pos, count, object_field, right, photon_rows, probe_modes, waves)
    g_own, g_right, g_below, g_corner, kept, sent = pl.pallas_call(
        functools.partial(lower_kernel, scale),
        out_shape=(own_shape, right_shape, shape(2, PATCH, cols), rim_shape, rim_shape, rim_shape),
        in_specs=[smem] * 3 + [hbm] * 10,
        out_specs=(hbm,) * 6,
        scratch_shapes=scratch(2 * PATCH),
        input_output_aliases={10: 0, 11: 1},
        compiler_params=params,
        cost_estimate=pl.CostEstimate(flops=8 * 10**9, bytes_accessed=4 * 2**20, transcendentals=0),
        name="lower_slots",
    )(pos, count, core, object_field, right, below, corner, photon_rows, probe_modes, waves, g_own, g_right, probe_1)

    plane, depth = lax.axis_size(PLANE), lax.axis_size(DEPTH)
    swap = [(0, 1), (1, 0)]
    above = lax.ppermute(g_below, ROW, down)
    value = kept + lax.ppermute(sent, "core", swap)
    shares = lax.all_to_all(value.reshape(plane, -1, PATCH), PLANE, 0, 0, tiled=True)
    share = jnp.sum(shares, axis=0)
    share, g_right, g_corner = lax.optimization_barrier((share, g_right, g_corner))
    left = lax.ppermute(g_right, COL, along)
    from_corner = lax.ppermute(g_corner, BOTH, diagonal)
    share = jnp.sum(everyone(share, DEPTH, depth), axis=0)
    share, above = lax.optimization_barrier((share, above))
    value = everyone(share, PLANE, plane).reshape(kept.shape)
    other = lax.ppermute(value, "core", swap)

    object_gradient, probe_gradient = pl.pallas_call(
        seam_kernel,
        out_shape=(own_shape, probe_shape),
        in_specs=[smem] + [hbm] * 6,
        out_specs=(hbm, hbm),
        scratch_shapes=[
            pltpu.VMEM((2, PATCH, cols), F32),
            pltpu.VMEM((2, rows - PATCH, PATCH), F32),
            pltpu.VMEM((2, PATCH, cols), F32),
            pltpu.VMEM((2, rows, PATCH), F32),
            pltpu.VMEM((2, PATCH, PATCH), F32),
            pltpu.VMEM(probe_modes.shape, F32),
            pltpu.SemaphoreType.DMA((7,)),
        ],
        input_output_aliases={1: 0},
        compiler_params=pltpu.CompilerParams(vmem_limit_bytes=8 * 2**20),
        name="seams",
    )(core, g_own, above, left, from_corner, value, other)
    return (object_gradient, probe_gradient)


def solution(mesh):
    fine = Mesh(mesh.devices.reshape(4, 4, 4, 2, 2), BOTH)
    in_specs = (
        P(None, ROW, COL),
        P(),
        P(ROW, COL, None, None, None),
        P(ROW, COL, None, None),
        P(ROW, COL),
    )
    out_specs = (P(None, ROW, COL), P())
    return jax.shard_map(body, mesh=fine, in_specs=in_specs, out_specs=out_specs, check_vma=False)
```

```python
import functools
import math

import jax
import jax.numpy as jnp
import numpy as np
from jax import lax
from jax.experimental import pallas as pl
from jax.experimental.pallas import tpu as pltpu
from jax.sharding import Mesh
from jax.sharding import PartitionSpec as P

F32 = jnp.float32
BF16 = jnp.bfloat16
PATCH = 128
BLOCK = 8
VMEM_LIMIT = 63 * 2**20
ROW = "z_hi"
COL = ("x", "y", "z_lo", "core")
BOTH = (ROW,) + COL
PLANE = ("x", "y")
DEPTH = ("z_hi", "z_lo")


def waves_of(patch_len):
    index_range = np.arange(patch_len)
    product = (index_range[:, None] * index_range[None, :]) % patch_len
    angle = product.astype(np.float32) * np.float32(2.0 * math.pi / patch_len)
    pair = np.stack([np.cos(angle), np.sin(angle)]) / np.float32(math.sqrt(patch_len))
    return jnp.asarray(pair, F32)


def dot(a, b):
    return jnp.dot(a, b, preferred_element_type=F32)


def slot_block(at, slots, valids, pos, row_base, field, grad, photons, probe, probe_sum, plus_ref, minus_ref):
    n = len(slots)
    lane = lax.broadcasted_iota(jnp.int32, (PATCH, PATCH), 1)
    plus = plus_ref[...]
    minus = minus_ref[...]
    places, patches, waves = [], [], []
    for s in slots:
        top = pos[0, s] - row_base
        left = pos[1, s]
        tile = left // PATCH
        shift = left % PATCH
        back = (PATCH - shift) % PATCH
        keep = lane >= shift
        patch = []
        for k in range(2):
            a = field[tile, k, pl.ds(top, PATCH), :]
            b = field[tile + 1, k, pl.ds(top, PATCH), :]
            patch.append(pltpu.roll(jnp.where(keep, a, b), back, 1))
        places.append((top, tile, shift, keep))
        patches.append(patch)
        for m in range(2):
            pr = probe[0, m]
            pi = probe[1, m]
            wr = (pr * patch[0] - pi * patch[1]).astype(BF16)
            wi = (pr * patch[1] + pi * patch[0]).astype(BF16)
            waves.append(jnp.concatenate([wr, wi], axis=0))
    first = dot(plus, jnp.concatenate(waves, axis=1)).astype(BF16)
    cols = [slice(q * PATCH, (q + 1) * PATCH) for q in range(2 * n)]
    turned = [jnp.concatenate([first[:PATCH, q], first[PATCH:, q]], axis=1) for q in cols]
    far = dot(jnp.concatenate(turned, axis=0), minus)
    scaled = []
    for i in range(n):
        f0 = far[2 * i * PATCH:(2 * i + 1) * PATCH]
        f1 = far[(2 * i + 1) * PATCH:(2 * i + 2) * PATCH]
        power = f0 * f0 + f1 * f1
        intensity = power[:, :PATCH] + power[:, PATCH:]
        factor = (1.0 - photons[at[i]].astype(F32) / (intensity + 1.0)) * valids[i]
        for f in (f0, f1):
            re = (f[:, :PATCH] * factor).astype(BF16)
            im = (f[:, PATCH:] * factor).astype(BF16)
            scaled.append(jnp.concatenate([re, im], axis=1))
    back_pass = dot(jnp.concatenate(scaled, axis=0), plus).astype(BF16)
    unturned = [jnp.concatenate([back_pass[q, :PATCH], back_pass[q, PATCH:]], axis=0) for q in cols]
    exit_grad = dot(minus, jnp.concatenate(unturned, axis=1))
    for m in range(2):
        sum_re = sum_im = None
        for i in range(n):
            er = exit_grad[:PATCH, cols[2 * i + m]]
            ei = exit_grad[PATCH:, cols[2 * i + m]]
            o_re, o_im = patches[i]
            t_re = o_re * er + o_im * ei
            t_im = o_re * ei - o_im * er
            sum_re = t_re if sum_re is None else sum_re + t_re
            sum_im = t_im if sum_im is None else sum_im + t_im
        probe_sum[0, m] += sum_re
        probe_sum[1, m] += sum_im
    for i in range(n):
        g_re = g_im = None
        for m in range(2):
            er = exit_grad[:PATCH, cols[2 * i + m]]
            ei = exit_grad[PATCH:, cols[2 * i + m]]
            pr = probe[0, m]
            pi = probe[1, m]
            t_re = pr * er + pi * ei
            t_im = pr * ei - pi * er
            g_re = t_re if g_re is None else g_re + t_re
            g_im = t_im if g_im is None else g_im + t_im
        top, tile, shift, keep = places[i]
        for k, g in ((0, g_re), (1, g_im)):
            g = pltpu.roll(g, shift, 1)
            grad[tile, k, pl.ds(top, PATCH), :] += jnp.where(keep, g, 0.0)
            grad[tile + 1, k, pl.ds(top, PATCH), :] += jnp.where(keep, 0.0, g)


def fill_tables(waves, plus_ref, minus_ref):
    c = waves[0].astype(BF16)
    s = waves[1].astype(BF16)
    plus_ref[:PATCH, :PATCH] = c
    plus_ref[:PATCH, PATCH:] = s
    plus_ref[PATCH:, :PATCH] = -s
    plus_ref[PATCH:, PATCH:] = c
    minus_ref[:PATCH, :PATCH] = c
    minus_ref[:PATCH, PATCH:] = -s
    minus_ref[PATCH:, :PATCH] = s
    minus_ref[PATCH:, PATCH:] = c


def list_slots(wanted, pos, count, listed, photons, photon_buf, photon_sems):
    def list_step(s, found):
        chosen = wanted(pos[0, s])

        @pl.when(chosen)
        def _():
            listed[found] = s
            pltpu.make_async_copy(photons.at[s], photon_buf.at[found], photon_sems.at[found]).start()

        return found + chosen.astype(jnp.int32)

    return lax.fori_loop(0, count, list_step, jnp.int32(0))


def run_slots(found, pos, row_base, listed, field, grad, photons, photon_buf, photon_sems, probe, probe_sum,
              plus_ref, minus_ref):
    def step(k, carry, first=0, width=BLOCK):
        places = [first + k * width + i for i in range(width)]
        at = [jnp.minimum(p, found - 1) for p in places]
        slots = [listed[a] for a in at]
        valids = [jnp.where(p < found, 1.0, 0.0).astype(F32) for p in places]
        for p, a, s in zip(places, at, slots):
            @pl.when(p < found)
            def _(a=a, s=s):
                pltpu.make_async_copy(photons.at[s], photon_buf.at[a], photon_sems.at[a]).wait()

        slot_block(at, slots, valids, pos, row_base, field, grad, photon_buf, probe, probe_sum, plus_ref, minus_ref)
        return carry

    rest = found % BLOCK
    small = (rest > 0) & (rest <= BLOCK // 2)
    blocks = found // BLOCK + ((rest > 0) & jnp.logical_not(small)).astype(jnp.int32)
    lax.fori_loop(0, blocks, step, 0)

    @pl.when(small)
    def _():
        step(0, 0, blocks * BLOCK, BLOCK // 2)


def copies_of(pairs, sems):
    return [pltpu.make_async_copy(a, b, sems.at[i]) for i, (a, b) in enumerate(pairs)]


def start_all(copies):
    for c in copies:
        c.start()


def wait_all(copies):
    for c in copies:
        c.wait()


def by_tiles(array, tiles):
    return [array.at[:, :, pl.ds(t * PATCH, PATCH)] for t in range(tiles)]


def rim_kernel(own, below, right, below_buf, right_buf, sems):
    rim = pl.ds(0, PATCH)
    loads = copies_of([(own.at[:, rim, :], below_buf), (own.at[:, :, rim], right_buf)], sems)
    stores = copies_of([(below_buf, below), (right_buf, right)], sems)
    start_all(loads)
    wait_all(loads)
    start_all(stores)
    wait_all(stores)


def upper_kernel(pos, count, own, right, photons, probe_in, waves_in, g_own, g_right, probe_out,
                 field, grad, photon_buf, probe, waves, plus_ref, minus_ref, probe_sum, listed, sems, photon_sems):
    rows, cols = own.shape[1], own.shape[2]
    tiles = cols // PATCH
    loads = copies_of(
        [(waves_in, waves), (probe_in, probe)]
        + [(a, field.at[t]) for t, a in enumerate(by_tiles(own, tiles))]
        + [(right, field.at[tiles])],
        sems,
    )
    start_all(loads)
    found = list_slots(lambda top: top <= rows - PATCH, pos, count[0], listed, photons, photon_buf, photon_sems)
    grad[...] = jnp.zeros(grad.shape, F32)
    probe_sum[...] = jnp.zeros(probe_sum.shape, F32)
    loads[0].wait()
    fill_tables(waves, plus_ref, minus_ref)
    wait_all(loads[1:])
    run_slots(found, pos, 0, listed, field, grad, photons, photon_buf, photon_sems, probe, probe_sum,
              plus_ref, minus_ref)
    stores = copies_of(
        [(probe_sum, probe_out)]
        + [(grad.at[t], a) for t, a in enumerate(by_tiles(g_own, tiles))]
        + [(grad.at[tiles], g_right)],
        sems,
    )
    start_all(stores)
    wait_all(stores)


def lower_kernel(scale, pos, count, core, own, right, below, corner, photons, probe_in, waves_in, own_in, right_in, sum_in,
                 g_own, g_right, g_below, kept, sent,
                 field, grad, photon_buf, probe, waves, plus_ref, minus_ref, probe_sum, listed, sems, photon_sems):
    rows, cols = own.shape[1], own.shape[2]
    tiles = cols // PATCH
    base = rows - PATCH
    last, upper, lower = pl.ds(base, PATCH), pl.ds(0, PATCH), pl.ds(PATCH, PATCH)

    def last_rows(array):
        return [array.at[:, last, pl.ds(t * PATCH, PATCH)] for t in range(tiles)]

    loads = copies_of(
        [(waves_in, waves), (probe_in, probe), (sum_in, probe_sum)]
        + [(a, field.at[t, :, upper, :]) for t, a in enumerate(last_rows(own) + [right.at[:, last, :]])]
        + [(a, field.at[t, :, lower, :]) for t, a in enumerate(by_tiles(below, tiles) + [corner])]
        + [(a, grad.at[t, :, upper, :]) for t, a in enumerate(last_rows(own_in) + [right_in.at[:, last, :]])],
        sems,
    )
    start_all(loads)
    found = list_slots(lambda top: top > base, pos, count[0], listed, photons, photon_buf, photon_sems)
    for t in range(tiles + 1):
        grad[t, :, lower, :] = jnp.zeros((2, PATCH, PATCH), F32)
    loads[0].wait()
    fill_tables(waves, plus_ref, minus_ref)
    wait_all(loads[1:])
    run_slots(found, pos, base, listed, field, grad, photons, photon_buf, photon_sems, probe, probe_sum,
              plus_ref, minus_ref)
    probe_sum[...] = probe_sum[...] * scale
    stores = copies_of(
        [(probe_sum.at[core[0]], kept), (probe_sum.at[1 - core[0]], sent)]
        + [(grad.at[t, :, lower, :], a) for t, a in enumerate(by_tiles(g_below, tiles + 1))]
        + [(grad.at[t, :, upper, :], a) for t, a in enumerate(last_rows(g_own) + [g_right.at[:, last, :]])],
        sems,
    )
    start_all(stores)
    wait_all(stores)


def seam_kernel(core, grad_in, above, left, value, other, grad, probe,
                top_buf, left_buf, above_buf, beside_buf, probe_buf, sems):
    rows, cols = grad.shape[1], grad.shape[2]
    rest = rows - PATCH
    top_rim = grad.at[:, pl.ds(0, PATCH), :]
    left_rim = grad.at[:, pl.ds(PATCH, rest), pl.ds(0, PATCH)]
    loads = copies_of(
        [(top_rim, top_buf), (left_rim, left_buf), (above.at[:, :, pl.ds(0, cols)], above_buf), (left, beside_buf),
         (value, probe_buf.at[core[0]]), (other, probe_buf.at[1 - core[0]])],
        sems,
    )
    start_all(loads)
    wait_all(loads)
    join = pltpu.make_async_copy(probe_buf, probe, sems.at[2])
    join.start()
    top_buf[:, :, PATCH:] += above_buf[:, :, PATCH:]
    top_buf[:, :, :PATCH] += above_buf[:, :, :PATCH] + beside_buf[:, :PATCH, :]
    left_buf[...] += beside_buf[:, PATCH:, :]
    stores = copies_of([(top_buf, top_rim), (left_buf, left_rim)], sems)
    start_all(stores)
    wait_all(stores)
    join.wait()


def shape(*dims):
    return jax.ShapeDtypeStruct(dims, F32)


def everyone(value, axes, count):
    sent = jnp.broadcast_to(value[None], (count,) + value.shape)
    return lax.all_to_all(sent, axes, 0, 0, tiled=True)


def body(object_field, probe_modes, photons, positions, counts):
    rows, cols = object_field.shape[1], object_field.shape[2]
    slot_count = photons.shape[2]
    tiles = cols // PATCH
    n_row, n_col = lax.axis_size(ROW), lax.axis_size(COL)
    pos = positions[0, 0].T
    count = counts[0]
    photon_rows = photons[0, 0]
    waves = waves_of(PATCH)
    scale = 1.0 / math.sqrt(n_row * n_col * slot_count)
    down = [(i, i + 1) for i in range(n_row - 1)]
    along = [(i, i + 1) for i in range(n_col - 1)]
    up, back = ([(j, i) for i, j in pairs] for pairs in (down, along))
    core = lax.axis_index("core")[None]
    smem = pl.BlockSpec(memory_space=pltpu.SMEM)
    hbm = pl.BlockSpec(memory_space=pl.ANY)
    params = pltpu.CompilerParams(vmem_limit_bytes=VMEM_LIMIT)

    rim_shape = shape(2, PATCH, PATCH)
    below, right = pl.pallas_call(
        rim_kernel,
        out_shape=(shape(2, PATCH, cols), shape(2, rows, PATCH)),
        in_specs=[hbm],
        out_specs=(hbm,) * 2,
        scratch_shapes=[
            pltpu.VMEM((2, PATCH, cols), F32),
            pltpu.VMEM((2, rows, PATCH), F32),
            pltpu.SemaphoreType.DMA((2,)),
        ],
        compiler_params=params,
        name="rims",
    )(object_field)
    right = lax.ppermute(right, COL, back)
    below, right = lax.optimization_barrier((below, right))
    below = lax.ppermute(below, ROW, up)

    def scratch(height):
        return [
            pltpu.VMEM((tiles + 1, 2, height, PATCH), F32),
            pltpu.VMEM((tiles + 1, 2, height, PATCH), F32),
            pltpu.VMEM(photon_rows.shape, BF16),
            pltpu.VMEM(probe_modes.shape, F32),
            pltpu.VMEM(waves.shape, F32),
            pltpu.VMEM((2 * PATCH, 2 * PATCH), BF16),
            pltpu.VMEM((2 * PATCH, 2 * PATCH), BF16),
            pltpu.VMEM(probe_modes.shape, F32),
            pltpu.SMEM((slot_count,), jnp.int32),
            pltpu.SemaphoreType.DMA((3 * tiles + 6,)),
            pltpu.SemaphoreType.DMA((slot_count,)),
        ]

    own_shape, right_shape, probe_shape = shape(2, rows, cols), shape(2, rows, PATCH), shape(*probe_modes.shape)
    g_own, g_right, probe_1 = pl.pallas_call(
        upper_kernel,
        out_shape=(own_shape, right_shape, probe_shape),
        in_specs=[smem, smem] + [hbm] * 5,
        out_specs=(hbm,) * 3,
        scratch_shapes=scratch(rows),
        compiler_params=params,
        cost_estimate=pl.CostEstimate(flops=24 * 10**9, bytes_accessed=8 * 2**20, transcendentals=0),
        name="upper_slots",
    )(pos, count, object_field, right, photon_rows, probe_modes, waves)
    below, probe_1 = lax.optimization_barrier((below, probe_1))
    corner = lax.ppermute(below[:, :, :PATCH], COL, back)
    g_own, g_right, g_below, kept, sent = pl.pallas_call(
        functools.partial(lower_kernel, scale),
        out_shape=(own_shape, right_shape, shape(2, PATCH, cols + PATCH), rim_shape, rim_shape),
        in_specs=[smem] * 3 + [hbm] * 10,
        out_specs=(hbm,) * 5,
        scratch_shapes=scratch(2 * PATCH),
        input_output_aliases={10: 0, 11: 1},
        compiler_params=params,
        cost_estimate=pl.CostEstimate(flops=8 * 10**9, bytes_accessed=4 * 2**20, transcendentals=0),
        name="lower_slots",
    )(pos, count, core, object_field, right, below, corner, photon_rows, probe_modes, waves, g_own, g_right, probe_1)

    plane, depth = lax.axis_size(PLANE), lax.axis_size(DEPTH)
    swap = [(0, 1), (1, 0)]
    above = lax.ppermute(g_below, ROW, down)
    value = kept + lax.ppermute(sent, "core", swap)
    shares = lax.all_to_all(value.reshape(plane, -1, PATCH), PLANE, 0, 0, tiled=True)
    share = jnp.sum(shares, axis=0)
    share = jnp.sum(everyone(share, DEPTH, depth), axis=0)
    share, above = lax.optimization_barrier((share, above))
    left = lax.ppermute(g_right.at[:, :PATCH, :].add(above[:, :, cols:]), COL, along)
    value = everyone(share, PLANE, plane).reshape(kept.shape)
    other = lax.ppermute(value, "core", swap)

    object_gradient, probe_gradient = pl.pallas_call(
        seam_kernel,
        out_shape=(own_shape, probe_shape),
        in_specs=[smem] + [hbm] * 5,
        out_specs=(hbm, hbm),
        scratch_shapes=[
            pltpu.VMEM((2, PATCH, cols), F32),
            pltpu.VMEM((2, rows - PATCH, PATCH), F32),
            pltpu.VMEM((2, PATCH, cols), F32),
            pltpu.VMEM((2, rows, PATCH), F32),
            pltpu.VMEM(probe_modes.shape, F32),
            pltpu.SemaphoreType.DMA((6,)),
        ],
        input_output_aliases={1: 0},
        compiler_params=pltpu.CompilerParams(vmem_limit_bytes=8 * 2**20),
        name="seams",
    )(core, g_own, above, left, value, other)
    return (object_gradient, probe_gradient)


def solution(mesh):
    fine = Mesh(mesh.devices.reshape(4, 4, 4, 2, 2), BOTH)
    in_specs = (
        P(None, ROW, COL),
        P(),
        P(ROW, COL, None, None, None),
        P(ROW, COL, None, None),
        P(ROW, COL),
    )
    out_specs = (P(None, ROW, COL), P())
    return jax.shard_map(body, mesh=fine, in_specs=in_specs, out_specs=out_specs, check_vma=False)
```

```python
import functools
import math

import jax
import jax.numpy as jnp
import numpy as np
from jax import lax
from jax.experimental import pallas as pl
from jax.experimental.pallas import tpu as pltpu
from jax.sharding import Mesh
from jax.sharding import PartitionSpec as P

F32 = jnp.float32
BF16 = jnp.bfloat16
PATCH = 128
BLOCK = 8
VMEM_LIMIT = 63 * 2**20
ROW = "z_hi"
COL = ("x", "y", "z_lo", "core")
BOTH = (ROW,) + COL
PLANE = ("x", "y")
DEPTH = ("z_hi", "z_lo")


def waves_of(patch_len):
    index_range = np.arange(patch_len)
    product = (index_range[:, None] * index_range[None, :]) % patch_len
    angle = product.astype(np.float32) * np.float32(2.0 * math.pi / patch_len)
    pair = np.stack([np.cos(angle), np.sin(angle)]) / np.float32(math.sqrt(patch_len))
    return jnp.asarray(pair, F32)


def dot(a, b):
    return jnp.dot(a, b, preferred_element_type=F32)


def slot_block(at, slots, valids, pos, row_base, field, grad, photons, probe, probe_sum, plus_ref, minus_ref):
    n = len(slots)
    lane = lax.broadcasted_iota(jnp.int32, (PATCH, PATCH), 1)
    plus = plus_ref[...]
    minus = minus_ref[...]
    places, patches, waves = [], [], []
    for s in slots:
        top = pos[0, s] - row_base
        left = pos[1, s]
        tile = left // PATCH
        shift = left % PATCH
        back = (PATCH - shift) % PATCH
        keep = lane >= shift
        patch = []
        for k in range(2):
            a = field[tile, k, pl.ds(top, PATCH), :]
            b = field[tile + 1, k, pl.ds(top, PATCH), :]
            patch.append(pltpu.roll(jnp.where(keep, a, b), back, 1))
        places.append((top, tile, shift, keep))
        patches.append(patch)
        for m in range(2):
            pr = probe[0, m]
            pi = probe[1, m]
            wr = (pr * patch[0] - pi * patch[1]).astype(BF16)
            wi = (pr * patch[1] + pi * patch[0]).astype(BF16)
            waves.append(jnp.concatenate([wr, wi], axis=0))
    first = dot(plus, jnp.concatenate(waves, axis=1)).astype(BF16)
    cols = [slice(q * PATCH, (q + 1) * PATCH) for q in range(2 * n)]
    turned = [jnp.concatenate([first[:PATCH, q], first[PATCH:, q]], axis=1) for q in cols]
    far = dot(jnp.concatenate(turned, axis=0), minus)
    scaled = []
    for i in range(n):
        f0 = far[2 * i * PATCH:(2 * i + 1) * PATCH]
        f1 = far[(2 * i + 1) * PATCH:(2 * i + 2) * PATCH]
        power = f0 * f0 + f1 * f1
        intensity = power[:, :PATCH] + power[:, PATCH:]
        factor = (1.0 - photons[at[i]].astype(F32) / (intensity + 1.0)) * valids[i]
        for f in (f0, f1):
            re = (f[:, :PATCH] * factor).astype(BF16)
            im = (f[:, PATCH:] * factor).astype(BF16)
            scaled.append(jnp.concatenate([re, im], axis=1))
    back_pass = dot(jnp.concatenate(scaled, axis=0), plus).astype(BF16)
    unturned = [jnp.concatenate([back_pass[q, :PATCH], back_pass[q, PATCH:]], axis=0) for q in cols]
    exit_grad = dot(minus, jnp.concatenate(unturned, axis=1))
    for m in range(2):
        sum_re = sum_im = None
        for i in range(n):
            er = exit_grad[:PATCH, cols[2 * i + m]]
            ei = exit_grad[PATCH:, cols[2 * i + m]]
            o_re, o_im = patches[i]
            t_re = o_re * er + o_im * ei
            t_im = o_re * ei - o_im * er
            sum_re = t_re if sum_re is None else sum_re + t_re
            sum_im = t_im if sum_im is None else sum_im + t_im
        probe_sum[0, m] += sum_re
        probe_sum[1, m] += sum_im
    for i in range(n):
        g_re = g_im = None
        for m in range(2):
            er = exit_grad[:PATCH, cols[2 * i + m]]
            ei = exit_grad[PATCH:, cols[2 * i + m]]
            pr = probe[0, m]
            pi = probe[1, m]
            t_re = pr * er + pi * ei
            t_im = pr * ei - pi * er
            g_re = t_re if g_re is None else g_re + t_re
            g_im = t_im if g_im is None else g_im + t_im
        top, tile, shift, keep = places[i]
        for k, g in ((0, g_re), (1, g_im)):
            g = pltpu.roll(g, shift, 1)
            grad[tile, k, pl.ds(top, PATCH), :] += jnp.where(keep, g, 0.0)
            grad[tile + 1, k, pl.ds(top, PATCH), :] += jnp.where(keep, 0.0, g)


def fill_tables(waves, plus_ref, minus_ref):
    c = waves[0].astype(BF16)
    s = waves[1].astype(BF16)
    plus_ref[:PATCH, :PATCH] = c
    plus_ref[:PATCH, PATCH:] = s
    plus_ref[PATCH:, :PATCH] = -s
    plus_ref[PATCH:, PATCH:] = c
    minus_ref[:PATCH, :PATCH] = c
    minus_ref[:PATCH, PATCH:] = -s
    minus_ref[PATCH:, :PATCH] = s
    minus_ref[PATCH:, PATCH:] = c


def list_slots(wanted, pos, count, listed, photons, photon_buf, photon_sems):
    def list_step(s, found):
        chosen = wanted(pos[0, s])

        @pl.when(chosen)
        def _():
            listed[found] = s
            pltpu.make_async_copy(photons.at[s], photon_buf.at[found], photon_sems.at[found]).start()

        return found + chosen.astype(jnp.int32)

    return lax.fori_loop(0, count, list_step, jnp.int32(0))


def run_slots(found, pos, row_base, listed, field, grad, photons, photon_buf, photon_sems, probe, probe_sum,
              plus_ref, minus_ref):
    def step(k, carry, first=0, width=BLOCK):
        places = [first + k * width + i for i in range(width)]
        at = [jnp.minimum(p, found - 1) for p in places]
        slots = [listed[a] for a in at]
        valids = [jnp.where(p < found, 1.0, 0.0).astype(F32) for p in places]
        for p, a, s in zip(places, at, slots):
            @pl.when(p < found)
            def _(a=a, s=s):
                pltpu.make_async_copy(photons.at[s], photon_buf.at[a], photon_sems.at[a]).wait()

        slot_block(at, slots, valids, pos, row_base, field, grad, photon_buf, probe, probe_sum, plus_ref, minus_ref)
        return carry

    rest = found % BLOCK
    small = (rest > 0) & (rest <= BLOCK // 2)
    blocks = found // BLOCK + ((rest > 0) & jnp.logical_not(small)).astype(jnp.int32)
    lax.fori_loop(0, blocks, step, 0)

    @pl.when(small)
    def _():
        step(0, 0, blocks * BLOCK, BLOCK // 2)


def copies_of(pairs, sems):
    return [pltpu.make_async_copy(a, b, sems.at[i]) for i, (a, b) in enumerate(pairs)]


def start_all(copies):
    for c in copies:
        c.start()


def wait_all(copies):
    for c in copies:
        c.wait()


def by_tiles(array, tiles):
    return [array.at[:, :, pl.ds(t * PATCH, PATCH)] for t in range(tiles)]


def rim_kernel(own, below, right, corner, below_buf, right_buf, sems):
    rim = pl.ds(0, PATCH)
    loads = copies_of([(own.at[:, rim, :], below_buf), (own.at[:, :, rim], right_buf)], sems)
    stores = copies_of(
        [(below_buf, below), (right_buf, right), (below_buf.at[:, :, rim], corner)], sems
    )
    start_all(loads)
    wait_all(loads)
    start_all(stores)
    wait_all(stores)


def upper_kernel(pos, count, own, right, photons, probe_in, waves_in, g_own, g_right, probe_out,
                 field, grad, photon_buf, probe, waves, plus_ref, minus_ref, probe_sum, listed, sems, photon_sems):
    rows, cols = own.shape[1], own.shape[2]
    tiles = cols // PATCH
    loads = copies_of(
        [(waves_in, waves), (probe_in, probe)]
        + [(a, field.at[t]) for t, a in enumerate(by_tiles(own, tiles))]
        + [(right, field.at[tiles])],
        sems,
    )
    start_all(loads)
    found = list_slots(lambda top: top <= rows - PATCH, pos, count[0], listed, photons, photon_buf, photon_sems)
    grad[...] = jnp.zeros(grad.shape, F32)
    probe_sum[...] = jnp.zeros(probe_sum.shape, F32)
    loads[0].wait()
    fill_tables(waves, plus_ref, minus_ref)
    wait_all(loads[1:])
    run_slots(found, pos, 0, listed, field, grad, photons, photon_buf, photon_sems, probe, probe_sum,
              plus_ref, minus_ref)
    stores = copies_of(
        [(probe_sum, probe_out)]
        + [(grad.at[t], a) for t, a in enumerate(by_tiles(g_own, tiles))]
        + [(grad.at[tiles], g_right)],
        sems,
    )
    start_all(stores)
    wait_all(stores)


def lower_kernel(scale, pos, count, core, own, right, below, corner, photons, probe_in, waves_in, own_in, right_in, sum_in,
                 g_own, g_right, g_below, g_corner, kept, sent,
                 field, grad, photon_buf, probe, waves, plus_ref, minus_ref, probe_sum, listed, sems, photon_sems):
    rows, cols = own.shape[1], own.shape[2]
    tiles = cols // PATCH
    base = rows - PATCH
    last, upper, lower = pl.ds(base, PATCH), pl.ds(0, PATCH), pl.ds(PATCH, PATCH)

    def last_rows(array):
        return [array.at[:, last, pl.ds(t * PATCH, PATCH)] for t in range(tiles)]

    loads = copies_of(
        [(waves_in, waves), (probe_in, probe), (sum_in, probe_sum)]
        + [(a, field.at[t, :, upper, :]) for t, a in enumerate(last_rows(own) + [right.at[:, last, :]])]
        + [(a, field.at[t, :, lower, :]) for t, a in enumerate(by_tiles(below, tiles) + [corner])]
        + [(a, grad.at[t, :, upper, :]) for t, a in enumerate(last_rows(own_in) + [right_in.at[:, last, :]])],
        sems,
    )
    start_all(loads)
    found = list_slots(lambda top: top > base, pos, count[0], listed, photons, photon_buf, photon_sems)
    for t in range(tiles + 1):
        grad[t, :, lower, :] = jnp.zeros((2, PATCH, PATCH), F32)
    loads[0].wait()
    fill_tables(waves, plus_ref, minus_ref)
    wait_all(loads[1:])
    run_slots(found, pos, base, listed, field, grad, photons, photon_buf, photon_sems, probe, probe_sum,
              plus_ref, minus_ref)
    probe_sum[...] = probe_sum[...] * scale
    stores = copies_of(
        [(probe_sum.at[core[0]], kept), (probe_sum.at[1 - core[0]], sent)]
        + [(grad.at[t, :, lower, :], a) for t, a in enumerate(by_tiles(g_below, tiles) + [g_corner])]
        + [(grad.at[t, :, upper, :], a) for t, a in enumerate(last_rows(g_own) + [g_right.at[:, last, :]])],
        sems,
    )
    start_all(stores)
    wait_all(stores)


def seam_kernel(grad_in, above, left, corner, parts, grad, probe,
                top_buf, left_buf, above_buf, beside_buf, corner_buf, probe_buf, sems):
    rows, cols = grad.shape[1], grad.shape[2]
    rest = rows - PATCH
    top_rim = grad.at[:, pl.ds(0, PATCH), :]
    left_rim = grad.at[:, pl.ds(PATCH, rest), pl.ds(0, PATCH)]
    loads = copies_of(
        [(top_rim, top_buf), (left_rim, left_buf), (above, above_buf), (left, beside_buf), (corner, corner_buf),
         (parts.at[:, 0], probe_buf.at[0]), (parts.at[:, 1], probe_buf.at[1])],
        sems,
    )
    start_all(loads)
    wait_all(loads)
    join = pltpu.make_async_copy(probe_buf, probe, sems.at[2])
    join.start()
    top_buf[:, :, PATCH:] += above_buf[:, :, PATCH:]
    top_buf[:, :, :PATCH] += above_buf[:, :, :PATCH] + (beside_buf[:, :PATCH, :] + corner_buf[...])
    left_buf[...] += beside_buf[:, PATCH:, :]
    stores = copies_of([(top_buf, top_rim), (left_buf, left_rim)], sems)
    start_all(stores)
    wait_all(stores)
    join.wait()


def shape(*dims):
    return jax.ShapeDtypeStruct(dims, F32)


def everyone(value, axes, count):
    sent = jnp.broadcast_to(value[None], (count,) + value.shape)
    return lax.all_to_all(sent, axes, 0, 0, tiled=True)


def body(object_field, probe_modes, photons, positions, counts):
    rows, cols = object_field.shape[1], object_field.shape[2]
    slot_count = photons.shape[2]
    tiles = cols // PATCH
    n_row, n_col = lax.axis_size(ROW), lax.axis_size(COL)
    pos = positions[0, 0].T
    count = counts[0]
    photon_rows = photons[0, 0]
    waves = waves_of(PATCH)
    scale = 1.0 / math.sqrt(n_row * n_col * slot_count)
    down = [(i, i + 1) for i in range(n_row - 1)]
    along = [(i, i + 1) for i in range(n_col - 1)]
    up, back = ([(j, i) for i, j in pairs] for pairs in (down, along))
    diagonal = [
        (a * n_col + b, (a + 1) * n_col + b + 1) for a in range(n_row - 1) for b in range(n_col - 1)
    ]
    diagonal_back = [(j, i) for i, j in diagonal]
    core = lax.axis_index("core")[None]
    smem = pl.BlockSpec(memory_space=pltpu.SMEM)
    hbm = pl.BlockSpec(memory_space=pl.ANY)
    params = pltpu.CompilerParams(vmem_limit_bytes=VMEM_LIMIT)

    rim_shape = shape(2, PATCH, PATCH)
    below, right, corner = pl.pallas_call(
        rim_kernel,
        out_shape=(shape(2, PATCH, cols), shape(2, rows, PATCH), rim_shape),
        in_specs=[hbm],
        out_specs=(hbm,) * 3,
        scratch_shapes=[
            pltpu.VMEM((2, PATCH, cols), F32),
            pltpu.VMEM((2, rows, PATCH), F32),
            pltpu.SemaphoreType.DMA((3,)),
        ],
        compiler_params=params,
        name="rims",
    )(object_field)
    below = lax.ppermute(below, ROW, up)
    right = lax.ppermute(right, COL, back)
    corner = lax.ppermute(corner, BOTH, diagonal_back)

    def scratch(height):
        return [
            pltpu.VMEM((tiles + 1, 2, height, PATCH), F32),
            pltpu.VMEM((tiles + 1, 2, height, PATCH), F32),
            pltpu.VMEM(photon_rows.shape, BF16),
            pltpu.VMEM(probe_modes.shape, F32),
            pltpu.VMEM(waves.shape, F32),
            pltpu.VMEM((2 * PATCH, 2 * PATCH), BF16),
            pltpu.VMEM((2 * PATCH, 2 * PATCH), BF16),
            pltpu.VMEM(probe_modes.shape, F32),
            pltpu.SMEM((slot_count,), jnp.int32),
            pltpu.SemaphoreType.DMA((3 * tiles + 6,)),
            pltpu.SemaphoreType.DMA((slot_count,)),
        ]

    own_shape, right_shape, probe_shape = shape(2, rows, cols), shape(2, rows, PATCH), shape(*probe_modes.shape)
    g_own, g_right, probe_1 = pl.pallas_call(
        upper_kernel,
        out_shape=(own_shape, right_shape, probe_shape),
        in_specs=[smem, smem] + [hbm] * 5,
        out_specs=(hbm,) * 3,
        scratch_shapes=scratch(rows),
        compiler_params=params,
        cost_estimate=pl.CostEstimate(flops=24 * 10**9, bytes_accessed=8 * 2**20, transcendentals=0),
        name="upper_slots",
    )(pos, count, object_field, right, photon_rows, probe_modes, waves)
    g_own, g_right, g_below, g_corner, kept, sent = pl.pallas_call(
        functools.partial(lower_kernel, scale),
        out_shape=(own_shape, right_shape, shape(2, PATCH, cols), rim_shape, rim_shape, rim_shape),
        in_specs=[smem] * 3 + [hbm] * 10,
        out_specs=(hbm,) * 6,
        scratch_shapes=scratch(2 * PATCH),
        input_output_aliases={10: 0, 11: 1},
        compiler_params=params,
        cost_estimate=pl.CostEstimate(flops=8 * 10**9, bytes_accessed=4 * 2**20, transcendentals=0),
        name="lower_slots",
    )(pos, count, core, object_field, right, below, corner, photon_rows, probe_modes, waves, g_own, g_right, probe_1)

    plane, depth = lax.axis_size(PLANE), lax.axis_size(DEPTH)
    swap = [(0, 1), (1, 0)]
    above = lax.ppermute(g_below, ROW, down)
    value = kept + lax.ppermute(sent, "core", swap)
    shares = lax.all_to_all(value.reshape(plane, -1, PATCH), PLANE, 0, 0, tiled=True)
    share = jnp.sum(shares, axis=0)
    share = jnp.sum(everyone(share, DEPTH, depth), axis=0)
    share, above, g_right, g_corner = lax.optimization_barrier((share, above, g_right, g_corner))
    left = lax.ppermute(g_right, COL, along)
    from_corner = lax.ppermute(g_corner, BOTH, diagonal)
    parts = everyone(share, PLANE + ("core",), 2 * plane)
    parts = parts.reshape(plane, 2, *share.shape)

    object_gradient, probe_gradient = pl.pallas_call(
        seam_kernel,
        out_shape=(own_shape, shape(2, plane, *share.shape)),
        in_specs=[hbm] * 5,
        out_specs=(hbm, hbm),
        scratch_shapes=[
            pltpu.VMEM((2, PATCH, cols), F32),
            pltpu.VMEM((2, rows - PATCH, PATCH), F32),
            pltpu.VMEM((2, PATCH, cols), F32),
            pltpu.VMEM((2, rows, PATCH), F32),
            pltpu.VMEM((2, PATCH, PATCH), F32),
            pltpu.VMEM((2, plane) + share.shape, F32),
            pltpu.SemaphoreType.DMA((7,)),
        ],
        input_output_aliases={0: 0},
        compiler_params=pltpu.CompilerParams(vmem_limit_bytes=8 * 2**20),
        name="seams",
    )(g_own, above, left, from_corner, parts)
    return (object_gradient, probe_gradient.reshape(probe_modes.shape))


def solution(mesh):
    fine = Mesh(mesh.devices.reshape(4, 4, 4, 2, 2), BOTH)
    in_specs = (
        P(None, ROW, COL),
        P(),
        P(ROW, COL, None, None, None),
        P(ROW, COL, None, None),
        P(ROW, COL),
    )
    out_specs = (P(None, ROW, COL), P())
    return jax.shard_map(body, mesh=fine, in_specs=in_specs, out_specs=out_specs, check_vma=False)
```

```python
import functools
import math

import jax
import jax.numpy as jnp
import numpy as np
from jax import lax
from jax.experimental import pallas as pl
from jax.experimental.pallas import tpu as pltpu
from jax.sharding import Mesh
from jax.sharding import PartitionSpec as P

F32 = jnp.float32
BF16 = jnp.bfloat16
PATCH = 128
BLOCK = 8
VMEM_LIMIT = 63 * 2**20
ROW = "z_hi"
COL = ("x", "y", "z_lo", "core")
BOTH = (ROW,) + COL
PLANE = ("x", "y", "core")
DEPTH = ("z_hi", "z_lo")


def waves_of(patch_len):
    index_range = np.arange(patch_len)
    product = (index_range[:, None] * index_range[None, :]) % patch_len
    angle = product.astype(np.float32) * np.float32(2.0 * math.pi / patch_len)
    pair = np.stack([np.cos(angle), np.sin(angle)]) / np.float32(math.sqrt(patch_len))
    return jnp.asarray(pair, F32)


def dot(a, b):
    return jnp.dot(a, b, preferred_element_type=F32)


def slot_block(at, slots, valids, pos, row_base, field, grad, photons, probe, probe_sum, plus_ref, minus_ref):
    n = len(slots)
    lane = lax.broadcasted_iota(jnp.int32, (PATCH, PATCH), 1)
    plus = plus_ref[...]
    minus = minus_ref[...]
    places, patches, waves = [], [], []
    for s in slots:
        top = pos[0, s] - row_base
        left = pos[1, s]
        tile = left // PATCH
        shift = left % PATCH
        back = (PATCH - shift) % PATCH
        keep = lane >= shift
        patch = []
        for k in range(2):
            a = field[tile, k, pl.ds(top, PATCH), :]
            b = field[tile + 1, k, pl.ds(top, PATCH), :]
            patch.append(pltpu.roll(jnp.where(keep, a, b), back, 1))
        places.append((top, tile, shift, keep))
        patches.append(patch)
        for m in range(2):
            pr = probe[0, m]
            pi = probe[1, m]
            wr = (pr * patch[0] - pi * patch[1]).astype(BF16)
            wi = (pr * patch[1] + pi * patch[0]).astype(BF16)
            waves.append(jnp.concatenate([wr, wi], axis=0))
    first = dot(plus, jnp.concatenate(waves, axis=1)).astype(BF16)
    cols = [slice(q * PATCH, (q + 1) * PATCH) for q in range(2 * n)]
    turned = [jnp.concatenate([first[:PATCH, q], first[PATCH:, q]], axis=1) for q in cols]
    far = dot(jnp.concatenate(turned, axis=0), minus)
    scaled = []
    for i in range(n):
        f0 = far[2 * i * PATCH:(2 * i + 1) * PATCH]
        f1 = far[(2 * i + 1) * PATCH:(2 * i + 2) * PATCH]
        power = f0 * f0 + f1 * f1
        intensity = power[:, :PATCH] + power[:, PATCH:]
        factor = (1.0 - photons[at[i]].astype(F32) / (intensity + 1.0)) * valids[i]
        for f in (f0, f1):
            re = (f[:, :PATCH] * factor).astype(BF16)
            im = (f[:, PATCH:] * factor).astype(BF16)
            scaled.append(jnp.concatenate([re, im], axis=1))
    back_pass = dot(jnp.concatenate(scaled, axis=0), plus).astype(BF16)
    unturned = [jnp.concatenate([back_pass[q, :PATCH], back_pass[q, PATCH:]], axis=0) for q in cols]
    exit_grad = dot(minus, jnp.concatenate(unturned, axis=1))
    for m in range(2):
        sum_re = sum_im = None
        for i in range(n):
            er = exit_grad[:PATCH, cols[2 * i + m]]
            ei = exit_grad[PATCH:, cols[2 * i + m]]
            o_re, o_im = patches[i]
            t_re = o_re * er + o_im * ei
            t_im = o_re * ei - o_im * er
            sum_re = t_re if sum_re is None else sum_re + t_re
            sum_im = t_im if sum_im is None else sum_im + t_im
        probe_sum[0, m] += sum_re
        probe_sum[1, m] += sum_im
    for i in range(n):
        g_re = g_im = None
        for m in range(2):
            er = exit_grad[:PATCH, cols[2 * i + m]]
            ei = exit_grad[PATCH:, cols[2 * i + m]]
            pr = probe[0, m]
            pi = probe[1, m]
            t_re = pr * er + pi * ei
            t_im = pr * ei - pi * er
            g_re = t_re if g_re is None else g_re + t_re
            g_im = t_im if g_im is None else g_im + t_im
        top, tile, shift, keep = places[i]
        for k, g in ((0, g_re), (1, g_im)):
            g = pltpu.roll(g, shift, 1)
            grad[tile, k, pl.ds(top, PATCH), :] += jnp.where(keep, g, 0.0)
            grad[tile + 1, k, pl.ds(top, PATCH), :] += jnp.where(keep, 0.0, g)


def fill_tables(waves, plus_ref, minus_ref):
    c = waves[0].astype(BF16)
    s = waves[1].astype(BF16)
    plus_ref[:PATCH, :PATCH] = c
    plus_ref[:PATCH, PATCH:] = s
    plus_ref[PATCH:, :PATCH] = -s
    plus_ref[PATCH:, PATCH:] = c
    minus_ref[:PATCH, :PATCH] = c
    minus_ref[:PATCH, PATCH:] = -s
    minus_ref[PATCH:, :PATCH] = s
    minus_ref[PATCH:, PATCH:] = c


def list_slots(wanted, pos, count, listed, photons, photon_buf, photon_sems):
    def list_step(s, found):
        chosen = wanted(pos[0, s])

        @pl.when(chosen)
        def _():
            listed[found] = s
            pltpu.make_async_copy(photons.at[s], photon_buf.at[found], photon_sems.at[found]).start()

        return found + chosen.astype(jnp.int32)

    return lax.fori_loop(0, count, list_step, jnp.int32(0))


def run_slots(found, pos, row_base, listed, field, grad, photons, photon_buf, photon_sems, probe, probe_sum,
              plus_ref, minus_ref):
    def step(k, carry, first=0, width=BLOCK):
        places = [first + k * width + i for i in range(width)]
        at = [jnp.minimum(p, found - 1) for p in places]
        slots = [listed[a] for a in at]
        valids = [jnp.where(p < found, 1.0, 0.0).astype(F32) for p in places]
        for p, a, s in zip(places, at, slots):
            @pl.when(p < found)
            def _(a=a, s=s):
                pltpu.make_async_copy(photons.at[s], photon_buf.at[a], photon_sems.at[a]).wait()

        slot_block(at, slots, valids, pos, row_base, field, grad, photon_buf, probe, probe_sum, plus_ref, minus_ref)
        return carry

    rest = found % BLOCK
    small = (rest > 0) & (rest <= BLOCK // 2)
    blocks = found // BLOCK + ((rest > 0) & jnp.logical_not(small)).astype(jnp.int32)
    lax.fori_loop(0, blocks, step, 0)

    @pl.when(small)
    def _():
        step(0, 0, blocks * BLOCK, BLOCK // 2)


def copies_of(pairs, sems):
    return [pltpu.make_async_copy(a, b, sems.at[i]) for i, (a, b) in enumerate(pairs)]


def start_all(copies):
    for c in copies:
        c.start()


def wait_all(copies):
    for c in copies:
        c.wait()


def by_tiles(array, tiles):
    return [array.at[:, :, pl.ds(t * PATCH, PATCH)] for t in range(tiles)]


def rim_kernel(own, below, right, corner, below_buf, right_buf, sems):
    rim = pl.ds(0, PATCH)
    loads = copies_of([(own.at[:, rim, :], below_buf), (own.at[:, :, rim], right_buf)], sems)
    stores = copies_of(
        [(below_buf, below), (right_buf, right), (below_buf.at[:, :, rim], corner)], sems
    )
    start_all(loads)
    wait_all(loads)
    start_all(stores)
    wait_all(stores)


def upper_kernel(pos, count, own, right, photons, probe_in, waves_in, g_own, g_right, probe_out,
                 field, grad, photon_buf, probe, waves, plus_ref, minus_ref, probe_sum, listed, sems, photon_sems):
    rows, cols = own.shape[1], own.shape[2]
    tiles = cols // PATCH
    loads = copies_of(
        [(waves_in, waves), (probe_in, probe)]
        + [(a, field.at[t]) for t, a in enumerate(by_tiles(own, tiles))]
        + [(right, field.at[tiles])],
        sems,
    )
    start_all(loads)
    found = list_slots(lambda top: top <= rows - PATCH, pos, count[0], listed, photons, photon_buf, photon_sems)
    grad[...] = jnp.zeros(grad.shape, F32)
    probe_sum[...] = jnp.zeros(probe_sum.shape, F32)
    loads[0].wait()
    fill_tables(waves, plus_ref, minus_ref)
    wait_all(loads[1:])
    run_slots(found, pos, 0, listed, field, grad, photons, photon_buf, photon_sems, probe, probe_sum,
              plus_ref, minus_ref)
    stores = copies_of(
        [(probe_sum, probe_out)]
        + [(grad.at[t], a) for t, a in enumerate(by_tiles(g_own, tiles))]
        + [(grad.at[tiles], g_right)],
        sems,
    )
    start_all(stores)
    wait_all(stores)


def lower_kernel(scale, pos, count, own, right, below, corner, photons, probe_in, waves_in, own_in, right_in, sum_in,
                 g_own, g_right, g_below, g_corner, probe_out,
                 field, grad, photon_buf, probe, waves, plus_ref, minus_ref, probe_sum, listed, sems, photon_sems):
    rows, cols = own.shape[1], own.shape[2]
    tiles = cols // PATCH
    base = rows - PATCH
    last, upper, lower = pl.ds(base, PATCH), pl.ds(0, PATCH), pl.ds(PATCH, PATCH)

    def last_rows(array):
        return [array.at[:, last, pl.ds(t * PATCH, PATCH)] for t in range(tiles)]

    loads = copies_of(
        [(waves_in, waves), (probe_in, probe), (sum_in, probe_sum)]
        + [(a, field.at[t, :, upper, :]) for t, a in enumerate(last_rows(own) + [right.at[:, last, :]])]
        + [(a, field.at[t, :, lower, :]) for t, a in enumerate(by_tiles(below, tiles) + [corner])]
        + [(a, grad.at[t, :, upper, :]) for t, a in enumerate(last_rows(own_in) + [right_in.at[:, last, :]])],
        sems,
    )
    start_all(loads)
    found = list_slots(lambda top: top > base, pos, count[0], listed, photons, photon_buf, photon_sems)
    for t in range(tiles + 1):
        grad[t, :, lower, :] = jnp.zeros((2, PATCH, PATCH), F32)
    loads[0].wait()
    fill_tables(waves, plus_ref, minus_ref)
    wait_all(loads[1:])
    run_slots(found, pos, base, listed, field, grad, photons, photon_buf, photon_sems, probe, probe_sum,
              plus_ref, minus_ref)
    probe_sum[...] = probe_sum[...] * scale
    stores = copies_of(
        [(probe_sum, probe_out)]
        + [(grad.at[t, :, lower, :], a) for t, a in enumerate(by_tiles(g_below, tiles) + [g_corner])]
        + [(grad.at[t, :, upper, :], a) for t, a in enumerate(last_rows(g_own) + [g_right.at[:, last, :]])],
        sems,
    )
    start_all(stores)
    wait_all(stores)


def seam_kernel(grad_in, above, left, corner, parts, grad, probe,
                top_buf, left_buf, above_buf, beside_buf, corner_buf, probe_buf, sems):
    rows, cols = grad.shape[1], grad.shape[2]
    rest = rows - PATCH
    top_rim = grad.at[:, pl.ds(0, PATCH), :]
    left_rim = grad.at[:, pl.ds(PATCH, rest), pl.ds(0, PATCH)]
    loads = copies_of(
        [(top_rim, top_buf), (left_rim, left_buf), (above, above_buf), (left, beside_buf), (corner, corner_buf),
         (parts, probe_buf)],
        sems,
    )
    start_all(loads)
    wait_all(loads)
    join = pltpu.make_async_copy(probe_buf, probe, sems.at[2])
    join.start()
    top_buf[:, :, PATCH:] += above_buf[:, :, PATCH:]
    top_buf[:, :, :PATCH] += above_buf[:, :, :PATCH] + (beside_buf[:, :PATCH, :] + corner_buf[...])
    left_buf[...] += beside_buf[:, PATCH:, :]
    stores = copies_of([(top_buf, top_rim), (left_buf, left_rim)], sems)
    start_all(stores)
    wait_all(stores)
    join.wait()


def shape(*dims):
    return jax.ShapeDtypeStruct(dims, F32)


def everyone(value, axes, count):
    sent = jnp.broadcast_to(value[None], (count,) + value.shape)
    return lax.all_to_all(sent, axes, 0, 0, tiled=True)


def body(object_field, probe_modes, photons, positions, counts):
    rows, cols = object_field.shape[1], object_field.shape[2]
    slot_count = photons.shape[2]
    tiles = cols // PATCH
    n_row, n_col = lax.axis_size(ROW), lax.axis_size(COL)
    pos = positions[0, 0].T
    count = counts[0]
    photon_rows = photons[0, 0]
    waves = waves_of(PATCH)
    scale = 1.0 / math.sqrt(n_row * n_col * slot_count)
    down = [(i, i + 1) for i in range(n_row - 1)]
    along = [(i, i + 1) for i in range(n_col - 1)]
    up, back = ([(j, i) for i, j in pairs] for pairs in (down, along))
    diagonal = [
        (a * n_col + b, (a + 1) * n_col + b + 1) for a in range(n_row - 1) for b in range(n_col - 1)
    ]
    diagonal_back = [(j, i) for i, j in diagonal]
    smem = pl.BlockSpec(memory_space=pltpu.SMEM)
    hbm = pl.BlockSpec(memory_space=pl.ANY)
    params = pltpu.CompilerParams(vmem_limit_bytes=VMEM_LIMIT)

    rim_shape = shape(2, PATCH, PATCH)
    below, right, corner = pl.pallas_call(
        rim_kernel,
        out_shape=(shape(2, PATCH, cols), shape(2, rows, PATCH), rim_shape),
        in_specs=[hbm],
        out_specs=(hbm,) * 3,
        scratch_shapes=[
            pltpu.VMEM((2, PATCH, cols), F32),
            pltpu.VMEM((2, rows, PATCH), F32),
            pltpu.SemaphoreType.DMA((3,)),
        ],
        compiler_params=params,
        name="rims",
    )(object_field)
    below = lax.ppermute(below, ROW, up)
    right = lax.ppermute(right, COL, back)
    corner = lax.ppermute(corner, BOTH, diagonal_back)

    def scratch(height):
        return [
            pltpu.VMEM((tiles + 1, 2, height, PATCH), F32),
            pltpu.VMEM((tiles + 1, 2, height, PATCH), F32),
            pltpu.VMEM(photon_rows.shape, BF16),
            pltpu.VMEM(probe_modes.shape, F32),
            pltpu.VMEM(waves.shape, F32),
            pltpu.VMEM((2 * PATCH, 2 * PATCH), BF16),
            pltpu.VMEM((2 * PATCH, 2 * PATCH), BF16),
            pltpu.VMEM(probe_modes.shape, F32),
            pltpu.SMEM((slot_count,), jnp.int32),
            pltpu.SemaphoreType.DMA((3 * tiles + 6,)),
            pltpu.SemaphoreType.DMA((slot_count,)),
        ]

    own_shape, right_shape, probe_shape = shape(2, rows, cols), shape(2, rows, PATCH), shape(*probe_modes.shape)
    g_own, g_right, probe_1 = pl.pallas_call(
        upper_kernel,
        out_shape=(own_shape, right_shape, probe_shape),
        in_specs=[smem, smem] + [hbm] * 5,
        out_specs=(hbm,) * 3,
        scratch_shapes=scratch(rows),
        compiler_params=params,
        cost_estimate=pl.CostEstimate(flops=10**9, bytes_accessed=2**20, transcendentals=0),
        name="upper_slots",
    )(pos, count, object_field, right, photon_rows, probe_modes, waves)
    g_own, g_right, g_below, g_corner, probe_2 = pl.pallas_call(
        functools.partial(lower_kernel, scale),
        out_shape=(own_shape, right_shape, shape(2, PATCH, cols), rim_shape, probe_shape),
        in_specs=[smem] * 2 + [hbm] * 10,
        out_specs=(hbm,) * 5,
        scratch_shapes=scratch(2 * PATCH),
        input_output_aliases={9: 0, 10: 1},
        compiler_params=params,
        cost_estimate=pl.CostEstimate(flops=10**9, bytes_accessed=2**20, transcendentals=0),
        name="lower_slots",
    )(pos, count, object_field, right, below, corner, photon_rows, probe_modes, waves, g_own, g_right, probe_1)

    plane, depth = lax.axis_size(PLANE), lax.axis_size(DEPTH)
    above = lax.ppermute(g_below, ROW, down)
    left = lax.ppermute(g_right, COL, along)
    from_corner = lax.ppermute(g_corner, BOTH, diagonal)
    shares = lax.all_to_all(probe_2.reshape(plane, -1, PATCH), PLANE, 0, 0, tiled=True)
    share = jnp.sum(shares, axis=0)
    share = jnp.sum(everyone(share, DEPTH, depth), axis=0)
    share, above, left, from_corner = lax.optimization_barrier((share, above, left, from_corner))
    parts = everyone(share, PLANE, plane)

    object_gradient, probe_gradient = pl.pallas_call(
        seam_kernel,
        out_shape=(own_shape, shape(*parts.shape)),
        in_specs=[hbm] * 5,
        out_specs=(hbm, hbm),
        scratch_shapes=[
            pltpu.VMEM((2, PATCH, cols), F32),
            pltpu.VMEM((2, rows - PATCH, PATCH), F32),
            pltpu.VMEM((2, PATCH, cols), F32),
            pltpu.VMEM((2, rows, PATCH), F32),
            pltpu.VMEM((2, PATCH, PATCH), F32),
            pltpu.VMEM(parts.shape, F32),
            pltpu.SemaphoreType.DMA((6,)),
        ],
        input_output_aliases={0: 0},
        compiler_params=pltpu.CompilerParams(vmem_limit_bytes=8 * 2**20),
        name="seams",
    )(g_own, above, left, from_corner, parts)
    return (object_gradient, probe_gradient.reshape(probe_modes.shape))


def solution(mesh):
    fine = Mesh(mesh.devices.reshape(4, 4, 4, 2, 2), BOTH)
    in_specs = (
        P(None, ROW, COL),
        P(),
        P(ROW, COL, None, None, None),
        P(ROW, COL, None, None),
        P(ROW, COL),
    )
    out_specs = (P(None, ROW, COL), P())
    return jax.shard_map(body, mesh=fine, in_specs=in_specs, out_specs=out_specs, check_vma=False)
```

```python
import functools
import math

import jax
import jax.numpy as jnp
import numpy as np
from jax import lax
from jax.experimental import pallas as pl
from jax.experimental.pallas import tpu as pltpu
from jax.sharding import Mesh
from jax.sharding import PartitionSpec as P

F32 = jnp.float32
BF16 = jnp.bfloat16
PATCH = 128
BLOCK = 8
VMEM_LIMIT = 63 * 2**20
ROW = "z_hi"
COL = ("x", "y", "z_lo", "core")
BOTH = (ROW,) + COL
PLANE = ("x", "y", "core")
DEPTH = ("z_hi", "z_lo")


def waves_of(patch_len):
    index_range = np.arange(patch_len)
    product = (index_range[:, None] * index_range[None, :]) % patch_len
    angle = product.astype(np.float32) * np.float32(2.0 * math.pi / patch_len)
    pair = np.stack([np.cos(angle), np.sin(angle)]) / np.float32(math.sqrt(patch_len))
    return jnp.asarray(pair, F32)


def dot(a, b):
    return jnp.dot(a, b, preferred_element_type=F32)


def slot_block(at, slots, valids, pos, row_base, field, grad, photons, probe, probe_sum, plus_ref, minus_ref):
    n = len(slots)
    lane = lax.broadcasted_iota(jnp.int32, (PATCH, PATCH), 1)
    plus = plus_ref[...]
    minus = minus_ref[...]
    places, patches, waves = [], [], []
    for s in slots:
        top = pos[0, s] - row_base
        left = pos[1, s]
        tile = left // PATCH
        shift = left % PATCH
        back = (PATCH - shift) % PATCH
        keep = lane >= shift
        patch = []
        for k in range(2):
            a = field[tile, k, pl.ds(top, PATCH), :]
            b = field[tile + 1, k, pl.ds(top, PATCH), :]
            patch.append(pltpu.roll(jnp.where(keep, a, b), back, 1))
        places.append((top, tile, shift, keep))
        patches.append(patch)
        for m in range(2):
            pr = probe[0, m]
            pi = probe[1, m]
            wr = (pr * patch[0] - pi * patch[1]).astype(BF16)
            wi = (pr * patch[1] + pi * patch[0]).astype(BF16)
            waves.append(jnp.concatenate([wr, wi], axis=0))
    first = dot(plus, jnp.concatenate(waves, axis=1)).astype(BF16)
    cols = [slice(q * PATCH, (q + 1) * PATCH) for q in range(2 * n)]
    turned = [jnp.concatenate([first[:PATCH, q], first[PATCH:, q]], axis=1) for q in cols]
    far = dot(jnp.concatenate(turned, axis=0), minus)
    scaled = []
    for i in range(n):
        f0 = far[2 * i * PATCH:(2 * i + 1) * PATCH]
        f1 = far[(2 * i + 1) * PATCH:(2 * i + 2) * PATCH]
        power = f0 * f0 + f1 * f1
        intensity = power[:, :PATCH] + power[:, PATCH:]
        factor = (1.0 - photons[at[i]].astype(F32) / (intensity + 1.0)) * valids[i]
        for f in (f0, f1):
            re = (f[:, :PATCH] * factor).astype(BF16)
            im = (f[:, PATCH:] * factor).astype(BF16)
            scaled.append(jnp.concatenate([re, im], axis=1))
    back_pass = dot(jnp.concatenate(scaled, axis=0), plus).astype(BF16)
    unturned = [jnp.concatenate([back_pass[q, :PATCH], back_pass[q, PATCH:]], axis=0) for q in cols]
    exit_grad = dot(minus, jnp.concatenate(unturned, axis=1))
    for m in range(2):
        sum_re = sum_im = None
        for i in range(n):
            er = exit_grad[:PATCH, cols[2 * i + m]]
            ei = exit_grad[PATCH:, cols[2 * i + m]]
            o_re, o_im = patches[i]
            t_re = o_re * er + o_im * ei
            t_im = o_re * ei - o_im * er
            sum_re = t_re if sum_re is None else sum_re + t_re
            sum_im = t_im if sum_im is None else sum_im + t_im
        probe_sum[0, m] += sum_re
        probe_sum[1, m] += sum_im
    for i in range(n):
        g_re = g_im = None
        for m in range(2):
            er = exit_grad[:PATCH, cols[2 * i + m]]
            ei = exit_grad[PATCH:, cols[2 * i + m]]
            pr = probe[0, m]
            pi = probe[1, m]
            t_re = pr * er + pi * ei
            t_im = pr * ei - pi * er
            g_re = t_re if g_re is None else g_re + t_re
            g_im = t_im if g_im is None else g_im + t_im
        top, tile, shift, keep = places[i]
        for k, g in ((0, g_re), (1, g_im)):
            g = pltpu.roll(g, shift, 1)
            grad[tile, k, pl.ds(top, PATCH), :] += jnp.where(keep, g, 0.0)
            grad[tile + 1, k, pl.ds(top, PATCH), :] += jnp.where(keep, 0.0, g)


def fill_tables(waves, plus_ref, minus_ref):
    c = waves[0].astype(BF16)
    s = waves[1].astype(BF16)
    plus_ref[:PATCH, :PATCH] = c
    plus_ref[:PATCH, PATCH:] = s
    plus_ref[PATCH:, :PATCH] = -s
    plus_ref[PATCH:, PATCH:] = c
    minus_ref[:PATCH, :PATCH] = c
    minus_ref[:PATCH, PATCH:] = -s
    minus_ref[PATCH:, :PATCH] = s
    minus_ref[PATCH:, PATCH:] = c


def list_slots(wanted, pos, count, listed, photons, photon_buf, photon_sems):
    def list_step(s, found):
        chosen = wanted(pos[0, s])

        @pl.when(chosen)
        def _():
            listed[found] = s
            pltpu.make_async_copy(photons.at[s], photon_buf.at[found], photon_sems.at[found]).start()

        return found + chosen.astype(jnp.int32)

    return lax.fori_loop(0, count, list_step, jnp.int32(0))


def run_slots(found, pos, row_base, listed, field, grad, photons, photon_buf, photon_sems, probe, probe_sum,
              plus_ref, minus_ref):
    def step(k, carry, first=0, width=BLOCK):
        places = [first + k * width + i for i in range(width)]
        at = [jnp.minimum(p, found - 1) for p in places]
        slots = [listed[a] for a in at]
        valids = [jnp.where(p < found, 1.0, 0.0).astype(F32) for p in places]
        for p, a, s in zip(places, at, slots):
            @pl.when(p < found)
            def _(a=a, s=s):
                pltpu.make_async_copy(photons.at[s], photon_buf.at[a], photon_sems.at[a]).wait()

        slot_block(at, slots, valids, pos, row_base, field, grad, photon_buf, probe, probe_sum, plus_ref, minus_ref)
        return carry

    rest = found % BLOCK
    small = (rest > 0) & (rest <= BLOCK // 2)
    blocks = found // BLOCK + ((rest > 0) & jnp.logical_not(small)).astype(jnp.int32)
    lax.fori_loop(0, blocks, step, 0)

    @pl.when(small)
    def _():
        step(0, 0, blocks * BLOCK, BLOCK // 2)


def copies_of(pairs, sems):
    return [pltpu.make_async_copy(a, b, sems.at[i]) for i, (a, b) in enumerate(pairs)]


def start_all(copies):
    for c in copies:
        c.start()


def wait_all(copies):
    for c in copies:
        c.wait()


def by_tiles(array, tiles):
    return [array.at[:, :, pl.ds(t * PATCH, PATCH)] for t in range(tiles)]


def rim_kernel(own, below, right, corner, below_buf, right_buf, sems):
    rim = pl.ds(0, PATCH)
    loads = copies_of([(own.at[:, rim, :], below_buf), (own.at[:, :, rim], right_buf)], sems)
    stores = copies_of(
        [(below_buf, below), (right_buf, right), (below_buf.at[:, :, rim], corner)], sems
    )
    start_all(loads)
    wait_all(loads)
    start_all(stores)
    wait_all(stores)


def upper_kernel(pos, count, own, right, photons, probe_in, waves_in, g_own, g_right, probe_out,
                 field, grad, photon_buf, probe, waves, plus_ref, minus_ref, probe_sum, listed, sems, photon_sems):
    rows, cols = own.shape[1], own.shape[2]
    tiles = cols // PATCH
    loads = copies_of(
        [(waves_in, waves), (probe_in, probe)]
        + [(a, field.at[t]) for t, a in enumerate(by_tiles(own, tiles))]
        + [(right, field.at[tiles])],
        sems,
    )
    start_all(loads)
    found = list_slots(lambda top: top <= rows - PATCH, pos, count[0], listed, photons, photon_buf, photon_sems)
    grad[...] = jnp.zeros(grad.shape, F32)
    probe_sum[...] = jnp.zeros(probe_sum.shape, F32)
    loads[0].wait()
    fill_tables(waves, plus_ref, minus_ref)
    wait_all(loads[1:])
    run_slots(found, pos, 0, listed, field, grad, photons, photon_buf, photon_sems, probe, probe_sum,
              plus_ref, minus_ref)
    stores = copies_of(
        [(probe_sum, probe_out)]
        + [(grad.at[t], a) for t, a in enumerate(by_tiles(g_own, tiles))]
        + [(grad.at[tiles], g_right)],
        sems,
    )
    start_all(stores)
    wait_all(stores)


def lower_kernel(scale, pos, count, own, right, below, corner, photons, probe_in, waves_in, own_in, right_in, sum_in,
                 g_own, g_right, g_below, probe_out,
                 field, grad, photon_buf, probe, waves, plus_ref, minus_ref, probe_sum, listed, sems, photon_sems):
    rows, cols = own.shape[1], own.shape[2]
    tiles = cols // PATCH
    base = rows - PATCH
    last, upper, lower = pl.ds(base, PATCH), pl.ds(0, PATCH), pl.ds(PATCH, PATCH)

    def last_rows(array):
        return [array.at[:, last, pl.ds(t * PATCH, PATCH)] for t in range(tiles)]

    loads = copies_of(
        [(waves_in, waves), (probe_in, probe), (sum_in, probe_sum)]
        + [(a, field.at[t, :, upper, :]) for t, a in enumerate(last_rows(own) + [right.at[:, last, :]])]
        + [(a, field.at[t, :, lower, :]) for t, a in enumerate(by_tiles(below, tiles) + [corner])]
        + [(a, grad.at[t, :, upper, :]) for t, a in enumerate(last_rows(own_in) + [right_in.at[:, last, :]])],
        sems,
    )
    start_all(loads)
    found = list_slots(lambda top: top > base, pos, count[0], listed, photons, photon_buf, photon_sems)
    for t in range(tiles + 1):
        grad[t, :, lower, :] = jnp.zeros((2, PATCH, PATCH), F32)
    loads[0].wait()
    fill_tables(waves, plus_ref, minus_ref)
    wait_all(loads[1:])
    run_slots(found, pos, base, listed, field, grad, photons, photon_buf, photon_sems, probe, probe_sum,
              plus_ref, minus_ref)
    probe_sum[...] = probe_sum[...] * scale
    stores = copies_of(
        [(probe_sum, probe_out)]
        + [(grad.at[t, :, lower, :], a) for t, a in enumerate(by_tiles(g_below, tiles + 1))]
        + [(grad.at[t, :, upper, :], a) for t, a in enumerate(last_rows(g_own) + [g_right.at[:, last, :]])],
        sems,
    )
    start_all(stores)
    wait_all(stores)


def corner_kernel(right_in, above, right, rim_buf, corner_buf, sems):
    rows = right.at[:, pl.ds(0, PATCH), :]
    corner = above.at[:, :, pl.ds(above.shape[2] - PATCH, PATCH)]
    loads = copies_of([(rows, rim_buf), (corner, corner_buf)], sems)
    start_all(loads)
    wait_all(loads)
    rim_buf[...] += corner_buf[...]
    store = pltpu.make_async_copy(rim_buf, rows, sems.at[0])
    store.start()
    store.wait()


def seam_kernel(grad_in, above, left, parts, grad, probe,
                top_buf, left_buf, above_buf, beside_buf, probe_buf, sems):
    rows, cols = grad.shape[1], grad.shape[2]
    rest = rows - PATCH
    top_rim = grad.at[:, pl.ds(0, PATCH), :]
    left_rim = grad.at[:, pl.ds(PATCH, rest), pl.ds(0, PATCH)]
    loads = copies_of(
        [(top_rim, top_buf), (left_rim, left_buf), (above.at[:, :, pl.ds(0, cols)], above_buf), (left, beside_buf),
         (parts, probe_buf)],
        sems,
    )
    start_all(loads)
    wait_all(loads)
    join = pltpu.make_async_copy(probe_buf, probe, sems.at[2])
    join.start()
    top_buf[:, :, PATCH:] += above_buf[:, :, PATCH:]
    top_buf[:, :, :PATCH] += above_buf[:, :, :PATCH] + beside_buf[:, :PATCH, :]
    left_buf[...] += beside_buf[:, PATCH:, :]
    stores = copies_of([(top_buf, top_rim), (left_buf, left_rim)], sems)
    start_all(stores)
    wait_all(stores)
    join.wait()


def shape(*dims):
    return jax.ShapeDtypeStruct(dims, F32)


def everyone(value, axes, count):
    sent = jnp.broadcast_to(value[None], (count,) + value.shape)
    return lax.all_to_all(sent, axes, 0, 0, tiled=True)


def body(object_field, probe_modes, photons, positions, counts):
    rows, cols = object_field.shape[1], object_field.shape[2]
    slot_count = photons.shape[2]
    tiles = cols // PATCH
    n_row, n_col = lax.axis_size(ROW), lax.axis_size(COL)
    pos = positions[0, 0].T
    count = counts[0]
    photon_rows = photons[0, 0]
    waves = waves_of(PATCH)
    scale = 1.0 / math.sqrt(n_row * n_col * slot_count)
    down = [(i, i + 1) for i in range(n_row - 1)]
    along = [(i, i + 1) for i in range(n_col - 1)]
    up, back = ([(j, i) for i, j in pairs] for pairs in (down, along))
    diagonal = [
        (a * n_col + b, (a + 1) * n_col + b + 1) for a in range(n_row - 1) for b in range(n_col - 1)
    ]
    diagonal_back = [(j, i) for i, j in diagonal]
    smem = pl.BlockSpec(memory_space=pltpu.SMEM)
    hbm = pl.BlockSpec(memory_space=pl.ANY)
    params = pltpu.CompilerParams(vmem_limit_bytes=VMEM_LIMIT)
    small = pltpu.CompilerParams(vmem_limit_bytes=8 * 2**20)

    rim_shape = shape(2, PATCH, PATCH)
    below, right, corner = pl.pallas_call(
        rim_kernel,
        out_shape=(shape(2, PATCH, cols), shape(2, rows, PATCH), rim_shape),
        in_specs=[hbm],
        out_specs=(hbm,) * 3,
        scratch_shapes=[
            pltpu.VMEM((2, PATCH, cols), F32),
            pltpu.VMEM((2, rows, PATCH), F32),
            pltpu.SemaphoreType.DMA((3,)),
        ],
        compiler_params=params,
        name="rims",
    )(object_field)
    below = lax.ppermute(below, ROW, up)
    right = lax.ppermute(right, COL, back)
    corner = lax.ppermute(corner, BOTH, diagonal_back)

    def scratch(height):
        return [
            pltpu.VMEM((tiles + 1, 2, height, PATCH), F32),
            pltpu.VMEM((tiles + 1, 2, height, PATCH), F32),
            pltpu.VMEM(photon_rows.shape, BF16),
            pltpu.VMEM(probe_modes.shape, F32),
            pltpu.VMEM(waves.shape, F32),
            pltpu.VMEM((2 * PATCH, 2 * PATCH), BF16),
            pltpu.VMEM((2 * PATCH, 2 * PATCH), BF16),
            pltpu.VMEM(probe_modes.shape, F32),
            pltpu.SMEM((slot_count,), jnp.int32),
            pltpu.SemaphoreType.DMA((3 * tiles + 6,)),
            pltpu.SemaphoreType.DMA((slot_count,)),
        ]

    own_shape, right_shape, probe_shape = shape(2, rows, cols), shape(2, rows, PATCH), shape(*probe_modes.shape)
    g_own, g_right, probe_1 = pl.pallas_call(
        upper_kernel,
        out_shape=(own_shape, right_shape, probe_shape),
        in_specs=[smem, smem] + [hbm] * 5,
        out_specs=(hbm,) * 3,
        scratch_shapes=scratch(rows),
        compiler_params=params,
        cost_estimate=pl.CostEstimate(flops=10**9, bytes_accessed=2**20, transcendentals=0),
        name="upper_slots",
    )(pos, count, object_field, right, photon_rows, probe_modes, waves)
    g_own, g_right, g_below, probe_2 = pl.pallas_call(
        functools.partial(lower_kernel, scale),
        out_shape=(own_shape, right_shape, shape(2, PATCH, cols + PATCH), probe_shape),
        in_specs=[smem] * 2 + [hbm] * 10,
        out_specs=(hbm,) * 4,
        scratch_shapes=scratch(2 * PATCH),
        input_output_aliases={9: 0, 10: 1},
        compiler_params=params,
        cost_estimate=pl.CostEstimate(flops=10**9, bytes_accessed=2**20, transcendentals=0),
        name="lower_slots",
    )(pos, count, object_field, right, below, corner, photon_rows, probe_modes, waves, g_own, g_right, probe_1)

    plane, depth = lax.axis_size(PLANE), lax.axis_size(DEPTH)
    above = lax.ppermute(g_below, ROW, down)
    shares = lax.all_to_all(probe_2.reshape(plane, -1, PATCH), PLANE, 0, 0, tiled=True)
    share = jnp.sum(shares, axis=0)
    share = jnp.sum(everyone(share, DEPTH, depth), axis=0)
    share, above = lax.optimization_barrier((share, above))
    g_right = pl.pallas_call(
        corner_kernel,
        out_shape=right_shape,
        in_specs=[hbm, hbm],
        out_specs=hbm,
        scratch_shapes=[
            pltpu.VMEM((2, PATCH, PATCH), F32),
            pltpu.VMEM((2, PATCH, PATCH), F32),
            pltpu.SemaphoreType.DMA((2,)),
        ],
        input_output_aliases={0: 0},
        compiler_params=small,
        name="corner",
    )(g_right, above)
    left = lax.ppermute(g_right, COL, along)
    parts = everyone(share, PLANE, plane)

    object_gradient, probe_gradient = pl.pallas_call(
        seam_kernel,
        out_shape=(own_shape, shape(*parts.shape)),
        in_specs=[hbm] * 4,
        out_specs=(hbm, hbm),
        scratch_shapes=[
            pltpu.VMEM((2, PATCH, cols), F32),
            pltpu.VMEM((2, rows - PATCH, PATCH), F32),
            pltpu.VMEM((2, PATCH, cols), F32),
            pltpu.VMEM((2, rows, PATCH), F32),
            pltpu.VMEM(parts.shape, F32),
            pltpu.SemaphoreType.DMA((5,)),
        ],
        input_output_aliases={0: 0},
        compiler_params=small,
        name="seams",
    )(g_own, above, left, parts)
    return (object_gradient, probe_gradient.reshape(probe_modes.shape))


def solution(mesh):
    fine = Mesh(mesh.devices.reshape(4, 4, 4, 2, 2), BOTH)
    in_specs = (
        P(None, ROW, COL),
        P(),
        P(ROW, COL, None, None, None),
        P(ROW, COL, None, None),
        P(ROW, COL),
    )
    out_specs = (P(None, ROW, COL), P())
    return jax.shard_map(body, mesh=fine, in_specs=in_specs, out_specs=out_specs, check_vma=False)
```

```python
import functools
import math

import jax
import jax.numpy as jnp
import numpy as np
from jax import lax
from jax.experimental import pallas as pl
from jax.experimental.pallas import tpu as pltpu
from jax.sharding import Mesh
from jax.sharding import PartitionSpec as P

F32 = jnp.float32
BF16 = jnp.bfloat16
PATCH = 128
BLOCK = 8
VMEM_LIMIT = 63 * 2**20
ROW = "z_hi"
COL = ("x", "y", "z_lo", "core")
BOTH = (ROW,) + COL
PLANE = ("x", "y", "core")
DEPTH = ("z_hi", "z_lo")


def waves_of(patch_len):
    index_range = np.arange(patch_len)
    product = (index_range[:, None] * index_range[None, :]) % patch_len
    angle = product.astype(np.float32) * np.float32(2.0 * math.pi / patch_len)
    pair = np.stack([np.cos(angle), np.sin(angle)]) / np.float32(math.sqrt(patch_len))
    return jnp.asarray(pair, F32)


def dot(a, b):
    return jnp.dot(a, b, preferred_element_type=F32)


def slot_block(at, slots, valids, pos, row_base, field, grad, photons, probe, probe_sum, plus_ref, minus_ref):
    n = len(slots)
    lane = lax.broadcasted_iota(jnp.int32, (PATCH, PATCH), 1)
    plus = plus_ref[...]
    minus = minus_ref[...]
    places, patches, waves = [], [], []
    for s in slots:
        top = pos[0, s] - row_base
        left = pos[1, s]
        tile = left // PATCH
        shift = left % PATCH
        back = (PATCH - shift) % PATCH
        keep = lane >= shift
        patch = []
        for k in range(2):
            a = field[tile, k, pl.ds(top, PATCH), :]
            b = field[tile + 1, k, pl.ds(top, PATCH), :]
            patch.append(pltpu.roll(jnp.where(keep, a, b), back, 1))
        places.append((top, tile, shift, keep))
        patches.append(patch)
        for m in range(2):
            pr = probe[0, m]
            pi = probe[1, m]
            wr = (pr * patch[0] - pi * patch[1]).astype(BF16)
            wi = (pr * patch[1] + pi * patch[0]).astype(BF16)
            waves.append(jnp.concatenate([wr, wi], axis=0))
    first = dot(plus, jnp.concatenate(waves, axis=1)).astype(BF16)
    cols = [slice(q * PATCH, (q + 1) * PATCH) for q in range(2 * n)]
    turned = [jnp.concatenate([first[:PATCH, q], first[PATCH:, q]], axis=1) for q in cols]
    far = dot(jnp.concatenate(turned, axis=0), minus)
    scaled = []
    for i in range(n):
        f0 = far[2 * i * PATCH:(2 * i + 1) * PATCH]
        f1 = far[(2 * i + 1) * PATCH:(2 * i + 2) * PATCH]
        power = f0 * f0 + f1 * f1
        intensity = power[:, :PATCH] + power[:, PATCH:]
        factor = (1.0 - photons[at[i]].astype(F32) / (intensity + 1.0)) * valids[i]
        for f in (f0, f1):
            re = (f[:, :PATCH] * factor).astype(BF16)
            im = (f[:, PATCH:] * factor).astype(BF16)
            scaled.append(jnp.concatenate([re, im], axis=1))
    back_pass = dot(jnp.concatenate(scaled, axis=0), plus).astype(BF16)
    unturned = [jnp.concatenate([back_pass[q, :PATCH], back_pass[q, PATCH:]], axis=0) for q in cols]
    exit_grad = dot(minus, jnp.concatenate(unturned, axis=1))
    for m in range(2):
        sum_re = sum_im = None
        for i in range(n):
            er = exit_grad[:PATCH, cols[2 * i + m]]
            ei = exit_grad[PATCH:, cols[2 * i + m]]
            o_re, o_im = patches[i]
            t_re = o_re * er + o_im * ei
            t_im = o_re * ei - o_im * er
            sum_re = t_re if sum_re is None else sum_re + t_re
            sum_im = t_im if sum_im is None else sum_im + t_im
        probe_sum[0, m] += sum_re
        probe_sum[1, m] += sum_im
    for i in range(n):
        g_re = g_im = None
        for m in range(2):
            er = exit_grad[:PATCH, cols[2 * i + m]]
            ei = exit_grad[PATCH:, cols[2 * i + m]]
            pr = probe[0, m]
            pi = probe[1, m]
            t_re = pr * er + pi * ei
            t_im = pr * ei - pi * er
            g_re = t_re if g_re is None else g_re + t_re
            g_im = t_im if g_im is None else g_im + t_im
        top, tile, shift, keep = places[i]
        for k, g in ((0, g_re), (1, g_im)):
            g = pltpu.roll(g, shift, 1)
            grad[tile, k, pl.ds(top, PATCH), :] += jnp.where(keep, g, 0.0)
            grad[tile + 1, k, pl.ds(top, PATCH), :] += jnp.where(keep, 0.0, g)


def fill_tables(waves, plus_ref, minus_ref):
    c = waves[0].astype(BF16)
    s = waves[1].astype(BF16)
    plus_ref[:PATCH, :PATCH] = c
    plus_ref[:PATCH, PATCH:] = s
    plus_ref[PATCH:, :PATCH] = -s
    plus_ref[PATCH:, PATCH:] = c
    minus_ref[:PATCH, :PATCH] = c
    minus_ref[:PATCH, PATCH:] = -s
    minus_ref[PATCH:, :PATCH] = s
    minus_ref[PATCH:, PATCH:] = c


def list_slots(wanted, pos, count, listed, photons, photon_buf, photon_sems):
    def list_step(s, found):
        chosen = wanted(pos[0, s])

        @pl.when(chosen)
        def _():
            listed[found] = s
            pltpu.make_async_copy(photons.at[s], photon_buf.at[found], photon_sems.at[found]).start()

        return found + chosen.astype(jnp.int32)

    return lax.fori_loop(0, count, list_step, jnp.int32(0))


def run_slots(found, pos, row_base, listed, field, grad, photons, photon_buf, photon_sems, probe, probe_sum,
              plus_ref, minus_ref):
    def step(k, carry, first=0, width=BLOCK):
        places = [first + k * width + i for i in range(width)]
        at = [jnp.minimum(p, found - 1) for p in places]
        slots = [listed[a] for a in at]
        valids = [jnp.where(p < found, 1.0, 0.0).astype(F32) for p in places]
        for p, a, s in zip(places, at, slots):
            @pl.when(p < found)
            def _(a=a, s=s):
                pltpu.make_async_copy(photons.at[s], photon_buf.at[a], photon_sems.at[a]).wait()

        slot_block(at, slots, valids, pos, row_base, field, grad, photon_buf, probe, probe_sum, plus_ref, minus_ref)
        return carry

    rest = found % BLOCK
    small = (rest > 0) & (rest <= BLOCK // 2)
    blocks = found // BLOCK + ((rest > 0) & jnp.logical_not(small)).astype(jnp.int32)
    lax.fori_loop(0, blocks, step, 0)

    @pl.when(small)
    def _():
        step(0, 0, blocks * BLOCK, BLOCK // 2)


def copies_of(pairs, sems):
    return [pltpu.make_async_copy(a, b, sems.at[i]) for i, (a, b) in enumerate(pairs)]


def start_all(copies):
    for c in copies:
        c.start()


def wait_all(copies):
    for c in copies:
        c.wait()


def by_tiles(array, tiles):
    return [array.at[:, :, pl.ds(t * PATCH, PATCH)] for t in range(tiles)]


def right_rim_kernel(own, right, right_buf, sems):
    load = pltpu.make_async_copy(own.at[:, :, pl.ds(0, PATCH)], right_buf, sems.at[0])
    load.start()
    load.wait()
    store = pltpu.make_async_copy(right_buf, right, sems.at[0])
    store.start()
    store.wait()


def below_rim_kernel(own, after, below, corner, below_buf, sems):
    rim = pl.ds(0, PATCH)
    load = pltpu.make_async_copy(own.at[:, rim, :], below_buf, sems.at[0])
    load.start()
    load.wait()
    stores = copies_of([(below_buf, below), (below_buf.at[:, :, rim], corner)], sems)
    start_all(stores)
    wait_all(stores)


def upper_kernel(pos, count, own, right, photons, probe_in, waves_in, g_own, g_right, probe_out,
                 field, grad, photon_buf, probe, waves, plus_ref, minus_ref, probe_sum, listed, sems, photon_sems):
    rows, cols = own.shape[1], own.shape[2]
    tiles = cols // PATCH
    loads = copies_of(
        [(waves_in, waves), (probe_in, probe)]
        + [(a, field.at[t]) for t, a in enumerate(by_tiles(own, tiles))]
        + [(right, field.at[tiles])],
        sems,
    )
    start_all(loads)
    found = list_slots(lambda top: top <= rows - PATCH, pos, count[0], listed, photons, photon_buf, photon_sems)
    grad[...] = jnp.zeros(grad.shape, F32)
    probe_sum[...] = jnp.zeros(probe_sum.shape, F32)
    loads[0].wait()
    fill_tables(waves, plus_ref, minus_ref)
    wait_all(loads[1:])
    run_slots(found, pos, 0, listed, field, grad, photons, photon_buf, photon_sems, probe, probe_sum,
              plus_ref, minus_ref)
    stores = copies_of(
        [(probe_sum, probe_out)]
        + [(grad.at[t], a) for t, a in enumerate(by_tiles(g_own, tiles))]
        + [(grad.at[tiles], g_right)],
        sems,
    )
    start_all(stores)
    wait_all(stores)


def lower_kernel(scale, pos, count, own, right, below, corner, photons, probe_in, waves_in, own_in, right_in, sum_in,
                 g_own, g_right, g_below, probe_out,
                 field, grad, photon_buf, probe, waves, plus_ref, minus_ref, probe_sum, listed, sems, photon_sems):
    rows, cols = own.shape[1], own.shape[2]
    tiles = cols // PATCH
    base = rows - PATCH
    last, upper, lower = pl.ds(base, PATCH), pl.ds(0, PATCH), pl.ds(PATCH, PATCH)

    def last_rows(array):
        return [array.at[:, last, pl.ds(t * PATCH, PATCH)] for t in range(tiles)]

    loads = copies_of(
        [(waves_in, waves), (probe_in, probe), (sum_in, probe_sum)]
        + [(a, field.at[t, :, upper, :]) for t, a in enumerate(last_rows(own) + [right.at[:, last, :]])]
        + [(a, field.at[t, :, lower, :]) for t, a in enumerate(by_tiles(below, tiles) + [corner])]
        + [(a, grad.at[t, :, upper, :]) for t, a in enumerate(last_rows(own_in) + [right_in.at[:, last, :]])],
        sems,
    )
    start_all(loads)
    found = list_slots(lambda top: top > base, pos, count[0], listed, photons, photon_buf, photon_sems)
    for t in range(tiles + 1):
        grad[t, :, lower, :] = jnp.zeros((2, PATCH, PATCH), F32)
    loads[0].wait()
    fill_tables(waves, plus_ref, minus_ref)
    wait_all(loads[1:])
    run_slots(found, pos, base, listed, field, grad, photons, photon_buf, photon_sems, probe, probe_sum,
              plus_ref, minus_ref)
    probe_sum[...] = probe_sum[...] * scale
    stores = copies_of(
        [(probe_sum, probe_out)]
        + [(grad.at[t, :, lower, :], a) for t, a in enumerate(by_tiles(g_below, tiles + 1))]
        + [(grad.at[t, :, upper, :], a) for t, a in enumerate(last_rows(g_own) + [g_right.at[:, last, :]])],
        sems,
    )
    start_all(stores)
    wait_all(stores)


def corner_kernel(right_in, above, right, rim_buf, corner_buf, sems):
    rows = right.at[:, pl.ds(0, PATCH), :]
    corner = above.at[:, :, pl.ds(above.shape[2] - PATCH, PATCH)]
    loads = copies_of([(rows, rim_buf), (corner, corner_buf)], sems)
    start_all(loads)
    wait_all(loads)
    rim_buf[...] += corner_buf[...]
    store = pltpu.make_async_copy(rim_buf, rows, sems.at[0])
    store.start()
    store.wait()


def seam_kernel(grad_in, above, left, parts, grad, probe,
                top_buf, left_buf, above_buf, beside_buf, probe_buf, sems):
    rows, cols = grad.shape[1], grad.shape[2]
    rest = rows - PATCH
    top_rim = grad.at[:, pl.ds(0, PATCH), :]
    left_rim = grad.at[:, pl.ds(PATCH, rest), pl.ds(0, PATCH)]
    loads = copies_of(
        [(top_rim, top_buf), (left_rim, left_buf), (above.at[:, :, pl.ds(0, cols)], above_buf), (left, beside_buf),
         (parts, probe_buf)],
        sems,
    )
    start_all(loads)
    wait_all(loads)
    join = pltpu.make_async_copy(probe_buf, probe, sems.at[2])
    join.start()
    top_buf[:, :, PATCH:] += above_buf[:, :, PATCH:]
    top_buf[:, :, :PATCH] += above_buf[:, :, :PATCH] + beside_buf[:, :PATCH, :]
    left_buf[...] += beside_buf[:, PATCH:, :]
    stores = copies_of([(top_buf, top_rim), (left_buf, left_rim)], sems)
    start_all(stores)
    wait_all(stores)
    join.wait()


def shape(*dims):
    return jax.ShapeDtypeStruct(dims, F32)


def everyone(value, axes, count):
    sent = jnp.broadcast_to(value[None], (count,) + value.shape)
    return lax.all_to_all(sent, axes, 0, 0, tiled=True)


def body(object_field, probe_modes, photons, positions, counts):
    rows, cols = object_field.shape[1], object_field.shape[2]
    slot_count = photons.shape[2]
    tiles = cols // PATCH
    n_row, n_col = lax.axis_size(ROW), lax.axis_size(COL)
    pos = positions[0, 0].T
    count = counts[0]
    photon_rows = photons[0, 0]
    waves = waves_of(PATCH)
    scale = 1.0 / math.sqrt(n_row * n_col * slot_count)
    down = [(i, i + 1) for i in range(n_row - 1)]
    along = [(i, i + 1) for i in range(n_col - 1)]
    up, back = ([(j, i) for i, j in pairs] for pairs in (down, along))
    diagonal = [
        (a * n_col + b, (a + 1) * n_col + b + 1) for a in range(n_row - 1) for b in range(n_col - 1)
    ]
    diagonal_back = [(j, i) for i, j in diagonal]
    smem = pl.BlockSpec(memory_space=pltpu.SMEM)
    hbm = pl.BlockSpec(memory_space=pl.ANY)
    params = pltpu.CompilerParams(vmem_limit_bytes=VMEM_LIMIT)
    small = pltpu.CompilerParams(vmem_limit_bytes=8 * 2**20)

    right = pl.pallas_call(
        right_rim_kernel,
        out_shape=shape(2, rows, PATCH),
        in_specs=[hbm],
        out_specs=hbm,
        scratch_shapes=[pltpu.VMEM((2, rows, PATCH), F32), pltpu.SemaphoreType.DMA((1,))],
        compiler_params=params,
        name="right_rim",
    )(object_field)
    below, corner = pl.pallas_call(
        below_rim_kernel,
        out_shape=(shape(2, PATCH, cols), shape(2, PATCH, PATCH)),
        in_specs=[hbm, hbm],
        out_specs=(hbm,) * 2,
        scratch_shapes=[pltpu.VMEM((2, PATCH, cols), F32), pltpu.SemaphoreType.DMA((2,))],
        compiler_params=params,
        name="below_rim",
    )(object_field, right)
    below = lax.ppermute(below, ROW, up)
    right = lax.ppermute(right, COL, back)
    corner = lax.ppermute(corner, BOTH, diagonal_back)

    def scratch(height):
        return [
            pltpu.VMEM((tiles + 1, 2, height, PATCH), F32),
            pltpu.VMEM((tiles + 1, 2, height, PATCH), F32),
            pltpu.VMEM(photon_rows.shape, BF16),
            pltpu.VMEM(probe_modes.shape, F32),
            pltpu.VMEM(waves.shape, F32),
            pltpu.VMEM((2 * PATCH, 2 * PATCH), BF16),
            pltpu.VMEM((2 * PATCH, 2 * PATCH), BF16),
            pltpu.VMEM(probe_modes.shape, F32),
            pltpu.SMEM((slot_count,), jnp.int32),
            pltpu.SemaphoreType.DMA((3 * tiles + 6,)),
            pltpu.SemaphoreType.DMA((slot_count,)),
        ]

    own_shape, right_shape, probe_shape = shape(2, rows, cols), shape(2, rows, PATCH), shape(*probe_modes.shape)
    g_own, g_right, probe_1 = pl.pallas_call(
        upper_kernel,
        out_shape=(own_shape, right_shape, probe_shape),
        in_specs=[smem, smem] + [hbm] * 5,
        out_specs=(hbm,) * 3,
        scratch_shapes=scratch(rows),
        compiler_params=params,
        cost_estimate=pl.CostEstimate(flops=10**9, bytes_accessed=2**20, transcendentals=0),
        name="upper_slots",
    )(pos, count, object_field, right, photon_rows, probe_modes, waves)
    g_own, g_right, g_below, probe_2 = pl.pallas_call(
        functools.partial(lower_kernel, scale),
        out_shape=(own_shape, right_shape, shape(2, PATCH, cols + PATCH), probe_shape),
        in_specs=[smem] * 2 + [hbm] * 10,
        out_specs=(hbm,) * 4,
        scratch_shapes=scratch(2 * PATCH),
        input_output_aliases={9: 0, 10: 1},
        compiler_params=params,
        cost_estimate=pl.CostEstimate(flops=10**9, bytes_accessed=2**20, transcendentals=0),
        name="lower_slots",
    )(pos, count, object_field, right, below, corner, photon_rows, probe_modes, waves, g_own, g_right, probe_1)

    plane, depth = lax.axis_size(PLANE), lax.axis_size(DEPTH)
    above = lax.ppermute(g_below, ROW, down)
    shares = lax.all_to_all(probe_2.reshape(plane, -1, PATCH), PLANE, 0, 0, tiled=True)
    share = jnp.sum(shares, axis=0)
    share = jnp.sum(everyone(share, DEPTH, depth), axis=0)
    g_right = pl.pallas_call(
        corner_kernel,
        out_shape=right_shape,
        in_specs=[hbm, hbm],
        out_specs=hbm,
        scratch_shapes=[
            pltpu.VMEM((2, PATCH, PATCH), F32),
            pltpu.VMEM((2, PATCH, PATCH), F32),
            pltpu.SemaphoreType.DMA((2,)),
        ],
        input_output_aliases={0: 0},
        compiler_params=small,
        name="corner",
    )(g_right, above)
    share, g_right = lax.optimization_barrier((share, g_right))
    left = lax.ppermute(g_right, COL, along)
    parts = everyone(share, PLANE, plane)

    object_gradient, probe_gradient = pl.pallas_call(
        seam_kernel,
        out_shape=(own_shape, shape(*parts.shape)),
        in_specs=[hbm] * 4,
        out_specs=(hbm, hbm),
        scratch_shapes=[
            pltpu.VMEM((2, PATCH, cols), F32),
            pltpu.VMEM((2, rows - PATCH, PATCH), F32),
            pltpu.VMEM((2, PATCH, cols), F32),
            pltpu.VMEM((2, rows, PATCH), F32),
            pltpu.VMEM(parts.shape, F32),
            pltpu.SemaphoreType.DMA((5,)),
        ],
        input_output_aliases={0: 0},
        compiler_params=small,
        name="seams",
    )(g_own, above, left, parts)
    return (object_gradient, probe_gradient.reshape(probe_modes.shape))


def solution(mesh):
    fine = Mesh(mesh.devices.reshape(4, 4, 4, 2, 2), BOTH)
    in_specs = (
        P(None, ROW, COL),
        P(),
        P(ROW, COL, None, None, None),
        P(ROW, COL, None, None),
        P(ROW, COL),
    )
    out_specs = (P(None, ROW, COL), P())
    return jax.shard_map(body, mesh=fine, in_specs=in_specs, out_specs=out_specs, check_vma=False)
```

```python
import functools
import math

import jax
import jax.numpy as jnp
import numpy as np
from jax import lax
from jax.experimental import pallas as pl
from jax.experimental.pallas import tpu as pltpu
from jax.sharding import Mesh
from jax.sharding import PartitionSpec as P

F32 = jnp.float32
BF16 = jnp.bfloat16
PATCH = 128
BLOCK = 8
VMEM_LIMIT = 63 * 2**20
SPLIT = 2 * PATCH
ROW = "z_hi"
COL = ("x", "y", "z_lo", "core")
BOTH = (ROW,) + COL
PLANE = ("x", "y", "core")
DEPTH = ("z_hi", "z_lo")


def waves_of(patch_len):
    index_range = np.arange(patch_len)
    product = (index_range[:, None] * index_range[None, :]) % patch_len
    angle = product.astype(np.float32) * np.float32(2.0 * math.pi / patch_len)
    pair = np.stack([np.cos(angle), np.sin(angle)]) / np.float32(math.sqrt(patch_len))
    return jnp.asarray(pair, F32)


def dot(a, b):
    return jnp.dot(a, b, preferred_element_type=F32)


def slot_block(at, slots, valids, pos, row_base, first_tile, field, grad, photons, probe, probe_sum, plus_ref, minus_ref):
    n = len(slots)
    lane = lax.broadcasted_iota(jnp.int32, (PATCH, PATCH), 1)
    plus = plus_ref[...]
    minus = minus_ref[...]
    places, patches, waves = [], [], []
    for s in slots:
        top = pos[0, s] - row_base
        left = pos[1, s]
        tile = left // PATCH - first_tile
        shift = left % PATCH
        back = (PATCH - shift) % PATCH
        keep = lane >= shift
        patch = []
        for k in range(2):
            a = field[tile, k, pl.ds(top, PATCH), :]
            b = field[tile + 1, k, pl.ds(top, PATCH), :]
            patch.append(pltpu.roll(jnp.where(keep, a, b), back, 1))
        places.append((top, tile, shift, keep))
        patches.append(patch)
        for m in range(2):
            pr = probe[0, m]
            pi = probe[1, m]
            wr = (pr * patch[0] - pi * patch[1]).astype(BF16)
            wi = (pr * patch[1] + pi * patch[0]).astype(BF16)
            waves.append(jnp.concatenate([wr, wi], axis=0))
    first = dot(plus, jnp.concatenate(waves, axis=1)).astype(BF16)
    cols = [slice(q * PATCH, (q + 1) * PATCH) for q in range(2 * n)]
    turned = [jnp.concatenate([first[:PATCH, q], first[PATCH:, q]], axis=1) for q in cols]
    far = dot(jnp.concatenate(turned, axis=0), minus)
    scaled = []
    for i in range(n):
        f0 = far[2 * i * PATCH:(2 * i + 1) * PATCH]
        f1 = far[(2 * i + 1) * PATCH:(2 * i + 2) * PATCH]
        power = f0 * f0 + f1 * f1
        intensity = power[:, :PATCH] + power[:, PATCH:]
        factor = (1.0 - photons[at[i]].astype(F32) / (intensity + 1.0)) * valids[i]
        for f in (f0, f1):
            re = (f[:, :PATCH] * factor).astype(BF16)
            im = (f[:, PATCH:] * factor).astype(BF16)
            scaled.append(jnp.concatenate([re, im], axis=1))
    back_pass = dot(jnp.concatenate(scaled, axis=0), plus).astype(BF16)
    unturned = [jnp.concatenate([back_pass[q, :PATCH], back_pass[q, PATCH:]], axis=0) for q in cols]
    exit_grad = dot(minus, jnp.concatenate(unturned, axis=1))
    for m in range(2):
        sum_re = sum_im = None
        for i in range(n):
            er = exit_grad[:PATCH, cols[2 * i + m]]
            ei = exit_grad[PATCH:, cols[2 * i + m]]
            o_re, o_im = patches[i]
            t_re = o_re * er + o_im * ei
            t_im = o_re * ei - o_im * er
            sum_re = t_re if sum_re is None else sum_re + t_re
            sum_im = t_im if sum_im is None else sum_im + t_im
        probe_sum[0, m] += sum_re
        probe_sum[1, m] += sum_im
    for i in range(n):
        g_re = g_im = None
        for m in range(2):
            er = exit_grad[:PATCH, cols[2 * i + m]]
            ei = exit_grad[PATCH:, cols[2 * i + m]]
            pr = probe[0, m]
            pi = probe[1, m]
            t_re = pr * er + pi * ei
            t_im = pr * ei - pi * er
            g_re = t_re if g_re is None else g_re + t_re
            g_im = t_im if g_im is None else g_im + t_im
        top, tile, shift, keep = places[i]
        for k, g in ((0, g_re), (1, g_im)):
            g = pltpu.roll(g, shift, 1)
            grad[tile, k, pl.ds(top, PATCH), :] += jnp.where(keep, g, 0.0)
            grad[tile + 1, k, pl.ds(top, PATCH), :] += jnp.where(keep, 0.0, g)


def fill_tables(waves, plus_ref, minus_ref):
    c = waves[0].astype(BF16)
    s = waves[1].astype(BF16)
    plus_ref[:PATCH, :PATCH] = c
    plus_ref[:PATCH, PATCH:] = s
    plus_ref[PATCH:, :PATCH] = -s
    plus_ref[PATCH:, PATCH:] = c
    minus_ref[:PATCH, :PATCH] = c
    minus_ref[:PATCH, PATCH:] = -s
    minus_ref[PATCH:, :PATCH] = s
    minus_ref[PATCH:, PATCH:] = c


def list_slots(wanted, pos, count, listed, photons, photon_buf, photon_sems):
    def list_step(s, found):
        chosen = wanted(pos[0, s], pos[1, s])

        @pl.when(chosen)
        def _():
            listed[found] = s
            pltpu.make_async_copy(photons.at[s], photon_buf.at[found], photon_sems.at[found]).start()

        return found + chosen.astype(jnp.int32)

    return lax.fori_loop(0, count, list_step, jnp.int32(0))


def run_slots(found, pos, row_base, first_tile, listed, field, grad, photons, photon_buf, photon_sems, probe, probe_sum,
              plus_ref, minus_ref):
    def step(k, carry, first=0, width=BLOCK):
        places = [first + k * width + i for i in range(width)]
        at = [jnp.minimum(p, found - 1) for p in places]
        slots = [listed[a] for a in at]
        valids = [jnp.where(p < found, 1.0, 0.0).astype(F32) for p in places]
        for p, a, s in zip(places, at, slots):
            @pl.when(p < found)
            def _(a=a, s=s):
                pltpu.make_async_copy(photons.at[s], photon_buf.at[a], photon_sems.at[a]).wait()

        slot_block(at, slots, valids, pos, row_base, first_tile, field, grad, photon_buf, probe, probe_sum, plus_ref, minus_ref)
        return carry

    rest = found % BLOCK
    small = (rest > 0) & (rest <= BLOCK // 2)
    blocks = found // BLOCK + ((rest > 0) & jnp.logical_not(small)).astype(jnp.int32)
    lax.fori_loop(0, blocks, step, 0)

    @pl.when(small)
    def _():
        step(0, 0, blocks * BLOCK, BLOCK // 2)


def copies_of(pairs, sems):
    return [pltpu.make_async_copy(a, b, sems.at[i]) for i, (a, b) in enumerate(pairs)]


def start_all(copies):
    for c in copies:
        c.start()


def wait_all(copies):
    for c in copies:
        c.wait()


def by_tiles(array, tiles):
    return [array.at[:, :, pl.ds(t * PATCH, PATCH)] for t in range(tiles)]


def right_rim_kernel(own, right, right_buf, sems):
    load = pltpu.make_async_copy(own.at[:, :, pl.ds(0, PATCH)], right_buf, sems.at[0])
    load.start()
    load.wait()
    store = pltpu.make_async_copy(right_buf, right, sems.at[0])
    store.start()
    store.wait()


def below_rim_kernel(own, after, below_left, below_right, corner, below_buf, sems):
    rim = pl.ds(0, PATCH)
    left_cols = below_left.shape[2]
    load = pltpu.make_async_copy(own.at[:, rim, :], below_buf, sems.at[0])
    load.start()
    load.wait()
    stores = copies_of(
        [(below_buf.at[:, :, pl.ds(0, left_cols)], below_left),
         (below_buf.at[:, :, pl.ds(left_cols, below_right.shape[2])], below_right),
         (below_buf.at[:, :, rim], corner)],
        sems,
    )
    start_all(stores)
    wait_all(stores)


def upper_kernel(pos, count, own, right, photons, probe_in, waves_in, g_own, g_right, probe_out,
                 field, grad, photon_buf, probe, waves, plus_ref, minus_ref, probe_sum, listed, sems, photon_sems):
    rows, cols = own.shape[1], own.shape[2]
    tiles = cols // PATCH
    loads = copies_of(
        [(waves_in, waves), (probe_in, probe)]
        + [(a, field.at[t]) for t, a in enumerate(by_tiles(own, tiles))]
        + [(right, field.at[tiles])],
        sems,
    )
    start_all(loads)
    found = list_slots(lambda top, left: top <= rows - PATCH, pos, count[0], listed, photons, photon_buf, photon_sems)
    grad[...] = jnp.zeros(grad.shape, F32)
    probe_sum[...] = jnp.zeros(probe_sum.shape, F32)
    loads[0].wait()
    fill_tables(waves, plus_ref, minus_ref)
    wait_all(loads[1:])
    run_slots(found, pos, 0, 0, listed, field, grad, photons, photon_buf, photon_sems, probe, probe_sum,
              plus_ref, minus_ref)
    stores = copies_of(
        [(probe_sum, probe_out)]
        + [(grad.at[t], a) for t, a in enumerate(by_tiles(g_own, tiles))]
        + [(grad.at[tiles], g_right)],
        sems,
    )
    start_all(stores)
    wait_all(stores)


def lower_kernel(wanted, first_tile, scale, pos, count, photons, probe_in, waves_in, sum_in, fields, grads, sends,
                 probe_out, field, grad, photon_buf, probe, waves, plus_ref, minus_ref, probe_sum, listed, sems,
                 photon_sems):
    upper, lower = pl.ds(0, PATCH), pl.ds(PATCH, PATCH)
    pairs = [(waves_in, waves), (probe_in, probe), (sum_in, probe_sum)]
    for t, (last, rim) in enumerate(fields):
        pairs += [(last, field.at[t, :, upper, :]), (rim, field.at[t, :, lower, :])]
    for t, (last_in, _, rim_in) in enumerate(grads):
        pairs.append((last_in, grad.at[t, :, upper, :]))
        if rim_in is not None:
            pairs.append((rim_in, grad.at[t, :, lower, :]))
    loads = copies_of(pairs, sems)
    start_all(loads)
    found = list_slots(wanted, pos, count[0], listed, photons, photon_buf, photon_sems)
    for t, (_, _, rim_in) in enumerate(grads):
        if rim_in is None:
            grad[t, :, lower, :] = jnp.zeros((2, PATCH, PATCH), F32)
    loads[0].wait()
    fill_tables(waves, plus_ref, minus_ref)
    wait_all(loads[1:])
    base = 3 * PATCH
    run_slots(found, pos, base, first_tile, listed, field, grad, photons, photon_buf, photon_sems, probe, probe_sum,
              plus_ref, minus_ref)
    if scale is not None:
        probe_sum[...] = probe_sum[...] * scale
    pairs = [(probe_sum, probe_out)]
    for t, (_, last_out, _) in enumerate(grads):
        pairs.append((grad.at[t, :, upper, :], last_out))
    for t, send in enumerate(sends):
        pairs.append((grad.at[t, :, lower, :], send))
    stores = copies_of(pairs, sems)
    start_all(stores)
    wait_all(stores)


def block_of(array, row, tile):
    return array.at[:, pl.ds(row, PATCH), pl.ds(tile * PATCH, PATCH)]


def lower_left_kernel(pos, count, own, below, photons, probe_in, waves_in, own_in, sum_in,
                      g_own, g_below, carried, probe_out, *scratch):
    base = own.shape[1] - PATCH
    lower_kernel(
        lambda top, left: (top > base) & (left < SPLIT), 0, None, pos, count, photons, probe_in, waves_in, sum_in,
        [(block_of(own, base, t), block_of(below, 0, t)) for t in range(3)],
        [(block_of(own_in, base, t), block_of(g_own, base, t), None) for t in range(3)],
        [block_of(g_below, 0, 0), block_of(g_below, 0, 1), carried],
        probe_out, *scratch,
    )


def lower_right_kernel(scale, pos, count, own, right, below_left, below_right, corner, photons, probe_in, waves_in,
                       own_in, right_in, carried, sum_in, g_own, g_right, g_below, probe_out, *scratch):
    base = own.shape[1] - PATCH
    last = pl.ds(base, PATCH)
    lower_kernel(
        lambda top, left: (top > base) & (left >= SPLIT), 2, scale, pos, count, photons, probe_in, waves_in, sum_in,
        [(block_of(own, base, 2), block_of(below_left, 0, 2)), (block_of(own, base, 3), below_right),
         (right.at[:, last, :], corner)],
        [(block_of(own_in, base, 2), block_of(g_own, base, 2), carried),
         (block_of(own_in, base, 3), block_of(g_own, base, 3), None),
         (right_in.at[:, last, :], g_right.at[:, last, :], None)],
        [block_of(g_below, 0, t) for t in range(3)],
        probe_out, *scratch,
    )


def corner_kernel(right_in, above, right, rim_buf, corner_buf, sems):
    rows = right.at[:, pl.ds(0, PATCH), :]
    corner = above.at[:, :, pl.ds(above.shape[2] - PATCH, PATCH)]
    loads = copies_of([(rows, rim_buf), (corner, corner_buf)], sems)
    start_all(loads)
    wait_all(loads)
    rim_buf[...] += corner_buf[...]
    store = pltpu.make_async_copy(rim_buf, rows, sems.at[0])
    store.start()
    store.wait()


def seam_kernel(grad_in, above_left, above_right, left, parts, grad, probe,
                top_buf, left_buf, above_buf, beside_buf, probe_buf, sems):
    rows, cols = grad.shape[1], grad.shape[2]
    rest = rows - PATCH
    top_rim = grad.at[:, pl.ds(0, PATCH), :]
    left_rim = grad.at[:, pl.ds(PATCH, rest), pl.ds(0, PATCH)]
    loads = copies_of(
        [(top_rim, top_buf), (left_rim, left_buf), (left, beside_buf),
         (above_left, above_buf.at[:, :, pl.ds(0, SPLIT)]),
         (above_right.at[:, :, pl.ds(0, cols - SPLIT)], above_buf.at[:, :, pl.ds(SPLIT, cols - SPLIT)]),
         (parts, probe_buf)],
        sems,
    )
    start_all(loads)
    wait_all(loads)
    join = pltpu.make_async_copy(probe_buf, probe, sems.at[2])
    join.start()
    top_buf[:, :, PATCH:] += above_buf[:, :, PATCH:]
    top_buf[:, :, :PATCH] += above_buf[:, :, :PATCH] + beside_buf[:, :PATCH, :]
    left_buf[...] += beside_buf[:, PATCH:, :]
    stores = copies_of([(top_buf, top_rim), (left_buf, left_rim)], sems)
    start_all(stores)
    wait_all(stores)
    join.wait()


def shape(*dims):
    return jax.ShapeDtypeStruct(dims, F32)


def everyone(value, axes, count):
    sent = jnp.broadcast_to(value[None], (count,) + value.shape)
    return lax.all_to_all(sent, axes, 0, 0, tiled=True)


def body(object_field, probe_modes, photons, positions, counts):
    rows, cols = object_field.shape[1], object_field.shape[2]
    slot_count = photons.shape[2]
    tiles = cols // PATCH
    n_row, n_col = lax.axis_size(ROW), lax.axis_size(COL)
    pos = positions[0, 0].T
    count = counts[0]
    photon_rows = photons[0, 0]
    waves = waves_of(PATCH)
    scale = 1.0 / math.sqrt(n_row * n_col * slot_count)
    down = [(i, i + 1) for i in range(n_row - 1)]
    along = [(i, i + 1) for i in range(n_col - 1)]
    up, back = ([(j, i) for i, j in pairs] for pairs in (down, along))
    diagonal = [
        (a * n_col + b, (a + 1) * n_col + b + 1) for a in range(n_row - 1) for b in range(n_col - 1)
    ]
    diagonal_back = [(j, i) for i, j in diagonal]
    smem = pl.BlockSpec(memory_space=pltpu.SMEM)
    hbm = pl.BlockSpec(memory_space=pl.ANY)
    params = pltpu.CompilerParams(vmem_limit_bytes=VMEM_LIMIT)
    small = pltpu.CompilerParams(vmem_limit_bytes=8 * 2**20)

    right = pl.pallas_call(
        right_rim_kernel,
        out_shape=shape(2, rows, PATCH),
        in_specs=[hbm],
        out_specs=hbm,
        scratch_shapes=[pltpu.VMEM((2, rows, PATCH), F32), pltpu.SemaphoreType.DMA((1,))],
        compiler_params=params,
        name="right_rim",
    )(object_field)
    rim_shape = shape(2, PATCH, PATCH)
    below_left, below_right, corner = pl.pallas_call(
        below_rim_kernel,
        out_shape=(shape(2, PATCH, SPLIT + PATCH), rim_shape, rim_shape),
        in_specs=[hbm, hbm],
        out_specs=(hbm,) * 3,
        scratch_shapes=[pltpu.VMEM((2, PATCH, cols), F32), pltpu.SemaphoreType.DMA((3,))],
        compiler_params=params,
        name="below_rim",
    )(object_field, right)
    below_left = lax.ppermute(below_left, ROW, up)
    right = lax.ppermute(right, COL, back)
    below_right, corner, right = lax.optimization_barrier((below_right, corner, right))
    below_right = lax.ppermute(below_right, ROW, up)
    corner = lax.ppermute(corner, BOTH, diagonal_back)

    def scratch(wide, height):
        return [
            pltpu.VMEM((wide, 2, height, PATCH), F32),
            pltpu.VMEM((wide, 2, height, PATCH), F32),
            pltpu.VMEM(photon_rows.shape, BF16),
            pltpu.VMEM(probe_modes.shape, F32),
            pltpu.VMEM(waves.shape, F32),
            pltpu.VMEM((2 * PATCH, 2 * PATCH), BF16),
            pltpu.VMEM((2 * PATCH, 2 * PATCH), BF16),
            pltpu.VMEM(probe_modes.shape, F32),
            pltpu.SMEM((slot_count,), jnp.int32),
            pltpu.SemaphoreType.DMA((tiles + 9,)),
            pltpu.SemaphoreType.DMA((slot_count,)),
        ]

    own_shape, right_shape, probe_shape = shape(2, rows, cols), shape(2, rows, PATCH), shape(*probe_modes.shape)
    g_own, g_right, probe_1 = pl.pallas_call(
        upper_kernel,
        out_shape=(own_shape, right_shape, probe_shape),
        in_specs=[smem, smem] + [hbm] * 5,
        out_specs=(hbm,) * 3,
        scratch_shapes=scratch(tiles + 1, rows),
        compiler_params=params,
        cost_estimate=pl.CostEstimate(flops=10**9, bytes_accessed=2**20, transcendentals=0),
        name="upper_slots",
    )(pos, count, object_field, right, photon_rows, probe_modes, waves)
    g_own, g_below_left, carried, probe_1 = pl.pallas_call(
        lower_left_kernel,
        out_shape=(own_shape, shape(2, PATCH, SPLIT), rim_shape, probe_shape),
        in_specs=[smem] * 2 + [hbm] * 7,
        out_specs=(hbm,) * 4,
        scratch_shapes=scratch(3, 2 * PATCH),
        input_output_aliases={7: 0},
        compiler_params=params,
        cost_estimate=pl.CostEstimate(flops=10**9, bytes_accessed=2**20, transcendentals=0),
        name="lower_left_slots",
    )(pos, count, object_field, below_left, photon_rows, probe_modes, waves, g_own, probe_1)
    above_left = lax.ppermute(g_below_left, ROW, down)
    g_own, g_right, g_below_right, probe_2 = pl.pallas_call(
        functools.partial(lower_right_kernel, scale),
        out_shape=(own_shape, right_shape, shape(2, PATCH, cols + PATCH - SPLIT), probe_shape),
        in_specs=[smem] * 2 + [hbm] * 12,
        out_specs=(hbm,) * 4,
        scratch_shapes=scratch(3, 2 * PATCH),
        input_output_aliases={10: 0, 11: 1},
        compiler_params=params,
        cost_estimate=pl.CostEstimate(flops=10**10, bytes_accessed=2**20, transcendentals=0),
        name="lower_right_slots",
    )(pos, count, object_field, right, below_left, below_right, corner, photon_rows, probe_modes, waves,
      g_own, g_right, carried, probe_1)

    plane, depth = lax.axis_size(PLANE), lax.axis_size(DEPTH)
    above_right = lax.ppermute(g_below_right, ROW, down)
    probe_2, above_left = lax.optimization_barrier((probe_2, above_left))
    shares = lax.all_to_all(probe_2.reshape(plane, -1, PATCH), PLANE, 0, 0, tiled=True)
    share = jnp.sum(shares, axis=0)
    share = jnp.sum(everyone(share, DEPTH, depth), axis=0)
    g_right = pl.pallas_call(
        corner_kernel,
        out_shape=right_shape,
        in_specs=[hbm, hbm],
        out_specs=hbm,
        scratch_shapes=[
            pltpu.VMEM((2, PATCH, PATCH), F32),
            pltpu.VMEM((2, PATCH, PATCH), F32),
            pltpu.SemaphoreType.DMA((2,)),
        ],
        input_output_aliases={0: 0},
        compiler_params=small,
        name="corner",
    )(g_right, above_right)
    share, g_right = lax.optimization_barrier((share, g_right))
    left = lax.ppermute(g_right, COL, along)
    parts = everyone(share, PLANE, plane)

    object_gradient, probe_gradient = pl.pallas_call(
        seam_kernel,
        out_shape=(own_shape, shape(*parts.shape)),
        in_specs=[hbm] * 5,
        out_specs=(hbm, hbm),
        scratch_shapes=[
            pltpu.VMEM((2, PATCH, cols), F32),
            pltpu.VMEM((2, rows - PATCH, PATCH), F32),
            pltpu.VMEM((2, PATCH, cols), F32),
            pltpu.VMEM((2, rows, PATCH), F32),
            pltpu.VMEM(parts.shape, F32),
            pltpu.SemaphoreType.DMA((6,)),
        ],
        input_output_aliases={0: 0},
        compiler_params=small,
        name="seams",
    )(g_own, above_left, above_right, left, parts)
    return (object_gradient, probe_gradient.reshape(probe_modes.shape))


def solution(mesh):
    fine = Mesh(mesh.devices.reshape(4, 4, 4, 2, 2), BOTH)
    in_specs = (
        P(None, ROW, COL),
        P(),
        P(ROW, COL, None, None, None),
        P(ROW, COL, None, None),
        P(ROW, COL),
    )
    out_specs = (P(None, ROW, COL), P())
    return jax.shard_map(body, mesh=fine, in_specs=in_specs, out_specs=out_specs, check_vma=False)
```

```python
import functools
import math

import jax
import jax.numpy as jnp
import numpy as np
from jax import lax
from jax.experimental import pallas as pl
from jax.experimental.pallas import tpu as pltpu
from jax.sharding import Mesh
from jax.sharding import PartitionSpec as P

F32 = jnp.float32
BF16 = jnp.bfloat16
PATCH = 128
BLOCK = 8
VMEM_LIMIT = 63 * 2**20
ROW = "z_hi"
COL = ("x", "y", "z_lo", "core")
BOTH = (ROW,) + COL
PLANE = ("x", "y", "core")
DEPTH = ("z_hi", "z_lo")


def waves_of(patch_len):
    index_range = np.arange(patch_len)
    product = (index_range[:, None] * index_range[None, :]) % patch_len
    angle = product.astype(np.float32) * np.float32(2.0 * math.pi / patch_len)
    pair = np.stack([np.cos(angle), np.sin(angle)]) / np.float32(math.sqrt(patch_len))
    return jnp.asarray(pair, F32)


def dot(a, b):
    return jnp.dot(a, b, preferred_element_type=F32)


def slot_block(at, slots, valids, pos, row_base, field, grad, photons, probe, probe_sum, plus_ref, minus_ref):
    n = len(slots)
    lane = lax.broadcasted_iota(jnp.int32, (PATCH, PATCH), 1)
    plus = plus_ref[...]
    minus = minus_ref[...]
    places, patches, waves = [], [], []
    for s in slots:
        top = pos[0, s] - row_base
        left = pos[1, s]
        tile = left // PATCH
        shift = left % PATCH
        back = (PATCH - shift) % PATCH
        keep = lane >= shift
        patch = []
        for k in range(2):
            a = field[tile, k, pl.ds(top, PATCH), :]
            b = field[tile + 1, k, pl.ds(top, PATCH), :]
            patch.append(pltpu.roll(jnp.where(keep, a, b), back, 1))
        places.append((top, tile, shift, keep))
        patches.append(patch)
        for m in range(2):
            pr = probe[0, m]
            pi = probe[1, m]
            wr = (pr * patch[0] - pi * patch[1]).astype(BF16)
            wi = (pr * patch[1] + pi * patch[0]).astype(BF16)
            waves.append(jnp.concatenate([wr, wi], axis=0))
    first = dot(plus, jnp.concatenate(waves, axis=1)).astype(BF16)
    cols = [slice(q * PATCH, (q + 1) * PATCH) for q in range(2 * n)]
    turned = [jnp.concatenate([first[:PATCH, q], first[PATCH:, q]], axis=1) for q in cols]
    far = dot(jnp.concatenate(turned, axis=0), minus)
    scaled = []
    for i in range(n):
        f0 = far[2 * i * PATCH:(2 * i + 1) * PATCH]
        f1 = far[(2 * i + 1) * PATCH:(2 * i + 2) * PATCH]
        power = f0 * f0 + f1 * f1
        intensity = power[:, :PATCH] + power[:, PATCH:]
        factor = (1.0 - photons[at[i]].astype(F32) / (intensity + 1.0)) * valids[i]
        for f in (f0, f1):
            re = (f[:, :PATCH] * factor).astype(BF16)
            im = (f[:, PATCH:] * factor).astype(BF16)
            scaled.append(jnp.concatenate([re, im], axis=1))
    back_pass = dot(jnp.concatenate(scaled, axis=0), plus).astype(BF16)
    unturned = [jnp.concatenate([back_pass[q, :PATCH], back_pass[q, PATCH:]], axis=0) for q in cols]
    exit_grad = dot(minus, jnp.concatenate(unturned, axis=1))
    for m in range(2):
        sum_re = sum_im = None
        for i in range(n):
            er = exit_grad[:PATCH, cols[2 * i + m]]
            ei = exit_grad[PATCH:, cols[2 * i + m]]
            o_re, o_im = patches[i]
            t_re = o_re * er + o_im * ei
            t_im = o_re * ei - o_im * er
            sum_re = t_re if sum_re is None else sum_re + t_re
            sum_im = t_im if sum_im is None else sum_im + t_im
        probe_sum[0, m] += sum_re
        probe_sum[1, m] += sum_im
    for i in range(n):
        g_re = g_im = None
        for m in range(2):
            er = exit_grad[:PATCH, cols[2 * i + m]]
            ei = exit_grad[PATCH:, cols[2 * i + m]]
            pr = probe[0, m]
            pi = probe[1, m]
            t_re = pr * er + pi * ei
            t_im = pr * ei - pi * er
            g_re = t_re if g_re is None else g_re + t_re
            g_im = t_im if g_im is None else g_im + t_im
        top, tile, shift, keep = places[i]
        for k, g in ((0, g_re), (1, g_im)):
            g = pltpu.roll(g, shift, 1)
            grad[tile, k, pl.ds(top, PATCH), :] += jnp.where(keep, g, 0.0)
            grad[tile + 1, k, pl.ds(top, PATCH), :] += jnp.where(keep, 0.0, g)


def fill_tables(waves, plus_ref, minus_ref):
    c = waves[0].astype(BF16)
    s = waves[1].astype(BF16)
    plus_ref[:PATCH, :PATCH] = c
    plus_ref[:PATCH, PATCH:] = s
    plus_ref[PATCH:, :PATCH] = -s
    plus_ref[PATCH:, PATCH:] = c
    minus_ref[:PATCH, :PATCH] = c
    minus_ref[:PATCH, PATCH:] = -s
    minus_ref[PATCH:, :PATCH] = s
    minus_ref[PATCH:, PATCH:] = c


def list_slots(wanted, pos, count, listed, photons, photon_buf, photon_sems):
    def list_step(s, found):
        chosen = wanted(pos[0, s])

        @pl.when(chosen)
        def _():
            listed[found] = s
            pltpu.make_async_copy(photons.at[s], photon_buf.at[found], photon_sems.at[found]).start()

        return found + chosen.astype(jnp.int32)

    return lax.fori_loop(0, count, list_step, jnp.int32(0))


def run_slots(found, pos, row_base, listed, field, grad, photons, photon_buf, photon_sems, probe, probe_sum,
              plus_ref, minus_ref):
    def step(k, carry, first=0, width=BLOCK):
        places = [first + k * width + i for i in range(width)]
        at = [jnp.minimum(p, found - 1) for p in places]
        slots = [listed[a] for a in at]
        valids = [jnp.where(p < found, 1.0, 0.0).astype(F32) for p in places]
        for p, a, s in zip(places, at, slots):
            @pl.when(p < found)
            def _(a=a, s=s):
                pltpu.make_async_copy(photons.at[s], photon_buf.at[a], photon_sems.at[a]).wait()

        slot_block(at, slots, valids, pos, row_base, field, grad, photon_buf, probe, probe_sum, plus_ref, minus_ref)
        return carry

    rest = found % BLOCK
    small = (rest > 0) & (rest <= BLOCK // 2)
    blocks = found // BLOCK + ((rest > 0) & jnp.logical_not(small)).astype(jnp.int32)
    lax.fori_loop(0, blocks, step, 0)

    @pl.when(small)
    def _():
        step(0, 0, blocks * BLOCK, BLOCK // 2)


def copies_of(pairs, sems):
    return [pltpu.make_async_copy(a, b, sems.at[i]) for i, (a, b) in enumerate(pairs)]


def start_all(copies):
    for c in copies:
        c.start()


def wait_all(copies):
    for c in copies:
        c.wait()


def by_tiles(array, tiles):
    return [array.at[:, :, pl.ds(t * PATCH, PATCH)] for t in range(tiles)]


def right_rim_kernel(own, right, right_buf, sems):
    load = pltpu.make_async_copy(own.at[:, :, pl.ds(0, PATCH)], right_buf, sems.at[0])
    load.start()
    load.wait()
    store = pltpu.make_async_copy(right_buf, right, sems.at[0])
    store.start()
    store.wait()


def below_rim_kernel(own, after, below, corner, below_buf, sems):
    rim = pl.ds(0, PATCH)
    load = pltpu.make_async_copy(own.at[:, rim, :], below_buf, sems.at[0])
    load.start()
    load.wait()
    stores = copies_of([(below_buf, below), (below_buf.at[:, :, rim], corner)], sems)
    start_all(stores)
    wait_all(stores)


def upper_kernel(pos, count, own, right, photons, probe_in, waves_in, g_own, g_right, probe_out,
                 field, grad, photon_buf, probe, waves, plus_ref, minus_ref, probe_sum, listed, sems, photon_sems):
    rows, cols = own.shape[1], own.shape[2]
    tiles = cols // PATCH
    loads = copies_of(
        [(waves_in, waves), (probe_in, probe)]
        + [(a, field.at[t]) for t, a in enumerate(by_tiles(own, tiles))]
        + [(right, field.at[tiles])],
        sems,
    )
    start_all(loads)
    found = list_slots(lambda top: top <= rows - PATCH, pos, count[0], listed, photons, photon_buf, photon_sems)
    grad[...] = jnp.zeros(grad.shape, F32)
    probe_sum[...] = jnp.zeros(probe_sum.shape, F32)
    loads[0].wait()
    fill_tables(waves, plus_ref, minus_ref)
    wait_all(loads[1:])
    run_slots(found, pos, 0, listed, field, grad, photons, photon_buf, photon_sems, probe, probe_sum,
              plus_ref, minus_ref)
    stores = copies_of(
        [(probe_sum, probe_out)]
        + [(grad.at[t], a) for t, a in enumerate(by_tiles(g_own, tiles))]
        + [(grad.at[tiles], g_right.at[:, pl.ds(0, rows), :])],
        sems,
    )
    start_all(stores)
    wait_all(stores)


def lower_kernel(scale, pos, count, own, right, below, corner, photons, probe_in, waves_in, own_in, right_in, sum_in,
                 g_own, g_right, g_first, g_rest, probe_out,
                 field, grad, photon_buf, probe, waves, plus_ref, minus_ref, probe_sum, listed, sems, photon_sems):
    rows, cols = own.shape[1], own.shape[2]
    tiles = cols // PATCH
    base = rows - PATCH
    last, upper, lower = pl.ds(base, PATCH), pl.ds(0, PATCH), pl.ds(PATCH, PATCH)

    def last_rows(array):
        return [array.at[:, last, pl.ds(t * PATCH, PATCH)] for t in range(tiles)]

    loads = copies_of(
        [(waves_in, waves), (probe_in, probe), (sum_in, probe_sum)]
        + [(a, field.at[t, :, upper, :]) for t, a in enumerate(last_rows(own) + [right.at[:, last, :]])]
        + [(a, field.at[t, :, lower, :]) for t, a in enumerate(by_tiles(below, tiles) + [corner])]
        + [(a, grad.at[t, :, upper, :]) for t, a in enumerate(last_rows(own_in) + [right_in.at[:, last, :]])],
        sems,
    )
    start_all(loads)
    found = list_slots(lambda top: top > base, pos, count[0], listed, photons, photon_buf, photon_sems)
    for t in range(tiles + 1):
        grad[t, :, lower, :] = jnp.zeros((2, PATCH, PATCH), F32)
    loads[0].wait()
    fill_tables(waves, plus_ref, minus_ref)
    wait_all(loads[1:])
    run_slots(found, pos, base, listed, field, grad, photons, photon_buf, photon_sems, probe, probe_sum,
              plus_ref, minus_ref)
    probe_sum[...] = probe_sum[...] * scale
    stores = copies_of(
        [(probe_sum, probe_out)]
        + [(grad.at[t, :, lower, :], a) for t, a in enumerate([g_first] + by_tiles(g_rest, tiles - 1))]
        + [(grad.at[t, :, upper, :], a) for t, a in enumerate(last_rows(g_own))]
        + [(grad.at[tiles], g_right.at[:, pl.ds(base, 2 * PATCH), :])],
        sems,
    )
    start_all(stores)
    wait_all(stores)


def corner_kernel(first, left, total, rim_buf, corner_buf, sems):
    corner = left.at[:, pl.ds(left.shape[1] - PATCH, PATCH), :]
    loads = copies_of([(first, rim_buf), (corner, corner_buf)], sems)
    start_all(loads)
    wait_all(loads)
    rim_buf[...] += corner_buf[...]
    store = pltpu.make_async_copy(rim_buf, total, sems.at[0])
    store.start()
    store.wait()


def seam_kernel(grad_in, above_first, above_rest, left, parts, grad, probe,
                top_buf, left_buf, above_buf, beside_buf, probe_buf, sems):
    rows, cols = grad.shape[1], grad.shape[2]
    rest = rows - PATCH
    top_rim = grad.at[:, pl.ds(0, PATCH), :]
    left_rim = grad.at[:, pl.ds(PATCH, rest), pl.ds(0, PATCH)]
    loads = copies_of(
        [(top_rim, top_buf), (left_rim, left_buf), (left.at[:, pl.ds(0, rows), :], beside_buf),
         (above_first, above_buf.at[:, :, pl.ds(0, PATCH)]),
         (above_rest, above_buf.at[:, :, pl.ds(PATCH, cols - PATCH)]),
         (parts, probe_buf)],
        sems,
    )
    start_all(loads)
    wait_all(loads)
    join = pltpu.make_async_copy(probe_buf, probe, sems.at[2])
    join.start()
    top_buf[:, :, PATCH:] += above_buf[:, :, PATCH:]
    top_buf[:, :, :PATCH] += above_buf[:, :, :PATCH] + beside_buf[:, :PATCH, :]
    left_buf[...] += beside_buf[:, PATCH:, :]
    stores = copies_of([(top_buf, top_rim), (left_buf, left_rim)], sems)
    start_all(stores)
    wait_all(stores)
    join.wait()


def shape(*dims):
    return jax.ShapeDtypeStruct(dims, F32)


def everyone(value, axes, count):
    sent = jnp.broadcast_to(value[None], (count,) + value.shape)
    return lax.all_to_all(sent, axes, 0, 0, tiled=True)


def body(object_field, probe_modes, photons, positions, counts):
    rows, cols = object_field.shape[1], object_field.shape[2]
    slot_count = photons.shape[2]
    tiles = cols // PATCH
    n_row, n_col = lax.axis_size(ROW), lax.axis_size(COL)
    pos = positions[0, 0].T
    count = counts[0]
    photon_rows = photons[0, 0]
    waves = waves_of(PATCH)
    scale = 1.0 / math.sqrt(n_row * n_col * slot_count)
    down = [(i, i + 1) for i in range(n_row - 1)]
    along = [(i, i + 1) for i in range(n_col - 1)]
    up, back = ([(j, i) for i, j in pairs] for pairs in (down, along))
    diagonal = [
        (a * n_col + b, (a + 1) * n_col + b + 1) for a in range(n_row - 1) for b in range(n_col - 1)
    ]
    diagonal_back = [(j, i) for i, j in diagonal]
    smem = pl.BlockSpec(memory_space=pltpu.SMEM)
    hbm = pl.BlockSpec(memory_space=pl.ANY)
    params = pltpu.CompilerParams(vmem_limit_bytes=VMEM_LIMIT)
    small = pltpu.CompilerParams(vmem_limit_bytes=8 * 2**20)

    right = pl.pallas_call(
        right_rim_kernel,
        out_shape=shape(2, rows, PATCH),
        in_specs=[hbm],
        out_specs=hbm,
        scratch_shapes=[pltpu.VMEM((2, rows, PATCH), F32), pltpu.SemaphoreType.DMA((1,))],
        compiler_params=params,
        name="right_rim",
    )(object_field)
    below, corner = pl.pallas_call(
        below_rim_kernel,
        out_shape=(shape(2, PATCH, cols), shape(2, PATCH, PATCH)),
        in_specs=[hbm, hbm],
        out_specs=(hbm,) * 2,
        scratch_shapes=[pltpu.VMEM((2, PATCH, cols), F32), pltpu.SemaphoreType.DMA((2,))],
        compiler_params=params,
        name="below_rim",
    )(object_field, right)
    below = lax.ppermute(below, ROW, up)
    right = lax.ppermute(right, COL, back)
    corner = lax.ppermute(corner, BOTH, diagonal_back)

    def scratch(height):
        return [
            pltpu.VMEM((tiles + 1, 2, height, PATCH), F32),
            pltpu.VMEM((tiles + 1, 2, height, PATCH), F32),
            pltpu.VMEM(photon_rows.shape, BF16),
            pltpu.VMEM(probe_modes.shape, F32),
            pltpu.VMEM(waves.shape, F32),
            pltpu.VMEM((2 * PATCH, 2 * PATCH), BF16),
            pltpu.VMEM((2 * PATCH, 2 * PATCH), BF16),
            pltpu.VMEM(probe_modes.shape, F32),
            pltpu.SMEM((slot_count,), jnp.int32),
            pltpu.SemaphoreType.DMA((3 * tiles + 6,)),
            pltpu.SemaphoreType.DMA((slot_count,)),
        ]

    own_shape, right_shape, probe_shape = shape(2, rows, cols), shape(2, rows + PATCH, PATCH), shape(*probe_modes.shape)
    g_own, g_right, probe_1 = pl.pallas_call(
        upper_kernel,
        out_shape=(own_shape, right_shape, probe_shape),
        in_specs=[smem, smem] + [hbm] * 5,
        out_specs=(hbm,) * 3,
        scratch_shapes=scratch(rows),
        compiler_params=params,
        cost_estimate=pl.CostEstimate(flops=10**9, bytes_accessed=2**20, transcendentals=0),
        name="upper_slots",
    )(pos, count, object_field, right, photon_rows, probe_modes, waves)
    rim_shape = shape(2, PATCH, PATCH)
    g_own, g_right, g_first, g_rest, probe_2 = pl.pallas_call(
        functools.partial(lower_kernel, scale),
        out_shape=(own_shape, right_shape, rim_shape, shape(2, PATCH, cols - PATCH), probe_shape),
        in_specs=[smem] * 2 + [hbm] * 10,
        out_specs=(hbm,) * 5,
        scratch_shapes=scratch(2 * PATCH),
        input_output_aliases={9: 0, 10: 1},
        compiler_params=params,
        cost_estimate=pl.CostEstimate(flops=10**9, bytes_accessed=2**20, transcendentals=0),
        name="lower_slots",
    )(pos, count, object_field, right, below, corner, photon_rows, probe_modes, waves, g_own, g_right, probe_1)

    plane, depth = lax.axis_size(PLANE), lax.axis_size(DEPTH)
    left = lax.ppermute(g_right, COL, along)
    above_rest = lax.ppermute(g_rest, ROW, down)
    shares = lax.all_to_all(probe_2.reshape(plane, -1, PATCH), PLANE, 0, 0, tiled=True)
    share = jnp.sum(shares, axis=0)
    share, left = lax.optimization_barrier((share, left))
    g_first = pl.pallas_call(
        corner_kernel,
        out_shape=rim_shape,
        in_specs=[hbm, hbm],
        out_specs=hbm,
        scratch_shapes=[
            pltpu.VMEM((2, PATCH, PATCH), F32),
            pltpu.VMEM((2, PATCH, PATCH), F32),
            pltpu.SemaphoreType.DMA((2,)),
        ],
        compiler_params=small,
        name="corner",
    )(g_first, left)
    share, g_first = lax.optimization_barrier((share, g_first))
    above_first = lax.ppermute(g_first, ROW, down)
    share = jnp.sum(everyone(share, DEPTH, depth), axis=0)
    share, above_first, above_rest = lax.optimization_barrier((share, above_first, above_rest))
    parts = everyone(share, PLANE, plane)

    object_gradient, probe_gradient = pl.pallas_call(
        seam_kernel,
        out_shape=(own_shape, shape(*parts.shape)),
        in_specs=[hbm] * 5,
        out_specs=(hbm, hbm),
        scratch_shapes=[
            pltpu.VMEM((2, PATCH, cols), F32),
            pltpu.VMEM((2, rows - PATCH, PATCH), F32),
            pltpu.VMEM((2, PATCH, cols), F32),
            pltpu.VMEM((2, rows, PATCH), F32),
            pltpu.VMEM(parts.shape, F32),
            pltpu.SemaphoreType.DMA((6,)),
        ],
        input_output_aliases={0: 0},
        compiler_params=small,
        name="seams",
    )(g_own, above_first, above_rest, left, parts)
    return (object_gradient, probe_gradient.reshape(probe_modes.shape))


def solution(mesh):
    fine = Mesh(mesh.devices.reshape(4, 4, 4, 2, 2), BOTH)
    in_specs = (
        P(None, ROW, COL),
        P(),
        P(ROW, COL, None, None, None),
        P(ROW, COL, None, None),
        P(ROW, COL),
    )
    out_specs = (P(None, ROW, COL), P())
    return jax.shard_map(body, mesh=fine, in_specs=in_specs, out_specs=out_specs, check_vma=False)
```

```python
import functools
import math

import jax
import jax.numpy as jnp
import numpy as np
from jax import lax
from jax.experimental import pallas as pl
from jax.experimental.pallas import tpu as pltpu
from jax.sharding import Mesh
from jax.sharding import PartitionSpec as P

F32 = jnp.float32
BF16 = jnp.bfloat16
PATCH = 128
BLOCK = 8
VMEM_LIMIT = 63 * 2**20
ROW = "z_hi"
COL = ("x", "y", "z_lo", "core")
BOTH = (ROW,) + COL
PLANE = ("x", "y", "core")
DEPTH = ("z_hi", "z_lo")


def waves_of(patch_len):
    index_range = np.arange(patch_len)
    product = (index_range[:, None] * index_range[None, :]) % patch_len
    angle = product.astype(np.float32) * np.float32(2.0 * math.pi / patch_len)
    pair = np.stack([np.cos(angle), np.sin(angle)]) / np.float32(math.sqrt(patch_len))
    return jnp.asarray(pair, F32)


def dot(a, b):
    return jnp.dot(a, b, preferred_element_type=F32)


def slot_block(at, slots, valids, pos, row_base, field, grad, photons, probe, probe_sum, plus_ref, minus_ref):
    n = len(slots)
    lane = lax.broadcasted_iota(jnp.int32, (PATCH, PATCH), 1)
    plus = plus_ref[...]
    minus = minus_ref[...]
    places, patches, waves = [], [], []
    for s in slots:
        top = pos[0, s] - row_base
        left = pos[1, s]
        tile = left // PATCH
        shift = left % PATCH
        back = (PATCH - shift) % PATCH
        keep = lane >= shift
        patch = []
        for k in range(2):
            a = field[tile, k, pl.ds(top, PATCH), :]
            b = field[tile + 1, k, pl.ds(top, PATCH), :]
            patch.append(pltpu.roll(jnp.where(keep, a, b), back, 1))
        places.append((top, tile, shift, keep))
        patches.append(patch)
        for m in range(2):
            pr = probe[0, m]
            pi = probe[1, m]
            wr = (pr * patch[0] - pi * patch[1]).astype(BF16)
            wi = (pr * patch[1] + pi * patch[0]).astype(BF16)
            waves.append(jnp.concatenate([wr, wi], axis=0))
    first = dot(plus, jnp.concatenate(waves, axis=1)).astype(BF16)
    cols = [slice(q * PATCH, (q + 1) * PATCH) for q in range(2 * n)]
    turned = [jnp.concatenate([first[:PATCH, q], first[PATCH:, q]], axis=1) for q in cols]
    far = dot(jnp.concatenate(turned, axis=0), minus)
    scaled = []
    for i in range(n):
        f0 = far[2 * i * PATCH:(2 * i + 1) * PATCH]
        f1 = far[(2 * i + 1) * PATCH:(2 * i + 2) * PATCH]
        power = f0 * f0 + f1 * f1
        intensity = power[:, :PATCH] + power[:, PATCH:]
        factor = (1.0 - photons[at[i]].astype(F32) / (intensity + 1.0)) * valids[i]
        for f in (f0, f1):
            re = (f[:, :PATCH] * factor).astype(BF16)
            im = (f[:, PATCH:] * factor).astype(BF16)
            scaled.append(jnp.concatenate([re, im], axis=1))
    back_pass = dot(jnp.concatenate(scaled, axis=0), plus).astype(BF16)
    unturned = [jnp.concatenate([back_pass[q, :PATCH], back_pass[q, PATCH:]], axis=0) for q in cols]
    exit_grad = dot(minus, jnp.concatenate(unturned, axis=1))
    for m in range(2):
        sum_re = sum_im = None
        for i in range(n):
            er = exit_grad[:PATCH, cols[2 * i + m]]
            ei = exit_grad[PATCH:, cols[2 * i + m]]
            o_re, o_im = patches[i]
            t_re = o_re * er + o_im * ei
            t_im = o_re * ei - o_im * er
            sum_re = t_re if sum_re is None else sum_re + t_re
            sum_im = t_im if sum_im is None else sum_im + t_im
        probe_sum[0, m] += sum_re
        probe_sum[1, m] += sum_im
    for i in range(n):
        g_re = g_im = None
        for m in range(2):
            er = exit_grad[:PATCH, cols[2 * i + m]]
            ei = exit_grad[PATCH:, cols[2 * i + m]]
            pr = probe[0, m]
            pi = probe[1, m]
            t_re = pr * er + pi * ei
            t_im = pr * ei - pi * er
            g_re = t_re if g_re is None else g_re + t_re
            g_im = t_im if g_im is None else g_im + t_im
        top, tile, shift, keep = places[i]
        for k, g in ((0, g_re), (1, g_im)):
            g = pltpu.roll(g, shift, 1)
            grad[tile, k, pl.ds(top, PATCH), :] += jnp.where(keep, g, 0.0)
            grad[tile + 1, k, pl.ds(top, PATCH), :] += jnp.where(keep, 0.0, g)


def fill_tables(waves, plus_ref, minus_ref):
    c = waves[0].astype(BF16)
    s = waves[1].astype(BF16)
    plus_ref[:PATCH, :PATCH] = c
    plus_ref[:PATCH, PATCH:] = s
    plus_ref[PATCH:, :PATCH] = -s
    plus_ref[PATCH:, PATCH:] = c
    minus_ref[:PATCH, :PATCH] = c
    minus_ref[:PATCH, PATCH:] = -s
    minus_ref[PATCH:, :PATCH] = s
    minus_ref[PATCH:, PATCH:] = c


def list_slots(wanted, pos, count, listed, photons, photon_buf, photon_sems):
    def list_step(s, found):
        chosen = wanted(pos[0, s])

        @pl.when(chosen)
        def _():
            listed[found] = s
            pltpu.make_async_copy(photons.at[s], photon_buf.at[found], photon_sems.at[found]).start()

        return found + chosen.astype(jnp.int32)

    return lax.fori_loop(0, count, list_step, jnp.int32(0))


def run_slots(found, pos, row_base, listed, field, grad, photons, photon_buf, photon_sems, probe, probe_sum,
              plus_ref, minus_ref):
    def step(k, carry, first=0, width=BLOCK):
        places = [first + k * width + i for i in range(width)]
        at = [jnp.minimum(p, found - 1) for p in places]
        slots = [listed[a] for a in at]
        valids = [jnp.where(p < found, 1.0, 0.0).astype(F32) for p in places]
        for p, a, s in zip(places, at, slots):
            @pl.when(p < found)
            def _(a=a, s=s):
                pltpu.make_async_copy(photons.at[s], photon_buf.at[a], photon_sems.at[a]).wait()

        slot_block(at, slots, valids, pos, row_base, field, grad, photon_buf, probe, probe_sum, plus_ref, minus_ref)
        return carry

    rest = found % BLOCK
    small = (rest > 0) & (rest <= BLOCK // 2)
    blocks = found // BLOCK + ((rest > 0) & jnp.logical_not(small)).astype(jnp.int32)
    lax.fori_loop(0, blocks, step, 0)

    @pl.when(small)
    def _():
        step(0, 0, blocks * BLOCK, BLOCK // 2)


def copies_of(pairs, sems):
    return [pltpu.make_async_copy(a, b, sems.at[i]) for i, (a, b) in enumerate(pairs)]


def start_all(copies):
    for c in copies:
        c.start()


def wait_all(copies):
    for c in copies:
        c.wait()


def by_tiles(array, tiles):
    return [array.at[:, :, pl.ds(t * PATCH, PATCH)] for t in range(tiles)]


def right_rim_kernel(own, right, right_buf, sems):
    load = pltpu.make_async_copy(own.at[:, :, pl.ds(0, PATCH)], right_buf, sems.at[0])
    load.start()
    load.wait()
    store = pltpu.make_async_copy(right_buf, right, sems.at[0])
    store.start()
    store.wait()


def below_rim_kernel(own, after, below, corner, below_buf, sems):
    rim = pl.ds(0, PATCH)
    load = pltpu.make_async_copy(own.at[:, rim, :], below_buf, sems.at[0])
    load.start()
    load.wait()
    stores = copies_of([(below_buf, below), (below_buf.at[:, :, rim], corner)], sems)
    start_all(stores)
    wait_all(stores)


def upper_kernel(pos, count, own, right, photons, probe_in, waves_in, g_own, g_right, probe_out,
                 field, grad, photon_buf, probe, waves, plus_ref, minus_ref, probe_sum, listed, sems, photon_sems):
    rows, cols = own.shape[1], own.shape[2]
    tiles = cols // PATCH
    loads = copies_of(
        [(waves_in, waves), (probe_in, probe)]
        + [(a, field.at[t]) for t, a in enumerate(by_tiles(own, tiles))]
        + [(right, field.at[tiles])],
        sems,
    )
    start_all(loads)
    found = list_slots(lambda top: top <= rows - PATCH, pos, count[0], listed, photons, photon_buf, photon_sems)
    grad[...] = jnp.zeros(grad.shape, F32)
    probe_sum[...] = jnp.zeros(probe_sum.shape, F32)
    loads[0].wait()
    fill_tables(waves, plus_ref, minus_ref)
    wait_all(loads[1:])
    run_slots(found, pos, 0, listed, field, grad, photons, photon_buf, photon_sems, probe, probe_sum,
              plus_ref, minus_ref)
    stores = copies_of(
        [(probe_sum, probe_out)]
        + [(grad.at[t], a) for t, a in enumerate(by_tiles(g_own, tiles))]
        + [(grad.at[tiles], g_right.at[:, pl.ds(0, rows), :])],
        sems,
    )
    start_all(stores)
    wait_all(stores)


def lower_kernel(scale, pos, count, own, right, below, corner, photons, probe_in, waves_in, own_in, right_in, sum_in,
                 g_own, g_right, g_first, g_rest, probe_out,
                 field, grad, photon_buf, probe, waves, plus_ref, minus_ref, probe_sum, listed, sems, photon_sems):
    rows, cols = own.shape[1], own.shape[2]
    tiles = cols // PATCH
    base = rows - PATCH
    last, upper, lower = pl.ds(base, PATCH), pl.ds(0, PATCH), pl.ds(PATCH, PATCH)

    def last_rows(array):
        return [array.at[:, last, pl.ds(t * PATCH, PATCH)] for t in range(tiles)]

    loads = copies_of(
        [(waves_in, waves), (probe_in, probe), (sum_in, probe_sum)]
        + [(a, field.at[t, :, upper, :]) for t, a in enumerate(last_rows(own) + [right.at[:, last, :]])]
        + [(a, field.at[t, :, lower, :]) for t, a in enumerate(by_tiles(below, tiles) + [corner])]
        + [(a, grad.at[t, :, upper, :]) for t, a in enumerate(last_rows(own_in) + [right_in.at[:, last, :]])],
        sems,
    )
    start_all(loads)
    found = list_slots(lambda top: top > base, pos, count[0], listed, photons, photon_buf, photon_sems)
    for t in range(tiles + 1):
        grad[t, :, lower, :] = jnp.zeros((2, PATCH, PATCH), F32)
    loads[0].wait()
    fill_tables(waves, plus_ref, minus_ref)
    wait_all(loads[1:])
    run_slots(found, pos, base, listed, field, grad, photons, photon_buf, photon_sems, probe, probe_sum,
              plus_ref, minus_ref)
    probe_sum[...] = probe_sum[...] * scale
    stores = copies_of(
        [(probe_sum, probe_out)]
        + [(grad.at[t, :, lower, :], a) for t, a in enumerate([g_first] + by_tiles(g_rest, tiles - 1))]
        + [(grad.at[t, :, upper, :], a) for t, a in enumerate(last_rows(g_own))]
        + [(grad.at[tiles], g_right.at[:, pl.ds(base, 2 * PATCH), :])],
        sems,
    )
    start_all(stores)
    wait_all(stores)


def corner_kernel(first, left, total, rim_buf, corner_buf, sems):
    corner = left.at[:, pl.ds(left.shape[1] - PATCH, PATCH), :]
    loads = copies_of([(first, rim_buf), (corner, corner_buf)], sems)
    start_all(loads)
    wait_all(loads)
    rim_buf[...] += corner_buf[...]
    store = pltpu.make_async_copy(rim_buf, total, sems.at[0])
    store.start()
    store.wait()


def seam_kernel(grad_in, above_first, above_rest, left, grad, top_buf, left_buf, above_buf, beside_buf, sems):
    rows, cols = grad.shape[1], grad.shape[2]
    rest = rows - PATCH
    top_rim = grad.at[:, pl.ds(0, PATCH), :]
    left_rim = grad.at[:, pl.ds(PATCH, rest), pl.ds(0, PATCH)]
    loads = copies_of(
        [(top_rim, top_buf), (left_rim, left_buf), (left.at[:, pl.ds(0, rows), :], beside_buf),
         (above_first, above_buf.at[:, :, pl.ds(0, PATCH)]),
         (above_rest, above_buf.at[:, :, pl.ds(PATCH, cols - PATCH)])],
        sems,
    )
    start_all(loads)
    wait_all(loads)
    top_buf[:, :, PATCH:] += above_buf[:, :, PATCH:]
    top_buf[:, :, :PATCH] += above_buf[:, :, :PATCH] + beside_buf[:, :PATCH, :]
    left_buf[...] += beside_buf[:, PATCH:, :]
    stores = copies_of([(top_buf, top_rim), (left_buf, left_rim)], sems)
    start_all(stores)
    wait_all(stores)


def shape(*dims):
    return jax.ShapeDtypeStruct(dims, F32)


def everyone(value, axes, count):
    sent = jnp.broadcast_to(value[None], (count,) + value.shape)
    return lax.all_to_all(sent, axes, 0, 0, tiled=True)


def body(object_field, probe_modes, photons, positions, counts):
    rows, cols = object_field.shape[1], object_field.shape[2]
    slot_count = photons.shape[2]
    tiles = cols // PATCH
    n_row, n_col = lax.axis_size(ROW), lax.axis_size(COL)
    pos = positions[0, 0].T
    count = counts[0]
    photon_rows = photons[0, 0]
    waves = waves_of(PATCH)
    scale = 1.0 / math.sqrt(n_row * n_col * slot_count)
    down = [(i, i + 1) for i in range(n_row - 1)]
    along = [(i, i + 1) for i in range(n_col - 1)]
    up, back = ([(j, i) for i, j in pairs] for pairs in (down, along))
    diagonal = [
        (a * n_col + b, (a + 1) * n_col + b + 1) for a in range(n_row - 1) for b in range(n_col - 1)
    ]
    diagonal_back = [(j, i) for i, j in diagonal]
    smem = pl.BlockSpec(memory_space=pltpu.SMEM)
    hbm = pl.BlockSpec(memory_space=pl.ANY)
    params = pltpu.CompilerParams(vmem_limit_bytes=VMEM_LIMIT)
    small = pltpu.CompilerParams(vmem_limit_bytes=8 * 2**20)

    right = pl.pallas_call(
        right_rim_kernel,
        out_shape=shape(2, rows, PATCH),
        in_specs=[hbm],
        out_specs=hbm,
        scratch_shapes=[pltpu.VMEM((2, rows, PATCH), F32), pltpu.SemaphoreType.DMA((1,))],
        compiler_params=params,
        name="right_rim",
    )(object_field)
    below, corner = pl.pallas_call(
        below_rim_kernel,
        out_shape=(shape(2, PATCH, cols), shape(2, PATCH, PATCH)),
        in_specs=[hbm, hbm],
        out_specs=(hbm,) * 2,
        scratch_shapes=[pltpu.VMEM((2, PATCH, cols), F32), pltpu.SemaphoreType.DMA((2,))],
        compiler_params=params,
        name="below_rim",
    )(object_field, right)
    below = lax.ppermute(below, ROW, up)
    right = lax.ppermute(right, COL, back)
    corner = lax.ppermute(corner, BOTH, diagonal_back)

    def scratch(height):
        return [
            pltpu.VMEM((tiles + 1, 2, height, PATCH), F32),
            pltpu.VMEM((tiles + 1, 2, height, PATCH), F32),
            pltpu.VMEM(photon_rows.shape, BF16),
            pltpu.VMEM(probe_modes.shape, F32),
            pltpu.VMEM(waves.shape, F32),
            pltpu.VMEM((2 * PATCH, 2 * PATCH), BF16),
            pltpu.VMEM((2 * PATCH, 2 * PATCH), BF16),
            pltpu.VMEM(probe_modes.shape, F32),
            pltpu.SMEM((slot_count,), jnp.int32),
            pltpu.SemaphoreType.DMA((3 * tiles + 6,)),
            pltpu.SemaphoreType.DMA((slot_count,)),
        ]

    own_shape, right_shape, probe_shape = shape(2, rows, cols), shape(2, rows + PATCH, PATCH), shape(*probe_modes.shape)
    g_own, g_right, probe_1 = pl.pallas_call(
        upper_kernel,
        out_shape=(own_shape, right_shape, probe_shape),
        in_specs=[smem, smem] + [hbm] * 5,
        out_specs=(hbm,) * 3,
        scratch_shapes=scratch(rows),
        compiler_params=params,
        cost_estimate=pl.CostEstimate(flops=10**9, bytes_accessed=2**20, transcendentals=0),
        name="upper_slots",
    )(pos, count, object_field, right, photon_rows, probe_modes, waves)
    rim_shape = shape(2, PATCH, PATCH)
    g_own, g_right, g_first, g_rest, probe_2 = pl.pallas_call(
        functools.partial(lower_kernel, scale),
        out_shape=(own_shape, right_shape, rim_shape, shape(2, PATCH, cols - PATCH), probe_shape),
        in_specs=[smem] * 2 + [hbm] * 10,
        out_specs=(hbm,) * 5,
        scratch_shapes=scratch(2 * PATCH),
        input_output_aliases={9: 0, 10: 1},
        compiler_params=params,
        cost_estimate=pl.CostEstimate(flops=10**9, bytes_accessed=2**20, transcendentals=0),
        name="lower_slots",
    )(pos, count, object_field, right, below, corner, photon_rows, probe_modes, waves, g_own, g_right, probe_1)

    plane, depth = lax.axis_size(PLANE), lax.axis_size(DEPTH)
    left = lax.ppermute(g_right, COL, along)
    above_rest = lax.ppermute(g_rest, ROW, down)
    shares = lax.all_to_all(probe_2.reshape(plane, -1, PATCH), PLANE, 0, 0, tiled=True)
    share = jnp.sum(shares, axis=0)
    g_first = pl.pallas_call(
        corner_kernel,
        out_shape=rim_shape,
        in_specs=[hbm, hbm],
        out_specs=hbm,
        scratch_shapes=[
            pltpu.VMEM((2, PATCH, PATCH), F32),
            pltpu.VMEM((2, PATCH, PATCH), F32),
            pltpu.SemaphoreType.DMA((2,)),
        ],
        compiler_params=small,
        name="corner",
    )(g_first, left)
    share, g_first = lax.optimization_barrier((share, g_first))
    above_first = lax.ppermute(g_first, ROW, down)
    share = jnp.sum(everyone(share, DEPTH, depth), axis=0)
    share, above_first, above_rest = lax.optimization_barrier((share, above_first, above_rest))
    parts = everyone(share, PLANE, plane)

    object_gradient = pl.pallas_call(
        seam_kernel,
        out_shape=own_shape,
        in_specs=[hbm] * 4,
        out_specs=hbm,
        scratch_shapes=[
            pltpu.VMEM((2, PATCH, cols), F32),
            pltpu.VMEM((2, rows - PATCH, PATCH), F32),
            pltpu.VMEM((2, PATCH, cols), F32),
            pltpu.VMEM((2, rows, PATCH), F32),
            pltpu.SemaphoreType.DMA((5,)),
        ],
        input_output_aliases={0: 0},
        compiler_params=small,
        cost_estimate=pl.CostEstimate(flops=10**9, bytes_accessed=2**20, transcendentals=0),
        name="seams",
    )(g_own, above_first, above_rest, left)
    return (object_gradient, parts.reshape(probe_modes.shape))


def solution(mesh):
    fine = Mesh(mesh.devices.reshape(4, 4, 4, 2, 2), BOTH)
    in_specs = (
        P(None, ROW, COL),
        P(),
        P(ROW, COL, None, None, None),
        P(ROW, COL, None, None),
        P(ROW, COL),
    )
    out_specs = (P(None, ROW, COL), P())
    return jax.shard_map(body, mesh=fine, in_specs=in_specs, out_specs=out_specs, check_vma=False)
```

```python
import functools
import math

import jax
import jax.numpy as jnp
import numpy as np
from jax import lax
from jax.experimental import pallas as pl
from jax.experimental.pallas import tpu as pltpu
from jax.sharding import Mesh
from jax.sharding import PartitionSpec as P

F32 = jnp.float32
BF16 = jnp.bfloat16
PATCH = 128
BLOCK = 8
VMEM_LIMIT = 63 * 2**20
ROW = "z_hi"
COL = ("x", "y", "z_lo", "core")
BOTH = (ROW,) + COL
PLANE = ("x", "y", "core")
DEPTH = ("z_hi", "z_lo")


def waves_of(patch_len):
    index_range = np.arange(patch_len)
    product = (index_range[:, None] * index_range[None, :]) % patch_len
    angle = product.astype(np.float32) * np.float32(2.0 * math.pi / patch_len)
    pair = np.stack([np.cos(angle), np.sin(angle)]) / np.float32(math.sqrt(patch_len))
    return jnp.asarray(pair, F32)


def dot(a, b):
    return jnp.dot(a, b, preferred_element_type=F32)


def slot_block(at, slots, valids, pos, row_base, field, grad, photons, probe, probe_sum, plus_ref, minus_ref):
    n = len(slots)
    lane = lax.broadcasted_iota(jnp.int32, (PATCH, PATCH), 1)
    plus = plus_ref[...]
    minus = minus_ref[...]
    places, patches, waves = [], [], []
    for s in slots:
        top = pos[0, s] - row_base
        left = pos[1, s]
        tile = left // PATCH
        shift = left % PATCH
        back = (PATCH - shift) % PATCH
        keep = lane >= shift
        patch = []
        for k in range(2):
            a = field[tile, k, pl.ds(top, PATCH), :]
            b = field[tile + 1, k, pl.ds(top, PATCH), :]
            patch.append(pltpu.roll(jnp.where(keep, a, b), back, 1))
        places.append((top, tile, shift, keep))
        patches.append(patch)
        for m in range(2):
            pr = probe[0, m]
            pi = probe[1, m]
            wr = (pr * patch[0] - pi * patch[1]).astype(BF16)
            wi = (pr * patch[1] + pi * patch[0]).astype(BF16)
            waves.append(jnp.concatenate([wr, wi], axis=0))
    first = dot(plus, jnp.concatenate(waves, axis=1)).astype(BF16)
    cols = [slice(q * PATCH, (q + 1) * PATCH) for q in range(2 * n)]
    turned = [jnp.concatenate([first[:PATCH, q], first[PATCH:, q]], axis=1) for q in cols]
    far = dot(jnp.concatenate(turned, axis=0), minus)
    scaled = []
    for i in range(n):
        f0 = far[2 * i * PATCH:(2 * i + 1) * PATCH]
        f1 = far[(2 * i + 1) * PATCH:(2 * i + 2) * PATCH]
        power = f0 * f0 + f1 * f1
        intensity = power[:, :PATCH] + power[:, PATCH:]
        factor = (1.0 - photons[at[i]].astype(F32) / (intensity + 1.0)) * valids[i]
        for f in (f0, f1):
            re = (f[:, :PATCH] * factor).astype(BF16)
            im = (f[:, PATCH:] * factor).astype(BF16)
            scaled.append(jnp.concatenate([re, im], axis=1))
    back_pass = dot(jnp.concatenate(scaled, axis=0), plus).astype(BF16)
    unturned = [jnp.concatenate([back_pass[q, :PATCH], back_pass[q, PATCH:]], axis=0) for q in cols]
    exit_grad = dot(minus, jnp.concatenate(unturned, axis=1))
    for m in range(2):
        sum_re = sum_im = None
        for i in range(n):
            er = exit_grad[:PATCH, cols[2 * i + m]]
            ei = exit_grad[PATCH:, cols[2 * i + m]]
            o_re, o_im = patches[i]
            t_re = o_re * er + o_im * ei
            t_im = o_re * ei - o_im * er
            sum_re = t_re if sum_re is None else sum_re + t_re
            sum_im = t_im if sum_im is None else sum_im + t_im
        probe_sum[0, m] += sum_re
        probe_sum[1, m] += sum_im
    for i in range(n):
        g_re = g_im = None
        for m in range(2):
            er = exit_grad[:PATCH, cols[2 * i + m]]
            ei = exit_grad[PATCH:, cols[2 * i + m]]
            pr = probe[0, m]
            pi = probe[1, m]
            t_re = pr * er + pi * ei
            t_im = pr * ei - pi * er
            g_re = t_re if g_re is None else g_re + t_re
            g_im = t_im if g_im is None else g_im + t_im
        top, tile, shift, keep = places[i]
        for k, g in ((0, g_re), (1, g_im)):
            g = pltpu.roll(g, shift, 1)
            grad[tile, k, pl.ds(top, PATCH), :] += jnp.where(keep, g, 0.0)
            grad[tile + 1, k, pl.ds(top, PATCH), :] += jnp.where(keep, 0.0, g)


def fill_tables(waves, plus_ref, minus_ref):
    c = waves[0].astype(BF16)
    s = waves[1].astype(BF16)
    plus_ref[:PATCH, :PATCH] = c
    plus_ref[:PATCH, PATCH:] = s
    plus_ref[PATCH:, :PATCH] = -s
    plus_ref[PATCH:, PATCH:] = c
    minus_ref[:PATCH, :PATCH] = c
    minus_ref[:PATCH, PATCH:] = -s
    minus_ref[PATCH:, :PATCH] = s
    minus_ref[PATCH:, PATCH:] = c


def list_slots(wanted, pos, count, listed, photons, photon_buf, photon_sems):
    def list_step(s, found):
        chosen = wanted(pos[0, s])

        @pl.when(chosen)
        def _():
            listed[found] = s
            pltpu.make_async_copy(photons.at[s], photon_buf.at[found], photon_sems.at[found]).start()

        return found + chosen.astype(jnp.int32)

    return lax.fori_loop(0, count, list_step, jnp.int32(0))


def run_slots(found, pos, row_base, listed, field, grad, photons, photon_buf, photon_sems, probe, probe_sum,
              plus_ref, minus_ref):
    def step(k, carry, first=0, width=BLOCK):
        places = [first + k * width + i for i in range(width)]
        at = [jnp.minimum(p, found - 1) for p in places]
        slots = [listed[a] for a in at]
        valids = [jnp.where(p < found, 1.0, 0.0).astype(F32) for p in places]
        for p, a, s in zip(places, at, slots):
            @pl.when(p < found)
            def _(a=a, s=s):
                pltpu.make_async_copy(photons.at[s], photon_buf.at[a], photon_sems.at[a]).wait()

        slot_block(at, slots, valids, pos, row_base, field, grad, photon_buf, probe, probe_sum, plus_ref, minus_ref)
        return carry

    rest = found % BLOCK
    small = (rest > 0) & (rest <= BLOCK // 2)
    blocks = found // BLOCK + ((rest > 0) & jnp.logical_not(small)).astype(jnp.int32)
    lax.fori_loop(0, blocks, step, 0)

    @pl.when(small)
    def _():
        step(0, 0, blocks * BLOCK, BLOCK // 2)


def copies_of(pairs, sems):
    return [pltpu.make_async_copy(a, b, sems.at[i]) for i, (a, b) in enumerate(pairs)]


def start_all(copies):
    for c in copies:
        c.start()


def wait_all(copies):
    for c in copies:
        c.wait()


def by_tiles(array, tiles):
    return [array.at[:, :, pl.ds(t * PATCH, PATCH)] for t in range(tiles)]


def right_rim_kernel(own, right, right_buf, sems):
    load = pltpu.make_async_copy(own.at[:, :, pl.ds(0, PATCH)], right_buf, sems.at[0])
    load.start()
    load.wait()
    store = pltpu.make_async_copy(right_buf, right, sems.at[0])
    store.start()
    store.wait()


def below_rim_kernel(own, after, below, corner, below_buf, sems):
    rim = pl.ds(0, PATCH)
    load = pltpu.make_async_copy(own.at[:, rim, :], below_buf, sems.at[0])
    load.start()
    load.wait()
    stores = copies_of([(below_buf, below), (below_buf.at[:, :, rim], corner)], sems)
    start_all(stores)
    wait_all(stores)


def upper_kernel(pos, count, own, right, photons, probe_in, waves_in, g_own, g_right, probe_out,
                 field, grad, photon_buf, probe, waves, plus_ref, minus_ref, probe_sum, listed, sems, photon_sems):
    rows, cols = own.shape[1], own.shape[2]
    tiles = cols // PATCH
    loads = copies_of(
        [(waves_in, waves), (probe_in, probe)]
        + [(a, field.at[t]) for t, a in enumerate(by_tiles(own, tiles))]
        + [(right, field.at[tiles])],
        sems,
    )
    start_all(loads)
    found = list_slots(lambda top: top <= rows - PATCH, pos, count[0], listed, photons, photon_buf, photon_sems)
    grad[...] = jnp.zeros(grad.shape, F32)
    probe_sum[...] = jnp.zeros(probe_sum.shape, F32)
    loads[0].wait()
    fill_tables(waves, plus_ref, minus_ref)
    wait_all(loads[1:])
    run_slots(found, pos, 0, listed, field, grad, photons, photon_buf, photon_sems, probe, probe_sum,
              plus_ref, minus_ref)
    stores = copies_of(
        [(probe_sum, probe_out)]
        + [(grad.at[t], a) for t, a in enumerate(by_tiles(g_own, tiles))]
        + [(grad.at[tiles], g_right)],
        sems,
    )
    start_all(stores)
    wait_all(stores)


def lower_kernel(scale, pos, count, own, right, below, corner, photons, probe_in, waves_in, own_in, right_in, sum_in,
                 g_own, g_right, g_below, g_corner, probe_out,
                 field, grad, photon_buf, probe, waves, plus_ref, minus_ref, probe_sum, listed, sems, photon_sems):
    rows, cols = own.shape[1], own.shape[2]
    tiles = cols // PATCH
    base = rows - PATCH
    last, upper, lower = pl.ds(base, PATCH), pl.ds(0, PATCH), pl.ds(PATCH, PATCH)

    def last_rows(array):
        return [array.at[:, last, pl.ds(t * PATCH, PATCH)] for t in range(tiles)]

    loads = copies_of(
        [(waves_in, waves), (probe_in, probe), (sum_in, probe_sum)]
        + [(a, field.at[t, :, upper, :]) for t, a in enumerate(last_rows(own) + [right.at[:, last, :]])]
        + [(a, field.at[t, :, lower, :]) for t, a in enumerate(by_tiles(below, tiles) + [corner])]
        + [(a, grad.at[t, :, upper, :]) for t, a in enumerate(last_rows(own_in) + [right_in.at[:, last, :]])],
        sems,
    )
    start_all(loads)
    found = list_slots(lambda top: top > base, pos, count[0], listed, photons, photon_buf, photon_sems)
    for t in range(tiles + 1):
        grad[t, :, lower, :] = jnp.zeros((2, PATCH, PATCH), F32)
    loads[0].wait()
    fill_tables(waves, plus_ref, minus_ref)
    wait_all(loads[1:])
    run_slots(found, pos, base, listed, field, grad, photons, photon_buf, photon_sems, probe, probe_sum,
              plus_ref, minus_ref)
    probe_sum[...] = probe_sum[...] * scale
    stores = copies_of(
        [(probe_sum, probe_out)]
        + [(grad.at[t, :, lower, :], a) for t, a in enumerate(by_tiles(g_below, tiles) + [g_corner])]
        + [(grad.at[t, :, upper, :], a) for t, a in enumerate(last_rows(g_own) + [g_right.at[:, last, :]])],
        sems,
    )
    start_all(stores)
    wait_all(stores)


def seam_kernel(grad_in, above, left, corner, grad, top_buf, left_buf, above_buf, beside_buf, corner_buf, sems):
    rows, cols = grad.shape[1], grad.shape[2]
    rest = rows - PATCH
    top_rim = grad.at[:, pl.ds(0, PATCH), :]
    left_rim = grad.at[:, pl.ds(PATCH, rest), pl.ds(0, PATCH)]
    loads = copies_of(
        [(top_rim, top_buf), (left_rim, left_buf), (above, above_buf), (left, beside_buf), (corner, corner_buf)],
        sems,
    )
    start_all(loads)
    wait_all(loads)
    top_buf[:, :, PATCH:] += above_buf[:, :, PATCH:]
    top_buf[:, :, :PATCH] += above_buf[:, :, :PATCH] + (beside_buf[:, :PATCH, :] + corner_buf[...])
    left_buf[...] += beside_buf[:, PATCH:, :]
    stores = copies_of([(top_buf, top_rim), (left_buf, left_rim)], sems)
    start_all(stores)
    wait_all(stores)


def shape(*dims):
    return jax.ShapeDtypeStruct(dims, F32)


def everyone(value, axes, count):
    sent = jnp.broadcast_to(value[None], (count,) + value.shape)
    return lax.all_to_all(sent, axes, 0, 0, tiled=True)


def body(object_field, probe_modes, photons, positions, counts):
    rows, cols = object_field.shape[1], object_field.shape[2]
    slot_count = photons.shape[2]
    tiles = cols // PATCH
    n_row, n_col = lax.axis_size(ROW), lax.axis_size(COL)
    pos = positions[0, 0].T
    count = counts[0]
    photon_rows = photons[0, 0]
    waves = waves_of(PATCH)
    scale = 1.0 / math.sqrt(n_row * n_col * slot_count)
    down = [(i, i + 1) for i in range(n_row - 1)]
    along = [(i, i + 1) for i in range(n_col - 1)]
    up, back = ([(j, i) for i, j in pairs] for pairs in (down, along))
    diagonal = [
        (a * n_col + b, (a + 1) * n_col + b + 1) for a in range(n_row - 1) for b in range(n_col - 1)
    ]
    diagonal_back = [(j, i) for i, j in diagonal]
    smem = pl.BlockSpec(memory_space=pltpu.SMEM)
    hbm = pl.BlockSpec(memory_space=pl.ANY)
    params = pltpu.CompilerParams(vmem_limit_bytes=VMEM_LIMIT)
    small = pltpu.CompilerParams(vmem_limit_bytes=8 * 2**20)

    right = pl.pallas_call(
        right_rim_kernel,
        out_shape=shape(2, rows, PATCH),
        in_specs=[hbm],
        out_specs=hbm,
        scratch_shapes=[pltpu.VMEM((2, rows, PATCH), F32), pltpu.SemaphoreType.DMA((1,))],
        compiler_params=params,
        name="right_rim",
    )(object_field)
    below, corner = pl.pallas_call(
        below_rim_kernel,
        out_shape=(shape(2, PATCH, cols), shape(2, PATCH, PATCH)),
        in_specs=[hbm, hbm],
        out_specs=(hbm,) * 2,
        scratch_shapes=[pltpu.VMEM((2, PATCH, cols), F32), pltpu.SemaphoreType.DMA((2,))],
        compiler_params=params,
        name="below_rim",
    )(object_field, right)
    below = lax.ppermute(below, ROW, up)
    right = lax.ppermute(right, COL, back)
    corner = lax.ppermute(corner, BOTH, diagonal_back)

    def scratch(height):
        return [
            pltpu.VMEM((tiles + 1, 2, height, PATCH), F32),
            pltpu.VMEM((tiles + 1, 2, height, PATCH), F32),
            pltpu.VMEM(photon_rows.shape, BF16),
            pltpu.VMEM(probe_modes.shape, F32),
            pltpu.VMEM(waves.shape, F32),
            pltpu.VMEM((2 * PATCH, 2 * PATCH), BF16),
            pltpu.VMEM((2 * PATCH, 2 * PATCH), BF16),
            pltpu.VMEM(probe_modes.shape, F32),
            pltpu.SMEM((slot_count,), jnp.int32),
            pltpu.SemaphoreType.DMA((3 * tiles + 6,)),
            pltpu.SemaphoreType.DMA((slot_count,)),
        ]

    own_shape, right_shape, probe_shape = shape(2, rows, cols), shape(2, rows, PATCH), shape(*probe_modes.shape)
    g_own, g_right, probe_1 = pl.pallas_call(
        upper_kernel,
        out_shape=(own_shape, right_shape, probe_shape),
        in_specs=[smem, smem] + [hbm] * 5,
        out_specs=(hbm,) * 3,
        scratch_shapes=scratch(rows),
        compiler_params=params,
        cost_estimate=pl.CostEstimate(flops=10**9, bytes_accessed=2**20, transcendentals=0),
        name="upper_slots",
    )(pos, count, object_field, right, photon_rows, probe_modes, waves)
    rim_shape = shape(2, PATCH, PATCH)
    g_own, g_right, g_below, g_corner, probe_2 = pl.pallas_call(
        functools.partial(lower_kernel, scale),
        out_shape=(own_shape, right_shape, shape(2, PATCH, cols), rim_shape, probe_shape),
        in_specs=[smem] * 2 + [hbm] * 10,
        out_specs=(hbm,) * 5,
        scratch_shapes=scratch(2 * PATCH),
        input_output_aliases={9: 0, 10: 1},
        compiler_params=params,
        cost_estimate=pl.CostEstimate(flops=10**9, bytes_accessed=2**20, transcendentals=0),
        name="lower_slots",
    )(pos, count, object_field, right, below, corner, photon_rows, probe_modes, waves, g_own, g_right, probe_1)

    plane, depth = lax.axis_size(PLANE), lax.axis_size(DEPTH)
    above = lax.ppermute(g_below, ROW, down)
    shares = lax.all_to_all(probe_2.reshape(plane, -1, PATCH), PLANE, 0, 0, tiled=True)
    share = jnp.sum(shares, axis=0)
    share, g_corner = lax.optimization_barrier((share, g_corner))
    from_corner = lax.ppermute(g_corner, BOTH, diagonal)
    share = jnp.sum(everyone(share, DEPTH, depth), axis=0)
    share, above, from_corner, g_right = lax.optimization_barrier((share, above, from_corner, g_right))
    left = lax.ppermute(g_right, COL, along)
    parts = everyone(share, PLANE, plane)

    object_gradient = pl.pallas_call(
        seam_kernel,
        out_shape=own_shape,
        in_specs=[hbm] * 4,
        out_specs=hbm,
        scratch_shapes=[
            pltpu.VMEM((2, PATCH, cols), F32),
            pltpu.VMEM((2, rows - PATCH, PATCH), F32),
            pltpu.VMEM((2, PATCH, cols), F32),
            pltpu.VMEM((2, rows, PATCH), F32),
            pltpu.VMEM((2, PATCH, PATCH), F32),
            pltpu.SemaphoreType.DMA((5,)),
        ],
        input_output_aliases={0: 0},
        compiler_params=small,
        cost_estimate=pl.CostEstimate(flops=10**9, bytes_accessed=2**20, transcendentals=0),
        name="seams",
    )(g_own, above, left, from_corner)
    return (object_gradient, parts.reshape(probe_modes.shape))


def solution(mesh):
    fine = Mesh(mesh.devices.reshape(4, 4, 4, 2, 2), BOTH)
    in_specs = (
        P(None, ROW, COL),
        P(),
        P(ROW, COL, None, None, None),
        P(ROW, COL, None, None),
        P(ROW, COL),
    )
    out_specs = (P(None, ROW, COL), P())
    return jax.shard_map(body, mesh=fine, in_specs=in_specs, out_specs=out_specs, check_vma=False)
```

```python
import functools
import math

import jax
import jax.numpy as jnp
import numpy as np
from jax import lax
from jax.experimental import pallas as pl
from jax.experimental.pallas import tpu as pltpu
from jax.sharding import Mesh
from jax.sharding import PartitionSpec as P

F32 = jnp.float32
BF16 = jnp.bfloat16
PATCH = 128
BLOCK = 8
VMEM_LIMIT = 63 * 2**20
ROW = "z_hi"
COL = ("x", "y", "z_lo", "core")
BOTH = (ROW,) + COL
PLANE = ("x", "y", "core")
DEPTH = ("z_hi", "z_lo")


def waves_of(patch_len):
    index_range = np.arange(patch_len)
    product = (index_range[:, None] * index_range[None, :]) % patch_len
    angle = product.astype(np.float32) * np.float32(2.0 * math.pi / patch_len)
    pair = np.stack([np.cos(angle), np.sin(angle)]) / np.float32(math.sqrt(patch_len))
    return jnp.asarray(pair, F32)


def dot(a, b):
    return jnp.dot(a, b, preferred_element_type=F32)


def slot_block(at, slots, valids, pos, row_base, field, grad, photons, probe, probe_sum, plus_ref, minus_ref):
    n = len(slots)
    lane = lax.broadcasted_iota(jnp.int32, (PATCH, PATCH), 1)
    plus = plus_ref[...]
    minus = minus_ref[...]
    places, patches, waves = [], [], []
    for s in slots:
        top = pos[0, s] - row_base
        left = pos[1, s]
        tile = left // PATCH
        shift = left % PATCH
        back = (PATCH - shift) % PATCH
        keep = lane >= shift
        patch = []
        for k in range(2):
            a = field[tile, k, pl.ds(top, PATCH), :]
            b = field[tile + 1, k, pl.ds(top, PATCH), :]
            patch.append(pltpu.roll(jnp.where(keep, a, b), back, 1))
        places.append((top, tile, shift, keep))
        patches.append(patch)
        for m in range(2):
            pr = probe[0, m]
            pi = probe[1, m]
            wr = (pr * patch[0] - pi * patch[1]).astype(BF16)
            wi = (pr * patch[1] + pi * patch[0]).astype(BF16)
            waves.append(jnp.concatenate([wr, wi], axis=0))
    first = dot(plus, jnp.concatenate(waves, axis=1)).astype(BF16)
    cols = [slice(q * PATCH, (q + 1) * PATCH) for q in range(2 * n)]
    turned = [jnp.concatenate([first[:PATCH, q], first[PATCH:, q]], axis=1) for q in cols]
    far = dot(jnp.concatenate(turned, axis=0), minus)
    scaled = []
    for i in range(n):
        f0 = far[2 * i * PATCH:(2 * i + 1) * PATCH]
        f1 = far[(2 * i + 1) * PATCH:(2 * i + 2) * PATCH]
        power = f0 * f0 + f1 * f1
        intensity = power[:, :PATCH] + power[:, PATCH:]
        factor = (1.0 - photons[at[i]].astype(F32) / (intensity + 1.0)) * valids[i]
        for f in (f0, f1):
            re = (f[:, :PATCH] * factor).astype(BF16)
            im = (f[:, PATCH:] * factor).astype(BF16)
            scaled.append(jnp.concatenate([re, im], axis=1))
    back_pass = dot(jnp.concatenate(scaled, axis=0), plus).astype(BF16)
    unturned = [jnp.concatenate([back_pass[q, :PATCH], back_pass[q, PATCH:]], axis=0) for q in cols]
    exit_grad = dot(minus, jnp.concatenate(unturned, axis=1))
    for m in range(2):
        sum_re = sum_im = None
        for i in range(n):
            er = exit_grad[:PATCH, cols[2 * i + m]]
            ei = exit_grad[PATCH:, cols[2 * i + m]]
            o_re, o_im = patches[i]
            t_re = o_re * er + o_im * ei
            t_im = o_re * ei - o_im * er
            sum_re = t_re if sum_re is None else sum_re + t_re
            sum_im = t_im if sum_im is None else sum_im + t_im
        probe_sum[0, m] += sum_re
        probe_sum[1, m] += sum_im
    for i in range(n):
        g_re = g_im = None
        for m in range(2):
            er = exit_grad[:PATCH, cols[2 * i + m]]
            ei = exit_grad[PATCH:, cols[2 * i + m]]
            pr = probe[0, m]
            pi = probe[1, m]
            t_re = pr * er + pi * ei
            t_im = pr * ei - pi * er
            g_re = t_re if g_re is None else g_re + t_re
            g_im = t_im if g_im is None else g_im + t_im
        top, tile, shift, keep = places[i]
        for k, g in ((0, g_re), (1, g_im)):
            g = pltpu.roll(g, shift, 1)
            grad[tile, k, pl.ds(top, PATCH), :] += jnp.where(keep, g, 0.0)
            grad[tile + 1, k, pl.ds(top, PATCH), :] += jnp.where(keep, 0.0, g)


def fill_tables(waves, plus_ref, minus_ref):
    c = waves[0].astype(BF16)
    s = waves[1].astype(BF16)
    plus_ref[:PATCH, :PATCH] = c
    plus_ref[:PATCH, PATCH:] = s
    plus_ref[PATCH:, :PATCH] = -s
    plus_ref[PATCH:, PATCH:] = c
    minus_ref[:PATCH, :PATCH] = c
    minus_ref[:PATCH, PATCH:] = -s
    minus_ref[PATCH:, :PATCH] = s
    minus_ref[PATCH:, PATCH:] = c


def list_slots(wanted, pos, count, listed, photons, photon_buf, photon_sems):
    def list_step(s, found):
        chosen = wanted(pos[0, s])

        @pl.when(chosen)
        def _():
            listed[found] = s
            pltpu.make_async_copy(photons.at[s], photon_buf.at[found], photon_sems.at[found]).start()

        return found + chosen.astype(jnp.int32)

    return lax.fori_loop(0, count, list_step, jnp.int32(0))


def run_slots(found, pos, row_base, listed, field, grad, photons, photon_buf, photon_sems, probe, probe_sum,
              plus_ref, minus_ref):
    def step(k, carry, first=0, width=BLOCK):
        places = [first + k * width + i for i in range(width)]
        at = [jnp.minimum(p, found - 1) for p in places]
        slots = [listed[a] for a in at]
        valids = [jnp.where(p < found, 1.0, 0.0).astype(F32) for p in places]
        for p, a, s in zip(places, at, slots):
            @pl.when(p < found)
            def _(a=a, s=s):
                pltpu.make_async_copy(photons.at[s], photon_buf.at[a], photon_sems.at[a]).wait()

        slot_block(at, slots, valids, pos, row_base, field, grad, photon_buf, probe, probe_sum, plus_ref, minus_ref)
        return carry

    rest = found % BLOCK
    small = (rest > 0) & (rest <= BLOCK // 2)
    blocks = found // BLOCK + ((rest > 0) & jnp.logical_not(small)).astype(jnp.int32)
    lax.fori_loop(0, blocks, step, 0)

    @pl.when(small)
    def _():
        step(0, 0, blocks * BLOCK, BLOCK // 2)


def copies_of(pairs, sems):
    return [pltpu.make_async_copy(a, b, sems.at[i]) for i, (a, b) in enumerate(pairs)]


def start_all(copies):
    for c in copies:
        c.start()


def wait_all(copies):
    for c in copies:
        c.wait()


def by_tiles(array, tiles):
    return [array.at[:, :, pl.ds(t * PATCH, PATCH)] for t in range(tiles)]


def right_rim_kernel(own, right, right_buf, sems):
    load = pltpu.make_async_copy(own.at[:, :, pl.ds(0, PATCH)], right_buf, sems.at[0])
    load.start()
    load.wait()
    store = pltpu.make_async_copy(right_buf, right, sems.at[0])
    store.start()
    store.wait()


def below_rim_kernel(own, after, below, corner, below_buf, sems):
    rim = pl.ds(0, PATCH)
    load = pltpu.make_async_copy(own.at[:, rim, :], below_buf, sems.at[0])
    load.start()
    load.wait()
    stores = copies_of([(below_buf, below), (below_buf.at[:, :, rim], corner)], sems)
    start_all(stores)
    wait_all(stores)


def upper_kernel(pos, count, own, right, photons, probe_in, waves_in, g_own, g_right, probe_out,
                 field, grad, photon_buf, probe, waves, plus_ref, minus_ref, probe_sum, listed, sems, photon_sems):
    rows, cols = own.shape[1], own.shape[2]
    tiles = cols // PATCH
    loads = copies_of(
        [(waves_in, waves), (probe_in, probe)]
        + [(a, field.at[t]) for t, a in enumerate(by_tiles(own, tiles))]
        + [(right, field.at[tiles])],
        sems,
    )
    start_all(loads)
    found = list_slots(lambda top: top <= rows - PATCH, pos, count[0], listed, photons, photon_buf, photon_sems)
    grad[...] = jnp.zeros(grad.shape, F32)
    probe_sum[...] = jnp.zeros(probe_sum.shape, F32)
    loads[0].wait()
    fill_tables(waves, plus_ref, minus_ref)
    wait_all(loads[1:])
    run_slots(found, pos, 0, listed, field, grad, photons, photon_buf, photon_sems, probe, probe_sum,
              plus_ref, minus_ref)
    stores = copies_of(
        [(probe_sum, probe_out)]
        + [(grad.at[t], a) for t, a in enumerate(by_tiles(g_own, tiles))]
        + [(grad.at[tiles], g_right)],
        sems,
    )
    start_all(stores)
    wait_all(stores)


def lower_kernel(scale, pos, count, own, right, below, corner, photons, probe_in, waves_in, own_in, right_in, sum_in,
                 g_own, g_right, g_below, g_corner, probe_out,
                 field, grad, photon_buf, probe, waves, plus_ref, minus_ref, probe_sum, listed, sems, photon_sems):
    rows, cols = own.shape[1], own.shape[2]
    tiles = cols // PATCH
    base = rows - PATCH
    last, upper, lower = pl.ds(base, PATCH), pl.ds(0, PATCH), pl.ds(PATCH, PATCH)

    def last_rows(array):
        return [array.at[:, last, pl.ds(t * PATCH, PATCH)] for t in range(tiles)]

    loads = copies_of(
        [(waves_in, waves), (probe_in, probe), (sum_in, probe_sum)]
        + [(a, field.at[t, :, upper, :]) for t, a in enumerate(last_rows(own) + [right.at[:, last, :]])]
        + [(a, field.at[t, :, lower, :]) for t, a in enumerate(by_tiles(below, tiles) + [corner])]
        + [(a, grad.at[t, :, upper, :]) for t, a in enumerate(last_rows(own_in) + [right_in.at[:, last, :]])],
        sems,
    )
    start_all(loads)
    found = list_slots(lambda top: top > base, pos, count[0], listed, photons, photon_buf, photon_sems)
    for t in range(tiles + 1):
        grad[t, :, lower, :] = jnp.zeros((2, PATCH, PATCH), F32)
    loads[0].wait()
    fill_tables(waves, plus_ref, minus_ref)
    wait_all(loads[1:])
    run_slots(found, pos, base, listed, field, grad, photons, photon_buf, photon_sems, probe, probe_sum,
              plus_ref, minus_ref)
    probe_sum[...] = probe_sum[...] * scale
    stores = copies_of(
        [(probe_sum, probe_out)]
        + [(grad.at[t, :, lower, :], a) for t, a in enumerate(by_tiles(g_below, tiles) + [g_corner])]
        + [(grad.at[t, :, upper, :], a) for t, a in enumerate(last_rows(g_own) + [g_right.at[:, last, :]])],
        sems,
    )
    start_all(stores)
    wait_all(stores)


def seam_kernel(grad_in, above, left, corner, grad, top_buf, left_buf, above_buf, beside_buf, corner_buf, sems):
    rows, cols = grad.shape[1], grad.shape[2]
    rest = rows - PATCH
    top_rim = grad.at[:, pl.ds(0, PATCH), :]
    left_rim = grad.at[:, pl.ds(PATCH, rest), pl.ds(0, PATCH)]
    loads = copies_of(
        [(top_rim, top_buf), (left_rim, left_buf), (above, above_buf), (left, beside_buf), (corner, corner_buf)],
        sems,
    )
    start_all(loads)
    wait_all(loads)
    top_buf[:, :, PATCH:] += above_buf[:, :, PATCH:]
    top_buf[:, :, :PATCH] += above_buf[:, :, :PATCH] + (beside_buf[:, :PATCH, :] + corner_buf[...])
    left_buf[...] += beside_buf[:, PATCH:, :]
    stores = copies_of([(top_buf, top_rim), (left_buf, left_rim)], sems)
    start_all(stores)
    wait_all(stores)


def shape(*dims):
    return jax.ShapeDtypeStruct(dims, F32)


def everyone(value, axes, count):
    sent = jnp.broadcast_to(value[None], (count,) + value.shape)
    return lax.all_to_all(sent, axes, 0, 0, tiled=True)


def body(object_field, probe_modes, photons, positions, counts):
    rows, cols = object_field.shape[1], object_field.shape[2]
    slot_count = photons.shape[2]
    tiles = cols // PATCH
    n_row, n_col = lax.axis_size(ROW), lax.axis_size(COL)
    pos = positions[0, 0].T
    count = counts[0]
    photon_rows = photons[0, 0]
    waves = waves_of(PATCH)
    scale = 1.0 / math.sqrt(n_row * n_col * slot_count)
    down = [(i, i + 1) for i in range(n_row - 1)]
    along = [(i, i + 1) for i in range(n_col - 1)]
    up, back = ([(j, i) for i, j in pairs] for pairs in (down, along))
    diagonal = [
        (a * n_col + b, (a + 1) * n_col + b + 1) for a in range(n_row - 1) for b in range(n_col - 1)
    ]
    diagonal_back = [(j, i) for i, j in diagonal]
    smem = pl.BlockSpec(memory_space=pltpu.SMEM)
    hbm = pl.BlockSpec(memory_space=pl.ANY)
    params = pltpu.CompilerParams(vmem_limit_bytes=VMEM_LIMIT)
    small = pltpu.CompilerParams(vmem_limit_bytes=8 * 2**20)

    right = pl.pallas_call(
        right_rim_kernel,
        out_shape=shape(2, rows, PATCH),
        in_specs=[hbm],
        out_specs=hbm,
        scratch_shapes=[pltpu.VMEM((2, rows, PATCH), F32), pltpu.SemaphoreType.DMA((1,))],
        compiler_params=params,
        name="right_rim",
    )(object_field)
    below, corner = pl.pallas_call(
        below_rim_kernel,
        out_shape=(shape(2, PATCH, cols), shape(2, PATCH, PATCH)),
        in_specs=[hbm, hbm],
        out_specs=(hbm,) * 2,
        scratch_shapes=[pltpu.VMEM((2, PATCH, cols), F32), pltpu.SemaphoreType.DMA((2,))],
        compiler_params=params,
        name="below_rim",
    )(object_field, right)
    below = lax.ppermute(below, ROW, up)
    right = lax.ppermute(right, COL, back)
    corner = lax.ppermute(corner, BOTH, diagonal_back)

    def scratch(height):
        return [
            pltpu.VMEM((tiles + 1, 2, height, PATCH), F32),
            pltpu.VMEM((tiles + 1, 2, height, PATCH), F32),
            pltpu.VMEM(photon_rows.shape, BF16),
            pltpu.VMEM(probe_modes.shape, F32),
            pltpu.VMEM(waves.shape, F32),
            pltpu.VMEM((2 * PATCH, 2 * PATCH), BF16),
            pltpu.VMEM((2 * PATCH, 2 * PATCH), BF16),
            pltpu.VMEM(probe_modes.shape, F32),
            pltpu.SMEM((slot_count,), jnp.int32),
            pltpu.SemaphoreType.DMA((3 * tiles + 6,)),
            pltpu.SemaphoreType.DMA((slot_count,)),
        ]

    own_shape, right_shape, probe_shape = shape(2, rows, cols), shape(2, rows, PATCH), shape(*probe_modes.shape)
    g_own, g_right, probe_1 = pl.pallas_call(
        upper_kernel,
        out_shape=(own_shape, right_shape, probe_shape),
        in_specs=[smem, smem] + [hbm] * 5,
        out_specs=(hbm,) * 3,
        scratch_shapes=scratch(rows),
        compiler_params=params,
        cost_estimate=pl.CostEstimate(flops=10**9, bytes_accessed=2**20, transcendentals=0),
        name="upper_slots",
    )(pos, count, object_field, right, photon_rows, probe_modes, waves)
    rim_shape = shape(2, PATCH, PATCH)
    g_own, g_right, g_below, g_corner, probe_2 = pl.pallas_call(
        functools.partial(lower_kernel, scale),
        out_shape=(own_shape, right_shape, shape(2, PATCH, cols), rim_shape, probe_shape),
        in_specs=[smem] * 2 + [hbm] * 10,
        out_specs=(hbm,) * 5,
        scratch_shapes=scratch(2 * PATCH),
        input_output_aliases={9: 0, 10: 1},
        compiler_params=params,
        cost_estimate=pl.CostEstimate(flops=10**9, bytes_accessed=2**20, transcendentals=0),
        name="lower_slots",
    )(pos, count, object_field, right, below, corner, photon_rows, probe_modes, waves, g_own, g_right, probe_1)

    plane, depth = lax.axis_size(PLANE), lax.axis_size(DEPTH)
    above = lax.ppermute(g_below, ROW, down)
    shares = lax.all_to_all(probe_2.reshape(plane, -1, PATCH), PLANE, 0, 0, tiled=True)
    share = jnp.sum(shares, axis=0)
    share = jnp.sum(everyone(share, DEPTH, depth), axis=0)
    share, above, g_right, g_corner = lax.optimization_barrier((share, above, g_right, g_corner))
    left = lax.ppermute(g_right, COL, along)
    from_corner = lax.ppermute(g_corner, BOTH, diagonal)
    parts = everyone(share, PLANE, plane)

    object_gradient = pl.pallas_call(
        seam_kernel,
        out_shape=own_shape,
        in_specs=[hbm] * 4,
        out_specs=hbm,
        scratch_shapes=[
            pltpu.VMEM((2, PATCH, cols), F32),
            pltpu.VMEM((2, rows - PATCH, PATCH), F32),
            pltpu.VMEM((2, PATCH, cols), F32),
            pltpu.VMEM((2, rows, PATCH), F32),
            pltpu.VMEM((2, PATCH, PATCH), F32),
            pltpu.SemaphoreType.DMA((5,)),
        ],
        input_output_aliases={0: 0},
        compiler_params=small,
        cost_estimate=pl.CostEstimate(flops=10**9, bytes_accessed=2**20, transcendentals=0),
        name="seams",
    )(g_own, above, left, from_corner)
    return (object_gradient, parts.reshape(probe_modes.shape))


def solution(mesh):
    fine = Mesh(mesh.devices.reshape(4, 4, 4, 2, 2), BOTH)
    in_specs = (
        P(None, ROW, COL),
        P(),
        P(ROW, COL, None, None, None),
        P(ROW, COL, None, None),
        P(ROW, COL),
    )
    out_specs = (P(None, ROW, COL), P())
    return jax.shard_map(body, mesh=fine, in_specs=in_specs, out_specs=out_specs, check_vma=False)
```

```python
import functools
import math

import jax
import jax.numpy as jnp
import numpy as np
from jax import lax
from jax.experimental import pallas as pl
from jax.experimental.pallas import tpu as pltpu
from jax.sharding import Mesh
from jax.sharding import PartitionSpec as P

F32 = jnp.float32
BF16 = jnp.bfloat16
PATCH = 128
BLOCK = 8
VMEM_LIMIT = 63 * 2**20
ROW = "z_hi"
COL = ("x", "y", "z_lo", "core")
BOTH = (ROW,) + COL
PLANE = ("x", "y", "core")
DEPTH = ("z_hi", "z_lo")


def waves_of(patch_len):
    index_range = np.arange(patch_len)
    product = (index_range[:, None] * index_range[None, :]) % patch_len
    angle = product.astype(np.float32) * np.float32(2.0 * math.pi / patch_len)
    pair = np.stack([np.cos(angle), np.sin(angle)]) / np.float32(math.sqrt(patch_len))
    return jnp.asarray(pair, F32)


def dot(a, b):
    return jnp.dot(a, b, preferred_element_type=F32)


def slot_block(at, slots, valids, pos, row_base, field, grad, photons, probe, probe_sum, plus_ref, minus_ref):
    n = len(slots)
    lane = lax.broadcasted_iota(jnp.int32, (PATCH, PATCH), 1)
    plus = plus_ref[...]
    minus = minus_ref[...]
    places, patches, waves = [], [], []
    for s in slots:
        top = pos[0, s] - row_base
        left = pos[1, s]
        tile = left // PATCH
        shift = left % PATCH
        back = (PATCH - shift) % PATCH
        keep = lane >= shift
        patch = []
        for k in range(2):
            a = field[tile, k, pl.ds(top, PATCH), :]
            b = field[tile + 1, k, pl.ds(top, PATCH), :]
            patch.append(pltpu.roll(jnp.where(keep, a, b), back, 1))
        places.append((top, tile, shift, keep))
        patches.append(patch)
        for m in range(2):
            pr = probe[0, m]
            pi = probe[1, m]
            wr = (pr * patch[0] - pi * patch[1]).astype(BF16)
            wi = (pr * patch[1] + pi * patch[0]).astype(BF16)
            waves.append(jnp.concatenate([wr, wi], axis=0))
    first = dot(plus, jnp.concatenate(waves, axis=1)).astype(BF16)
    cols = [slice(q * PATCH, (q + 1) * PATCH) for q in range(2 * n)]
    turned = [jnp.concatenate([first[:PATCH, q], first[PATCH:, q]], axis=1) for q in cols]
    far = dot(jnp.concatenate(turned, axis=0), minus)
    scaled = []
    for i in range(n):
        f0 = far[2 * i * PATCH:(2 * i + 1) * PATCH]
        f1 = far[(2 * i + 1) * PATCH:(2 * i + 2) * PATCH]
        power = f0 * f0 + f1 * f1
        intensity = power[:, :PATCH] + power[:, PATCH:]
        factor = (1.0 - photons[at[i]].astype(F32) / (intensity + 1.0)) * valids[i]
        for f in (f0, f1):
            re = (f[:, :PATCH] * factor).astype(BF16)
            im = (f[:, PATCH:] * factor).astype(BF16)
            scaled.append(jnp.concatenate([re, im], axis=1))
    back_pass = dot(jnp.concatenate(scaled, axis=0), plus).astype(BF16)
    unturned = [jnp.concatenate([back_pass[q, :PATCH], back_pass[q, PATCH:]], axis=0) for q in cols]
    exit_grad = dot(minus, jnp.concatenate(unturned, axis=1))
    for m in range(2):
        sum_re = sum_im = None
        for i in range(n):
            er = exit_grad[:PATCH, cols[2 * i + m]]
            ei = exit_grad[PATCH:, cols[2 * i + m]]
            o_re, o_im = patches[i]
            t_re = o_re * er + o_im * ei
            t_im = o_re * ei - o_im * er
            sum_re = t_re if sum_re is None else sum_re + t_re
            sum_im = t_im if sum_im is None else sum_im + t_im
        probe_sum[0, m] += sum_re
        probe_sum[1, m] += sum_im
    for i in range(n):
        g_re = g_im = None
        for m in range(2):
            er = exit_grad[:PATCH, cols[2 * i + m]]
            ei = exit_grad[PATCH:, cols[2 * i + m]]
            pr = probe[0, m]
            pi = probe[1, m]
            t_re = pr * er + pi * ei
            t_im = pr * ei - pi * er
            g_re = t_re if g_re is None else g_re + t_re
            g_im = t_im if g_im is None else g_im + t_im
        top, tile, shift, keep = places[i]
        for k, g in ((0, g_re), (1, g_im)):
            g = pltpu.roll(g, shift, 1)
            grad[tile, k, pl.ds(top, PATCH), :] += jnp.where(keep, g, 0.0)
            grad[tile + 1, k, pl.ds(top, PATCH), :] += jnp.where(keep, 0.0, g)


def fill_tables(waves, plus_ref, minus_ref):
    c = waves[0].astype(BF16)
    s = waves[1].astype(BF16)
    plus_ref[:PATCH, :PATCH] = c
    plus_ref[:PATCH, PATCH:] = s
    plus_ref[PATCH:, :PATCH] = -s
    plus_ref[PATCH:, PATCH:] = c
    minus_ref[:PATCH, :PATCH] = c
    minus_ref[:PATCH, PATCH:] = -s
    minus_ref[PATCH:, :PATCH] = s
    minus_ref[PATCH:, PATCH:] = c


def list_slots(wanted, pos, count, listed, photons, photon_buf, photon_sems):
    def list_step(s, found):
        chosen = wanted(pos[0, s])

        @pl.when(chosen)
        def _():
            listed[found] = s
            pltpu.make_async_copy(photons.at[s], photon_buf.at[found], photon_sems.at[found]).start()

        return found + chosen.astype(jnp.int32)

    return lax.fori_loop(0, count, list_step, jnp.int32(0))


def run_slots(found, pos, row_base, listed, field, grad, photons, photon_buf, photon_sems, probe, probe_sum,
              plus_ref, minus_ref):
    def step(k, carry, first=0, width=BLOCK):
        places = [first + k * width + i for i in range(width)]
        at = [jnp.minimum(p, found - 1) for p in places]
        slots = [listed[a] for a in at]
        valids = [jnp.where(p < found, 1.0, 0.0).astype(F32) for p in places]
        for p, a, s in zip(places, at, slots):
            @pl.when(p < found)
            def _(a=a, s=s):
                pltpu.make_async_copy(photons.at[s], photon_buf.at[a], photon_sems.at[a]).wait()

        slot_block(at, slots, valids, pos, row_base, field, grad, photon_buf, probe, probe_sum, plus_ref, minus_ref)
        return carry

    rest = found % BLOCK
    small = (rest > 0) & (rest <= BLOCK // 2)
    blocks = found // BLOCK + ((rest > 0) & jnp.logical_not(small)).astype(jnp.int32)
    lax.fori_loop(0, blocks, step, 0)

    @pl.when(small)
    def _():
        step(0, 0, blocks * BLOCK, BLOCK // 2)


def copies_of(pairs, sems):
    return [pltpu.make_async_copy(a, b, sems.at[i]) for i, (a, b) in enumerate(pairs)]


def start_all(copies):
    for c in copies:
        c.start()


def wait_all(copies):
    for c in copies:
        c.wait()


def by_tiles(array, tiles):
    return [array.at[:, :, pl.ds(t * PATCH, PATCH)] for t in range(tiles)]


def right_rim_kernel(own, right, right_buf, sems):
    load = pltpu.make_async_copy(own.at[:, :, pl.ds(0, PATCH)], right_buf, sems.at[0])
    load.start()
    load.wait()
    store = pltpu.make_async_copy(right_buf, right, sems.at[0])
    store.start()
    store.wait()


def below_rim_kernel(own, after, below, corner, below_buf, sems):
    rim = pl.ds(0, PATCH)
    load = pltpu.make_async_copy(own.at[:, rim, :], below_buf, sems.at[0])
    load.start()
    load.wait()
    stores = copies_of([(below_buf, below), (below_buf.at[:, :, rim], corner)], sems)
    start_all(stores)
    wait_all(stores)


def upper_kernel(pos, count, own, right, photons, probe_in, waves_in, g_own, g_top, g_bottom, probe_out,
                 field, grad, photon_buf, probe, waves, plus_ref, minus_ref, probe_sum, listed, sems, photon_sems):
    rows, cols = own.shape[1], own.shape[2]
    tiles = cols // PATCH
    loads = copies_of(
        [(waves_in, waves), (probe_in, probe)]
        + [(a, field.at[t]) for t, a in enumerate(by_tiles(own, tiles))]
        + [(right, field.at[tiles])],
        sems,
    )
    start_all(loads)
    found = list_slots(lambda top: top <= rows - PATCH, pos, count[0], listed, photons, photon_buf, photon_sems)
    grad[...] = jnp.zeros(grad.shape, F32)
    probe_sum[...] = jnp.zeros(probe_sum.shape, F32)
    loads[0].wait()
    fill_tables(waves, plus_ref, minus_ref)
    wait_all(loads[1:])
    run_slots(found, pos, 0, listed, field, grad, photons, photon_buf, photon_sems, probe, probe_sum,
              plus_ref, minus_ref)
    stores = copies_of(
        [(probe_sum, probe_out)]
        + [(grad.at[t], a) for t, a in enumerate(by_tiles(g_own, tiles))]
        + [(grad.at[tiles, :, pl.ds(0, rows - PATCH), :], g_top),
           (grad.at[tiles, :, pl.ds(rows - PATCH, PATCH), :], g_bottom)],
        sems,
    )
    start_all(stores)
    wait_all(stores)


def lower_kernel(scale, pos, count, own, right, below, corner, photons, probe_in, waves_in, own_in, bottom_in, sum_in,
                 g_own, g_bottom, g_below, g_corner, probe_out,
                 field, grad, photon_buf, probe, waves, plus_ref, minus_ref, probe_sum, listed, sems, photon_sems):
    rows, cols = own.shape[1], own.shape[2]
    tiles = cols // PATCH
    base = rows - PATCH
    last, upper, lower = pl.ds(base, PATCH), pl.ds(0, PATCH), pl.ds(PATCH, PATCH)

    def last_rows(array):
        return [array.at[:, last, pl.ds(t * PATCH, PATCH)] for t in range(tiles)]

    loads = copies_of(
        [(waves_in, waves), (probe_in, probe), (sum_in, probe_sum)]
        + [(a, field.at[t, :, upper, :]) for t, a in enumerate(last_rows(own) + [right.at[:, last, :]])]
        + [(a, field.at[t, :, lower, :]) for t, a in enumerate(by_tiles(below, tiles) + [corner])]
        + [(a, grad.at[t, :, upper, :]) for t, a in enumerate(last_rows(own_in) + [bottom_in])],
        sems,
    )
    start_all(loads)
    found = list_slots(lambda top: top > base, pos, count[0], listed, photons, photon_buf, photon_sems)
    for t in range(tiles + 1):
        grad[t, :, lower, :] = jnp.zeros((2, PATCH, PATCH), F32)
    loads[0].wait()
    fill_tables(waves, plus_ref, minus_ref)
    wait_all(loads[1:])
    run_slots(found, pos, base, listed, field, grad, photons, photon_buf, photon_sems, probe, probe_sum,
              plus_ref, minus_ref)
    probe_sum[...] = probe_sum[...] * scale
    stores = copies_of(
        [(probe_sum, probe_out)]
        + [(grad.at[t, :, lower, :], a) for t, a in enumerate(by_tiles(g_below, tiles) + [g_corner])]
        + [(grad.at[t, :, upper, :], a) for t, a in enumerate(last_rows(g_own) + [g_bottom])],
        sems,
    )
    start_all(stores)
    wait_all(stores)


def seam_kernel(grad_in, above, left_top, left_bottom, corner, parts, grad, probe,
                top_buf, left_buf, above_buf, beside_buf, corner_buf, probe_buf, sems):
    rows, cols = grad.shape[1], grad.shape[2]
    rest = rows - PATCH
    top_rim = grad.at[:, pl.ds(0, PATCH), :]
    left_rim = grad.at[:, pl.ds(PATCH, rest), pl.ds(0, PATCH)]
    loads = copies_of(
        [(top_rim, top_buf), (left_rim, left_buf), (above, above_buf), (corner, corner_buf),
         (left_top, beside_buf.at[:, pl.ds(0, rest), :]), (left_bottom, beside_buf.at[:, pl.ds(rest, PATCH), :]),
         (parts, probe_buf)],
        sems,
    )
    start_all(loads)
    wait_all(loads)
    join = pltpu.make_async_copy(probe_buf, probe, sems.at[2])
    join.start()
    top_buf[:, :, PATCH:] += above_buf[:, :, PATCH:]
    top_buf[:, :, :PATCH] += above_buf[:, :, :PATCH] + (beside_buf[:, :PATCH, :] + corner_buf[...])
    left_buf[...] += beside_buf[:, PATCH:, :]
    stores = copies_of([(top_buf, top_rim), (left_buf, left_rim)], sems)
    start_all(stores)
    wait_all(stores)
    join.wait()


def shape(*dims):
    return jax.ShapeDtypeStruct(dims, F32)


def everyone(value, axes, count):
    sent = jnp.broadcast_to(value[None], (count,) + value.shape)
    return lax.all_to_all(sent, axes, 0, 0, tiled=True)


def body(object_field, probe_modes, photons, positions, counts):
    rows, cols = object_field.shape[1], object_field.shape[2]
    slot_count = photons.shape[2]
    tiles = cols // PATCH
    n_row, n_col = lax.axis_size(ROW), lax.axis_size(COL)
    pos = positions[0, 0].T
    count = counts[0]
    photon_rows = photons[0, 0]
    waves = waves_of(PATCH)
    scale = 1.0 / math.sqrt(n_row * n_col * slot_count)
    down = [(i, i + 1) for i in range(n_row - 1)]
    along = [(i, i + 1) for i in range(n_col - 1)]
    up, back = ([(j, i) for i, j in pairs] for pairs in (down, along))
    diagonal = [
        (a * n_col + b, (a + 1) * n_col + b + 1) for a in range(n_row - 1) for b in range(n_col - 1)
    ]
    diagonal_back = [(j, i) for i, j in diagonal]
    smem = pl.BlockSpec(memory_space=pltpu.SMEM)
    hbm = pl.BlockSpec(memory_space=pl.ANY)
    params = pltpu.CompilerParams(vmem_limit_bytes=VMEM_LIMIT)
    small = pltpu.CompilerParams(vmem_limit_bytes=8 * 2**20)

    right = pl.pallas_call(
        right_rim_kernel,
        out_shape=shape(2, rows, PATCH),
        in_specs=[hbm],
        out_specs=hbm,
        scratch_shapes=[pltpu.VMEM((2, rows, PATCH), F32), pltpu.SemaphoreType.DMA((1,))],
        compiler_params=params,
        name="right_rim",
    )(object_field)
    below, corner = pl.pallas_call(
        below_rim_kernel,
        out_shape=(shape(2, PATCH, cols), shape(2, PATCH, PATCH)),
        in_specs=[hbm, hbm],
        out_specs=(hbm,) * 2,
        scratch_shapes=[pltpu.VMEM((2, PATCH, cols), F32), pltpu.SemaphoreType.DMA((2,))],
        compiler_params=params,
        name="below_rim",
    )(object_field, right)
    below = lax.ppermute(below, ROW, up)
    right = lax.ppermute(right, COL, back)
    corner = lax.ppermute(corner, BOTH, diagonal_back)

    def scratch(height):
        return [
            pltpu.VMEM((tiles + 1, 2, height, PATCH), F32),
            pltpu.VMEM((tiles + 1, 2, height, PATCH), F32),
            pltpu.VMEM(photon_rows.shape, BF16),
            pltpu.VMEM(probe_modes.shape, F32),
            pltpu.VMEM(waves.shape, F32),
            pltpu.VMEM((2 * PATCH, 2 * PATCH), BF16),
            pltpu.VMEM((2 * PATCH, 2 * PATCH), BF16),
            pltpu.VMEM(probe_modes.shape, F32),
            pltpu.SMEM((slot_count,), jnp.int32),
            pltpu.SemaphoreType.DMA((3 * tiles + 6,)),
            pltpu.SemaphoreType.DMA((slot_count,)),
        ]

    own_shape, probe_shape, rim_shape = shape(2, rows, cols), shape(*probe_modes.shape), shape(2, PATCH, PATCH)
    g_own, g_top, g_bottom, probe_1 = pl.pallas_call(
        upper_kernel,
        out_shape=(own_shape, shape(2, rows - PATCH, PATCH), rim_shape, probe_shape),
        in_specs=[smem, smem] + [hbm] * 5,
        out_specs=(hbm,) * 4,
        scratch_shapes=scratch(rows),
        compiler_params=params,
        cost_estimate=pl.CostEstimate(flops=10**9, bytes_accessed=2**20, transcendentals=0),
        name="upper_slots",
    )(pos, count, object_field, right, photon_rows, probe_modes, waves)
    left_top = lax.ppermute(g_top, COL, along)
    g_own, g_bottom, g_below, g_corner, probe_2 = pl.pallas_call(
        functools.partial(lower_kernel, scale),
        out_shape=(own_shape, rim_shape, shape(2, PATCH, cols), rim_shape, probe_shape),
        in_specs=[smem] * 2 + [hbm] * 10,
        out_specs=(hbm,) * 5,
        scratch_shapes=scratch(2 * PATCH),
        input_output_aliases={9: 0, 10: 1},
        compiler_params=params,
        cost_estimate=pl.CostEstimate(flops=2 * 10**10, bytes_accessed=2**20, transcendentals=0),
        name="lower_slots",
    )(pos, count, object_field, right, below, corner, photon_rows, probe_modes, waves, g_own, g_bottom, probe_1)

    plane, depth = lax.axis_size(PLANE), lax.axis_size(DEPTH)
    above = lax.ppermute(g_below, ROW, down)
    probe_2, left_top = lax.optimization_barrier((probe_2, left_top))
    shares = lax.all_to_all(probe_2.reshape(plane, -1, PATCH), PLANE, 0, 0, tiled=True)
    share = jnp.sum(shares, axis=0)
    share = jnp.sum(everyone(share, DEPTH, depth), axis=0)
    share, above, g_bottom, g_corner = lax.optimization_barrier((share, above, g_bottom, g_corner))
    left_bottom = lax.ppermute(g_bottom, COL, along)
    from_corner = lax.ppermute(g_corner, BOTH, diagonal)
    parts = everyone(share, PLANE, plane)

    object_gradient, probe_gradient = pl.pallas_call(
        seam_kernel,
        out_shape=(own_shape, shape(*parts.shape)),
        in_specs=[hbm] * 6,
        out_specs=(hbm, hbm),
        scratch_shapes=[
            pltpu.VMEM((2, PATCH, cols), F32),
            pltpu.VMEM((2, rows - PATCH, PATCH), F32),
            pltpu.VMEM((2, PATCH, cols), F32),
            pltpu.VMEM((2, rows, PATCH), F32),
            pltpu.VMEM((2, PATCH, PATCH), F32),
            pltpu.VMEM(parts.shape, F32),
            pltpu.SemaphoreType.DMA((8,)),
        ],
        input_output_aliases={0: 0},
        compiler_params=small,
        cost_estimate=pl.CostEstimate(flops=10**9, bytes_accessed=2**20, transcendentals=0),
        name="seams",
    )(g_own, above, left_top, left_bottom, from_corner, parts)
    return (object_gradient, probe_gradient.reshape(probe_modes.shape))


def solution(mesh):
    fine = Mesh(mesh.devices.reshape(4, 4, 4, 2, 2), BOTH)
    in_specs = (
        P(None, ROW, COL),
        P(),
        P(ROW, COL, None, None, None),
        P(ROW, COL, None, None),
        P(ROW, COL),
    )
    out_specs = (P(None, ROW, COL), P())
    return jax.shard_map(body, mesh=fine, in_specs=in_specs, out_specs=out_specs, check_vma=False)
```

```python
import functools
import math

import jax
import jax.numpy as jnp
import numpy as np
from jax import lax
from jax.experimental import pallas as pl
from jax.experimental.pallas import tpu as pltpu
from jax.sharding import Mesh
from jax.sharding import PartitionSpec as P

F32 = jnp.float32
BF16 = jnp.bfloat16
PATCH = 128
BLOCK = 8
VMEM_LIMIT = 63 * 2**20
ROW = "z_hi"
COL = ("x", "y", "z_lo", "core")
BOTH = (ROW,) + COL
PLANE = ("x", "y", "core")
DEPTH = ("z_hi", "z_lo")


def waves_of(patch_len):
    index_range = np.arange(patch_len)
    product = (index_range[:, None] * index_range[None, :]) % patch_len
    angle = product.astype(np.float32) * np.float32(2.0 * math.pi / patch_len)
    pair = np.stack([np.cos(angle), np.sin(angle)]) / np.float32(math.sqrt(patch_len))
    return jnp.asarray(pair, F32)


def dot(a, b):
    return jnp.dot(a, b, preferred_element_type=F32)


def slot_block(at, slots, valids, pos, row_base, field, grad, photons, probe, probe_sum, plus_ref, minus_ref):
    n = len(slots)
    lane = lax.broadcasted_iota(jnp.int32, (PATCH, PATCH), 1)
    plus = plus_ref[...]
    minus = minus_ref[...]
    places, patches, waves = [], [], []
    for s in slots:
        top = pos[0, s] - row_base
        left = pos[1, s]
        tile = left // PATCH
        shift = left % PATCH
        back = (PATCH - shift) % PATCH
        keep = lane >= shift
        patch = []
        for k in range(2):
            a = field[tile, k, pl.ds(top, PATCH), :]
            b = field[tile + 1, k, pl.ds(top, PATCH), :]
            patch.append(pltpu.roll(jnp.where(keep, a, b), back, 1))
        places.append((top, tile, shift, keep))
        patches.append(patch)
        for m in range(2):
            pr = probe[0, m]
            pi = probe[1, m]
            wr = (pr * patch[0] - pi * patch[1]).astype(BF16)
            wi = (pr * patch[1] + pi * patch[0]).astype(BF16)
            waves.append(jnp.concatenate([wr, wi], axis=0))
    first = dot(plus, jnp.concatenate(waves, axis=1)).astype(BF16)
    cols = [slice(q * PATCH, (q + 1) * PATCH) for q in range(2 * n)]
    turned = [jnp.concatenate([first[:PATCH, q], first[PATCH:, q]], axis=1) for q in cols]
    far = dot(jnp.concatenate(turned, axis=0), minus)
    scaled = []
    for i in range(n):
        f0 = far[2 * i * PATCH:(2 * i + 1) * PATCH]
        f1 = far[(2 * i + 1) * PATCH:(2 * i + 2) * PATCH]
        power = f0 * f0 + f1 * f1
        intensity = power[:, :PATCH] + power[:, PATCH:]
        factor = (1.0 - photons[at[i]].astype(F32) / (intensity + 1.0)) * valids[i]
        for f in (f0, f1):
            re = (f[:, :PATCH] * factor).astype(BF16)
            im = (f[:, PATCH:] * factor).astype(BF16)
            scaled.append(jnp.concatenate([re, im], axis=1))
    back_pass = dot(jnp.concatenate(scaled, axis=0), plus).astype(BF16)
    unturned = [jnp.concatenate([back_pass[q, :PATCH], back_pass[q, PATCH:]], axis=0) for q in cols]
    exit_grad = dot(minus, jnp.concatenate(unturned, axis=1))
    for m in range(2):
        sum_re = sum_im = None
        for i in range(n):
            er = exit_grad[:PATCH, cols[2 * i + m]]
            ei = exit_grad[PATCH:, cols[2 * i + m]]
            o_re, o_im = patches[i]
            t_re = o_re * er + o_im * ei
            t_im = o_re * ei - o_im * er
            sum_re = t_re if sum_re is None else sum_re + t_re
            sum_im = t_im if sum_im is None else sum_im + t_im
        probe_sum[0, m] += sum_re
        probe_sum[1, m] += sum_im
    for i in range(n):
        g_re = g_im = None
        for m in range(2):
            er = exit_grad[:PATCH, cols[2 * i + m]]
            ei = exit_grad[PATCH:, cols[2 * i + m]]
            pr = probe[0, m]
            pi = probe[1, m]
            t_re = pr * er + pi * ei
            t_im = pr * ei - pi * er
            g_re = t_re if g_re is None else g_re + t_re
            g_im = t_im if g_im is None else g_im + t_im
        top, tile, shift, keep = places[i]
        for k, g in ((0, g_re), (1, g_im)):
            g = pltpu.roll(g, shift, 1)
            grad[tile, k, pl.ds(top, PATCH), :] += jnp.where(keep, g, 0.0)
            grad[tile + 1, k, pl.ds(top, PATCH), :] += jnp.where(keep, 0.0, g)


def fill_tables(waves, plus_ref, minus_ref):
    c = waves[0].astype(BF16)
    s = waves[1].astype(BF16)
    plus_ref[:PATCH, :PATCH] = c
    plus_ref[:PATCH, PATCH:] = s
    plus_ref[PATCH:, :PATCH] = -s
    plus_ref[PATCH:, PATCH:] = c
    minus_ref[:PATCH, :PATCH] = c
    minus_ref[:PATCH, PATCH:] = -s
    minus_ref[PATCH:, :PATCH] = s
    minus_ref[PATCH:, PATCH:] = c


def list_slots(wanted, pos, count, listed, photons, photon_buf, photon_sems):
    def list_step(s, found):
        chosen = wanted(pos[0, s])

        @pl.when(chosen)
        def _():
            listed[found] = s
            pltpu.make_async_copy(photons.at[s], photon_buf.at[found], photon_sems.at[found]).start()

        return found + chosen.astype(jnp.int32)

    return lax.fori_loop(0, count, list_step, jnp.int32(0))


def run_slots(found, pos, row_base, listed, field, grad, photons, photon_buf, photon_sems, probe, probe_sum,
              plus_ref, minus_ref):
    def step(k, carry, first=0, width=BLOCK):
        places = [first + k * width + i for i in range(width)]
        at = [jnp.minimum(p, found - 1) for p in places]
        slots = [listed[a] for a in at]
        valids = [jnp.where(p < found, 1.0, 0.0).astype(F32) for p in places]
        for p, a, s in zip(places, at, slots):
            @pl.when(p < found)
            def _(a=a, s=s):
                pltpu.make_async_copy(photons.at[s], photon_buf.at[a], photon_sems.at[a]).wait()

        slot_block(at, slots, valids, pos, row_base, field, grad, photon_buf, probe, probe_sum, plus_ref, minus_ref)
        return carry

    rest = found % BLOCK
    small = (rest > 0) & (rest <= BLOCK // 2)
    blocks = found // BLOCK + ((rest > 0) & jnp.logical_not(small)).astype(jnp.int32)
    lax.fori_loop(0, blocks, step, 0)

    @pl.when(small)
    def _():
        step(0, 0, blocks * BLOCK, BLOCK // 2)


def copies_of(pairs, sems):
    return [pltpu.make_async_copy(a, b, sems.at[i]) for i, (a, b) in enumerate(pairs)]


def start_all(copies):
    for c in copies:
        c.start()


def wait_all(copies):
    for c in copies:
        c.wait()


def by_tiles(array, tiles):
    return [array.at[:, :, pl.ds(t * PATCH, PATCH)] for t in range(tiles)]


def right_rim_kernel(own, right, right_buf, sems):
    load = pltpu.make_async_copy(own.at[:, :, pl.ds(0, PATCH)], right_buf, sems.at[0])
    load.start()
    load.wait()
    store = pltpu.make_async_copy(right_buf, right, sems.at[0])
    store.start()
    store.wait()


def below_rim_kernel(own, after, below, corner, below_buf, sems):
    rim = pl.ds(0, PATCH)
    load = pltpu.make_async_copy(own.at[:, rim, :], below_buf, sems.at[0])
    load.start()
    load.wait()
    stores = copies_of([(below_buf, below), (below_buf.at[:, :, rim], corner)], sems)
    start_all(stores)
    wait_all(stores)


def upper_kernel(pos, count, own, right, photons, probe_in, waves_in, g_own, g_top, g_bottom, probe_out,
                 field, grad, photon_buf, probe, waves, plus_ref, minus_ref, probe_sum, listed, sems, photon_sems):
    rows, cols = own.shape[1], own.shape[2]
    tiles = cols // PATCH
    loads = copies_of(
        [(waves_in, waves), (probe_in, probe)]
        + [(a, field.at[t]) for t, a in enumerate(by_tiles(own, tiles))]
        + [(right, field.at[tiles])],
        sems,
    )
    start_all(loads)
    found = list_slots(lambda top: top <= rows - PATCH, pos, count[0], listed, photons, photon_buf, photon_sems)
    grad[...] = jnp.zeros(grad.shape, F32)
    probe_sum[...] = jnp.zeros(probe_sum.shape, F32)
    loads[0].wait()
    fill_tables(waves, plus_ref, minus_ref)
    wait_all(loads[1:])
    run_slots(found, pos, 0, listed, field, grad, photons, photon_buf, photon_sems, probe, probe_sum,
              plus_ref, minus_ref)
    stores = copies_of(
        [(probe_sum, probe_out)]
        + [(grad.at[t], a) for t, a in enumerate(by_tiles(g_own, tiles))]
        + [(grad.at[tiles, :, pl.ds(0, rows - PATCH), :], g_top),
           (grad.at[tiles, :, pl.ds(rows - PATCH, PATCH), :], g_bottom)],
        sems,
    )
    start_all(stores)
    wait_all(stores)


def lower_kernel(scale, pos, count, own, right, below, corner, photons, probe_in, waves_in, own_in, bottom_in, sum_in,
                 g_own, g_bottom, g_below, g_corner, probe_out,
                 field, grad, photon_buf, probe, waves, plus_ref, minus_ref, probe_sum, listed, sems, photon_sems):
    rows, cols = own.shape[1], own.shape[2]
    tiles = cols // PATCH
    base = rows - PATCH
    last, upper, lower = pl.ds(base, PATCH), pl.ds(0, PATCH), pl.ds(PATCH, PATCH)

    def last_rows(array):
        return [array.at[:, last, pl.ds(t * PATCH, PATCH)] for t in range(tiles)]

    loads = copies_of(
        [(waves_in, waves), (probe_in, probe), (sum_in, probe_sum)]
        + [(a, field.at[t, :, upper, :]) for t, a in enumerate(last_rows(own) + [right.at[:, last, :]])]
        + [(a, field.at[t, :, lower, :]) for t, a in enumerate(by_tiles(below, tiles) + [corner])]
        + [(a, grad.at[t, :, upper, :]) for t, a in enumerate(last_rows(own_in) + [bottom_in])],
        sems,
    )
    start_all(loads)
    found = list_slots(lambda top: top > base, pos, count[0], listed, photons, photon_buf, photon_sems)
    for t in range(tiles + 1):
        grad[t, :, lower, :] = jnp.zeros((2, PATCH, PATCH), F32)
    loads[0].wait()
    fill_tables(waves, plus_ref, minus_ref)
    wait_all(loads[1:])
    run_slots(found, pos, base, listed, field, grad, photons, photon_buf, photon_sems, probe, probe_sum,
              plus_ref, minus_ref)
    probe_sum[...] = probe_sum[...] * scale
    stores = copies_of(
        [(probe_sum, probe_out)]
        + [(grad.at[t, :, lower, :], a) for t, a in enumerate(by_tiles(g_below, tiles) + [g_corner])]
        + [(grad.at[t, :, upper, :], a) for t, a in enumerate(last_rows(g_own) + [g_bottom])],
        sems,
    )
    start_all(stores)
    wait_all(stores)


def seam_kernel(grad_in, above, left_top, left_bottom, corner, parts, grad, probe,
                top_buf, left_buf, above_buf, beside_buf, corner_buf, probe_buf, sems):
    rows, cols = grad.shape[1], grad.shape[2]
    rest = rows - PATCH
    top_rim = grad.at[:, pl.ds(0, PATCH), :]
    left_rim = grad.at[:, pl.ds(PATCH, rest), pl.ds(0, PATCH)]
    loads = copies_of(
        [(top_rim, top_buf), (left_rim, left_buf), (above, above_buf), (corner, corner_buf),
         (left_top, beside_buf.at[:, pl.ds(0, rest), :]), (left_bottom, beside_buf.at[:, pl.ds(rest, PATCH), :]),
         (parts, probe_buf)],
        sems,
    )
    start_all(loads)
    wait_all(loads)
    join = pltpu.make_async_copy(probe_buf, probe, sems.at[2])
    join.start()
    top_buf[:, :, PATCH:] += above_buf[:, :, PATCH:]
    top_buf[:, :, :PATCH] += above_buf[:, :, :PATCH] + (beside_buf[:, :PATCH, :] + corner_buf[...])
    left_buf[...] += beside_buf[:, PATCH:, :]
    stores = copies_of([(top_buf, top_rim), (left_buf, left_rim)], sems)
    start_all(stores)
    wait_all(stores)
    join.wait()


def shape(*dims):
    return jax.ShapeDtypeStruct(dims, F32)


def everyone(value, axes, count):
    sent = jnp.broadcast_to(value[None], (count,) + value.shape)
    return lax.all_to_all(sent, axes, 0, 0, tiled=True)


def body(object_field, probe_modes, photons, positions, counts):
    rows, cols = object_field.shape[1], object_field.shape[2]
    slot_count = photons.shape[2]
    tiles = cols // PATCH
    n_row, n_col = lax.axis_size(ROW), lax.axis_size(COL)
    pos = positions[0, 0].T
    count = counts[0]
    photon_rows = photons[0, 0]
    waves = waves_of(PATCH)
    scale = 1.0 / math.sqrt(n_row * n_col * slot_count)
    down = [(i, i + 1) for i in range(n_row - 1)]
    along = [(i, i + 1) for i in range(n_col - 1)]
    up, back = ([(j, i) for i, j in pairs] for pairs in (down, along))
    diagonal = [
        (a * n_col + b, (a + 1) * n_col + b + 1) for a in range(n_row - 1) for b in range(n_col - 1)
    ]
    diagonal_back = [(j, i) for i, j in diagonal]
    smem = pl.BlockSpec(memory_space=pltpu.SMEM)
    hbm = pl.BlockSpec(memory_space=pl.ANY)
    params = pltpu.CompilerParams(vmem_limit_bytes=VMEM_LIMIT)
    small = pltpu.CompilerParams(vmem_limit_bytes=8 * 2**20)

    right = pl.pallas_call(
        right_rim_kernel,
        out_shape=shape(2, rows, PATCH),
        in_specs=[hbm],
        out_specs=hbm,
        scratch_shapes=[pltpu.VMEM((2, rows, PATCH), F32), pltpu.SemaphoreType.DMA((1,))],
        compiler_params=params,
        name="right_rim",
    )(object_field)
    below, corner = pl.pallas_call(
        below_rim_kernel,
        out_shape=(shape(2, PATCH, cols), shape(2, PATCH, PATCH)),
        in_specs=[hbm, hbm],
        out_specs=(hbm,) * 2,
        scratch_shapes=[pltpu.VMEM((2, PATCH, cols), F32), pltpu.SemaphoreType.DMA((2,))],
        compiler_params=params,
        name="below_rim",
    )(object_field, right)
    below = lax.ppermute(below, ROW, up)
    right = lax.ppermute(right, COL, back)
    corner = lax.ppermute(corner, BOTH, diagonal_back)

    def scratch(height):
        return [
            pltpu.VMEM((tiles + 1, 2, height, PATCH), F32),
            pltpu.VMEM((tiles + 1, 2, height, PATCH), F32),
            pltpu.VMEM(photon_rows.shape, BF16),
            pltpu.VMEM(probe_modes.shape, F32),
            pltpu.VMEM(waves.shape, F32),
            pltpu.VMEM((2 * PATCH, 2 * PATCH), BF16),
            pltpu.VMEM((2 * PATCH, 2 * PATCH), BF16),
            pltpu.VMEM(probe_modes.shape, F32),
            pltpu.SMEM((slot_count,), jnp.int32),
            pltpu.SemaphoreType.DMA((3 * tiles + 6,)),
            pltpu.SemaphoreType.DMA((slot_count,)),
        ]

    own_shape, probe_shape, rim_shape = shape(2, rows, cols), shape(*probe_modes.shape), shape(2, PATCH, PATCH)
    g_own, g_top, g_bottom, probe_1 = pl.pallas_call(
        upper_kernel,
        out_shape=(own_shape, shape(2, rows - PATCH, PATCH), rim_shape, probe_shape),
        in_specs=[smem, smem] + [hbm] * 5,
        out_specs=(hbm,) * 4,
        scratch_shapes=scratch(rows),
        compiler_params=params,
        cost_estimate=pl.CostEstimate(flops=10**9, bytes_accessed=2**20, transcendentals=0),
        name="upper_slots",
    )(pos, count, object_field, right, photon_rows, probe_modes, waves)
    left_top = lax.ppermute(g_top, COL, along)
    g_own, g_bottom, g_below, g_corner, probe_2 = pl.pallas_call(
        functools.partial(lower_kernel, scale),
        out_shape=(own_shape, rim_shape, shape(2, PATCH, cols), rim_shape, probe_shape),
        in_specs=[smem] * 2 + [hbm] * 10,
        out_specs=(hbm,) * 5,
        scratch_shapes=scratch(2 * PATCH),
        input_output_aliases={9: 0, 10: 1},
        compiler_params=params,
        cost_estimate=pl.CostEstimate(flops=2 * 10**10, bytes_accessed=2**20, transcendentals=0),
        name="lower_slots",
    )(pos, count, object_field, right, below, corner, photon_rows, probe_modes, waves, g_own, g_bottom, probe_1)

    plane, depth = lax.axis_size(PLANE), lax.axis_size(DEPTH)
    above = lax.ppermute(g_below, ROW, down)
    probe_2, left_top = lax.optimization_barrier((probe_2, left_top))
    shares = lax.all_to_all(probe_2.reshape(plane, -1, PATCH), PLANE, 0, 0, tiled=True)
    share = jnp.sum(shares, axis=0)
    left_bottom = lax.ppermute(g_bottom, COL, along)
    share, left_bottom = lax.optimization_barrier((share, left_bottom))
    share = jnp.sum(everyone(share, DEPTH, depth), axis=0)
    share, above, g_corner = lax.optimization_barrier((share, above, g_corner))
    from_corner = lax.ppermute(g_corner, BOTH, diagonal)
    parts = everyone(share, PLANE, plane)

    object_gradient, probe_gradient = pl.pallas_call(
        seam_kernel,
        out_shape=(own_shape, shape(*parts.shape)),
        in_specs=[hbm] * 6,
        out_specs=(hbm, hbm),
        scratch_shapes=[
            pltpu.VMEM((2, PATCH, cols), F32),
            pltpu.VMEM((2, rows - PATCH, PATCH), F32),
            pltpu.VMEM((2, PATCH, cols), F32),
            pltpu.VMEM((2, rows, PATCH), F32),
            pltpu.VMEM((2, PATCH, PATCH), F32),
            pltpu.VMEM(parts.shape, F32),
            pltpu.SemaphoreType.DMA((8,)),
        ],
        input_output_aliases={0: 0},
        compiler_params=small,
        cost_estimate=pl.CostEstimate(flops=10**9, bytes_accessed=2**20, transcendentals=0),
        name="seams",
    )(g_own, above, left_top, left_bottom, from_corner, parts)
    return (object_gradient, probe_gradient.reshape(probe_modes.shape))


def solution(mesh):
    fine = Mesh(mesh.devices.reshape(4, 4, 4, 2, 2), BOTH)
    in_specs = (
        P(None, ROW, COL),
        P(),
        P(ROW, COL, None, None, None),
        P(ROW, COL, None, None),
        P(ROW, COL),
    )
    out_specs = (P(None, ROW, COL), P())
    return jax.shard_map(body, mesh=fine, in_specs=in_specs, out_specs=out_specs, check_vma=False)
```

```python
import functools
import math

import jax
import jax.numpy as jnp
import numpy as np
from jax import lax
from jax.experimental import pallas as pl
from jax.experimental.pallas import tpu as pltpu
from jax.sharding import Mesh
from jax.sharding import PartitionSpec as P

F32 = jnp.float32
BF16 = jnp.bfloat16
PATCH = 128
BLOCK = 8
VMEM_LIMIT = 63 * 2**20
ROW = "z_hi"
COL = ("x", "y", "z_lo", "core")
BOTH = (ROW,) + COL
PLANE = ("x", "y", "core")
DEPTH = ("z_hi", "z_lo")


def waves_of(patch_len):
    index_range = np.arange(patch_len)
    product = (index_range[:, None] * index_range[None, :]) % patch_len
    angle = product.astype(np.float32) * np.float32(2.0 * math.pi / patch_len)
    pair = np.stack([np.cos(angle), np.sin(angle)]) / np.float32(math.sqrt(patch_len))
    return jnp.asarray(pair, F32)


def dot(a, b):
    return jnp.dot(a, b, preferred_element_type=F32)


def slot_block(at, slots, valids, pos, row_base, field, grad, photons, probe, probe_sum, plus_ref, minus_ref):
    n = len(slots)
    lane = lax.broadcasted_iota(jnp.int32, (PATCH, PATCH), 1)
    plus = plus_ref[...]
    minus = minus_ref[...]
    places, patches, waves = [], [], []
    for s in slots:
        top = pos[0, s] - row_base
        left = pos[1, s]
        tile = left // PATCH
        shift = left % PATCH
        back = (PATCH - shift) % PATCH
        keep = lane >= shift
        patch = []
        for k in range(2):
            a = field[tile, k, pl.ds(top, PATCH), :]
            b = field[tile + 1, k, pl.ds(top, PATCH), :]
            patch.append(pltpu.roll(jnp.where(keep, a, b), back, 1))
        places.append((top, tile, shift, keep))
        patches.append(patch)
        for m in range(2):
            pr = probe[0, m]
            pi = probe[1, m]
            wr = (pr * patch[0] - pi * patch[1]).astype(BF16)
            wi = (pr * patch[1] + pi * patch[0]).astype(BF16)
            waves.append(jnp.concatenate([wr, wi], axis=0))
    first = dot(plus, jnp.concatenate(waves, axis=1)).astype(BF16)
    cols = [slice(q * PATCH, (q + 1) * PATCH) for q in range(2 * n)]
    turned = [jnp.concatenate([first[:PATCH, q], first[PATCH:, q]], axis=1) for q in cols]
    far = dot(jnp.concatenate(turned, axis=0), minus)
    scaled = []
    for i in range(n):
        f0 = far[2 * i * PATCH:(2 * i + 1) * PATCH]
        f1 = far[(2 * i + 1) * PATCH:(2 * i + 2) * PATCH]
        power = f0 * f0 + f1 * f1
        intensity = power[:, :PATCH] + power[:, PATCH:]
        factor = (1.0 - photons[at[i]].astype(F32) / (intensity + 1.0)) * valids[i]
        for f in (f0, f1):
            re = (f[:, :PATCH] * factor).astype(BF16)
            im = (f[:, PATCH:] * factor).astype(BF16)
            scaled.append(jnp.concatenate([re, im], axis=1))
    back_pass = dot(jnp.concatenate(scaled, axis=0), plus).astype(BF16)
    unturned = [jnp.concatenate([back_pass[q, :PATCH], back_pass[q, PATCH:]], axis=0) for q in cols]
    exit_grad = dot(minus, jnp.concatenate(unturned, axis=1))
    for m in range(2):
        sum_re = sum_im = None
        for i in range(n):
            er = exit_grad[:PATCH, cols[2 * i + m]]
            ei = exit_grad[PATCH:, cols[2 * i + m]]
            o_re, o_im = patches[i]
            t_re = o_re * er + o_im * ei
            t_im = o_re * ei - o_im * er
            sum_re = t_re if sum_re is None else sum_re + t_re
            sum_im = t_im if sum_im is None else sum_im + t_im
        probe_sum[0, m] += sum_re
        probe_sum[1, m] += sum_im
    for i in range(n):
        g_re = g_im = None
        for m in range(2):
            er = exit_grad[:PATCH, cols[2 * i + m]]
            ei = exit_grad[PATCH:, cols[2 * i + m]]
            pr = probe[0, m]
            pi = probe[1, m]
            t_re = pr * er + pi * ei
            t_im = pr * ei - pi * er
            g_re = t_re if g_re is None else g_re + t_re
            g_im = t_im if g_im is None else g_im + t_im
        top, tile, shift, keep = places[i]
        for k, g in ((0, g_re), (1, g_im)):
            g = pltpu.roll(g, shift, 1)
            grad[tile, k, pl.ds(top, PATCH), :] += jnp.where(keep, g, 0.0)
            grad[tile + 1, k, pl.ds(top, PATCH), :] += jnp.where(keep, 0.0, g)


def fill_tables(waves, plus_ref, minus_ref):
    c = waves[0].astype(BF16)
    s = waves[1].astype(BF16)
    plus_ref[:PATCH, :PATCH] = c
    plus_ref[:PATCH, PATCH:] = s
    plus_ref[PATCH:, :PATCH] = -s
    plus_ref[PATCH:, PATCH:] = c
    minus_ref[:PATCH, :PATCH] = c
    minus_ref[:PATCH, PATCH:] = -s
    minus_ref[PATCH:, :PATCH] = s
    minus_ref[PATCH:, PATCH:] = c


def list_slots(wanted, pos, count, listed, photons, photon_buf, photon_sems):
    def list_step(s, found):
        chosen = wanted(pos[0, s])

        @pl.when(chosen)
        def _():
            listed[found] = s
            pltpu.make_async_copy(photons.at[s], photon_buf.at[found], photon_sems.at[found]).start()

        return found + chosen.astype(jnp.int32)

    return lax.fori_loop(0, count, list_step, jnp.int32(0))


def run_slots(found, pos, row_base, listed, field, grad, photons, photon_buf, photon_sems, probe, probe_sum,
              plus_ref, minus_ref):
    def step(k, carry, first=0, width=BLOCK):
        places = [first + k * width + i for i in range(width)]
        at = [jnp.minimum(p, found - 1) for p in places]
        slots = [listed[a] for a in at]
        valids = [jnp.where(p < found, 1.0, 0.0).astype(F32) for p in places]
        for p, a, s in zip(places, at, slots):
            @pl.when(p < found)
            def _(a=a, s=s):
                pltpu.make_async_copy(photons.at[s], photon_buf.at[a], photon_sems.at[a]).wait()

        slot_block(at, slots, valids, pos, row_base, field, grad, photon_buf, probe, probe_sum, plus_ref, minus_ref)
        return carry

    rest = found % BLOCK
    small = (rest > 0) & (rest <= BLOCK // 2)
    blocks = found // BLOCK + ((rest > 0) & jnp.logical_not(small)).astype(jnp.int32)
    lax.fori_loop(0, blocks, step, 0)

    @pl.when(small)
    def _():
        step(0, 0, blocks * BLOCK, BLOCK // 2)


def copies_of(pairs, sems):
    return [pltpu.make_async_copy(a, b, sems.at[i]) for i, (a, b) in enumerate(pairs)]


def start_all(copies):
    for c in copies:
        c.start()


def wait_all(copies):
    for c in copies:
        c.wait()


def by_tiles(array, tiles):
    return [array.at[:, :, pl.ds(t * PATCH, PATCH)] for t in range(tiles)]


def right_rim_kernel(own, right, right_buf, sems):
    load = pltpu.make_async_copy(own.at[:, :, pl.ds(0, PATCH)], right_buf, sems.at[0])
    load.start()
    load.wait()
    store = pltpu.make_async_copy(right_buf, right, sems.at[0])
    store.start()
    store.wait()


def below_rim_kernel(own, after, below, corner, below_buf, sems):
    rim = pl.ds(0, PATCH)
    load = pltpu.make_async_copy(own.at[:, rim, :], below_buf, sems.at[0])
    load.start()
    load.wait()
    stores = copies_of([(below_buf, below), (below_buf.at[:, :, rim], corner)], sems)
    start_all(stores)
    wait_all(stores)


def upper_kernel(pos, count, own, right, photons, probe_in, waves_in, g_own, g_top, g_bottom, probe_out,
                 field, grad, photon_buf, probe, waves, plus_ref, minus_ref, probe_sum, listed, sems, photon_sems):
    rows, cols = own.shape[1], own.shape[2]
    tiles = cols // PATCH
    loads = copies_of(
        [(waves_in, waves), (probe_in, probe)]
        + [(a, field.at[t]) for t, a in enumerate(by_tiles(own, tiles))]
        + [(right, field.at[tiles])],
        sems,
    )
    start_all(loads)
    found = list_slots(lambda top: top <= rows - PATCH, pos, count[0], listed, photons, photon_buf, photon_sems)
    grad[...] = jnp.zeros(grad.shape, F32)
    probe_sum[...] = jnp.zeros(probe_sum.shape, F32)
    loads[0].wait()
    fill_tables(waves, plus_ref, minus_ref)
    wait_all(loads[1:])
    run_slots(found, pos, 0, listed, field, grad, photons, photon_buf, photon_sems, probe, probe_sum,
              plus_ref, minus_ref)
    stores = copies_of(
        [(probe_sum, probe_out)]
        + [(grad.at[t], a) for t, a in enumerate(by_tiles(g_own, tiles))]
        + [(grad.at[tiles, :, pl.ds(0, rows - PATCH), :], g_top),
           (grad.at[tiles, :, pl.ds(rows - PATCH, PATCH), :], g_bottom)],
        sems,
    )
    start_all(stores)
    wait_all(stores)


def lower_kernel(scale, pos, count, own, right, below, corner, photons, probe_in, waves_in, own_in, bottom_in, sum_in,
                 g_own, g_bottom, g_below, g_corner, probe_out,
                 field, grad, photon_buf, probe, waves, plus_ref, minus_ref, probe_sum, listed, sems, photon_sems):
    rows, cols = own.shape[1], own.shape[2]
    tiles = cols // PATCH
    base = rows - PATCH
    last, upper, lower = pl.ds(base, PATCH), pl.ds(0, PATCH), pl.ds(PATCH, PATCH)

    def last_rows(array):
        return [array.at[:, last, pl.ds(t * PATCH, PATCH)] for t in range(tiles)]

    loads = copies_of(
        [(waves_in, waves), (probe_in, probe), (sum_in, probe_sum)]
        + [(a, field.at[t, :, upper, :]) for t, a in enumerate(last_rows(own) + [right.at[:, last, :]])]
        + [(a, field.at[t, :, lower, :]) for t, a in enumerate(by_tiles(below, tiles) + [corner])]
        + [(a, grad.at[t, :, upper, :]) for t, a in enumerate(last_rows(own_in) + [bottom_in])],
        sems,
    )
    start_all(loads)
    found = list_slots(lambda top: top > base, pos, count[0], listed, photons, photon_buf, photon_sems)
    for t in range(tiles + 1):
        grad[t, :, lower, :] = jnp.zeros((2, PATCH, PATCH), F32)
    loads[0].wait()
    fill_tables(waves, plus_ref, minus_ref)
    wait_all(loads[1:])
    run_slots(found, pos, base, listed, field, grad, photons, photon_buf, photon_sems, probe, probe_sum,
              plus_ref, minus_ref)
    probe_sum[...] = probe_sum[...] * scale
    stores = copies_of(
        [(probe_sum, probe_out)]
        + [(grad.at[t, :, lower, :], a) for t, a in enumerate(by_tiles(g_below, tiles) + [g_corner])]
        + [(grad.at[t, :, upper, :], a) for t, a in enumerate(last_rows(g_own) + [g_bottom])],
        sems,
    )
    start_all(stores)
    wait_all(stores)


def seam_kernel(grad_in, above, left_top, left_bottom, corner, parts, grad, probe,
                top_buf, left_buf, above_buf, beside_buf, corner_buf, probe_buf, sems):
    rows, cols = grad.shape[1], grad.shape[2]
    rest = rows - PATCH
    top_rim = grad.at[:, pl.ds(0, PATCH), :]
    left_rim = grad.at[:, pl.ds(PATCH, rest), pl.ds(0, PATCH)]
    loads = copies_of(
        [(top_rim, top_buf), (left_rim, left_buf), (above, above_buf), (corner, corner_buf),
         (left_top, beside_buf.at[:, pl.ds(0, rest), :]), (left_bottom, beside_buf.at[:, pl.ds(rest, PATCH), :]),
         (parts, probe_buf)],
        sems,
    )
    start_all(loads)
    wait_all(loads)
    join = pltpu.make_async_copy(probe_buf, probe, sems.at[2])
    join.start()
    top_buf[:, :, PATCH:] += above_buf[:, :, PATCH:]
    top_buf[:, :, :PATCH] += above_buf[:, :, :PATCH] + (beside_buf[:, :PATCH, :] + corner_buf[...])
    left_buf[...] += beside_buf[:, PATCH:, :]
    stores = copies_of([(top_buf, top_rim), (left_buf, left_rim)], sems)
    start_all(stores)
    wait_all(stores)
    join.wait()


def shape(*dims):
    return jax.ShapeDtypeStruct(dims, F32)


def everyone(value, axes, count):
    sent = jnp.broadcast_to(value[None], (count,) + value.shape)
    return lax.all_to_all(sent, axes, 0, 0, tiled=True)


def body(object_field, probe_modes, photons, positions, counts):
    rows, cols = object_field.shape[1], object_field.shape[2]
    slot_count = photons.shape[2]
    tiles = cols // PATCH
    n_row, n_col = lax.axis_size(ROW), lax.axis_size(COL)
    pos = positions[0, 0].T
    count = counts[0]
    photon_rows = photons[0, 0]
    waves = waves_of(PATCH)
    scale = 1.0 / math.sqrt(n_row * n_col * slot_count)
    down = [(i, i + 1) for i in range(n_row - 1)]
    along = [(i, i + 1) for i in range(n_col - 1)]
    up, back = ([(j, i) for i, j in pairs] for pairs in (down, along))
    diagonal = [
        (a * n_col + b, (a + 1) * n_col + b + 1) for a in range(n_row - 1) for b in range(n_col - 1)
    ]
    diagonal_back = [(j, i) for i, j in diagonal]
    smem = pl.BlockSpec(memory_space=pltpu.SMEM)
    hbm = pl.BlockSpec(memory_space=pl.ANY)
    params = pltpu.CompilerParams(vmem_limit_bytes=VMEM_LIMIT)
    small = pltpu.CompilerParams(vmem_limit_bytes=8 * 2**20)

    right = pl.pallas_call(
        right_rim_kernel,
        out_shape=shape(2, rows, PATCH),
        in_specs=[hbm],
        out_specs=hbm,
        scratch_shapes=[pltpu.VMEM((2, rows, PATCH), F32), pltpu.SemaphoreType.DMA((1,))],
        compiler_params=params,
        name="right_rim",
    )(object_field)
    below, corner = pl.pallas_call(
        below_rim_kernel,
        out_shape=(shape(2, PATCH, cols), shape(2, PATCH, PATCH)),
        in_specs=[hbm, hbm],
        out_specs=(hbm,) * 2,
        scratch_shapes=[pltpu.VMEM((2, PATCH, cols), F32), pltpu.SemaphoreType.DMA((2,))],
        compiler_params=params,
        name="below_rim",
    )(object_field, right)
    below = lax.ppermute(below, ROW, up)
    right = lax.ppermute(right, COL, back)
    corner = lax.ppermute(corner, BOTH, diagonal_back)

    def scratch(height):
        return [
            pltpu.VMEM((tiles + 1, 2, height, PATCH), F32),
            pltpu.VMEM((tiles + 1, 2, height, PATCH), F32),
            pltpu.VMEM(photon_rows.shape, BF16),
            pltpu.VMEM(probe_modes.shape, F32),
            pltpu.VMEM(waves.shape, F32),
            pltpu.VMEM((2 * PATCH, 2 * PATCH), BF16),
            pltpu.VMEM((2 * PATCH, 2 * PATCH), BF16),
            pltpu.VMEM(probe_modes.shape, F32),
            pltpu.SMEM((slot_count,), jnp.int32),
            pltpu.SemaphoreType.DMA((3 * tiles + 6,)),
            pltpu.SemaphoreType.DMA((slot_count,)),
        ]

    own_shape, probe_shape, rim_shape = shape(2, rows, cols), shape(*probe_modes.shape), shape(2, PATCH, PATCH)
    g_own, g_top, g_bottom, probe_1 = pl.pallas_call(
        upper_kernel,
        out_shape=(own_shape, shape(2, rows - PATCH, PATCH), rim_shape, probe_shape),
        in_specs=[smem, smem] + [hbm] * 5,
        out_specs=(hbm,) * 4,
        scratch_shapes=scratch(rows),
        compiler_params=params,
        cost_estimate=pl.CostEstimate(flops=10**9, bytes_accessed=2**20, transcendentals=0),
        name="upper_slots",
    )(pos, count, object_field, right, photon_rows, probe_modes, waves)
    left_top = lax.ppermute(g_top, COL, along)
    g_own, g_bottom, g_below, g_corner, probe_2 = pl.pallas_call(
        functools.partial(lower_kernel, scale),
        out_shape=(own_shape, rim_shape, shape(2, PATCH, cols), rim_shape, probe_shape),
        in_specs=[smem] * 2 + [hbm] * 10,
        out_specs=(hbm,) * 5,
        scratch_shapes=scratch(2 * PATCH),
        input_output_aliases={9: 0, 10: 1},
        compiler_params=params,
        cost_estimate=pl.CostEstimate(flops=2 * 10**10, bytes_accessed=2**20, transcendentals=0),
        name="lower_slots",
    )(pos, count, object_field, right, below, corner, photon_rows, probe_modes, waves, g_own, g_bottom, probe_1)

    plane, depth = lax.axis_size(PLANE), lax.axis_size(DEPTH)
    above = lax.ppermute(g_below, ROW, down)
    probe_2, left_top = lax.optimization_barrier((probe_2, left_top))
    shares = lax.all_to_all(probe_2.reshape(plane, -1, PATCH), PLANE, 0, 0, tiled=True)
    share = jnp.sum(shares, axis=0)
    share = jnp.sum(everyone(share, DEPTH, depth), axis=0)
    share, above, g_bottom, g_corner = lax.optimization_barrier((share, above, g_bottom, g_corner))
    from_corner = lax.ppermute(g_corner, BOTH, diagonal)
    left_bottom = lax.ppermute(g_bottom, COL, along)
    parts = everyone(share, PLANE, plane)

    object_gradient, probe_gradient = pl.pallas_call(
        seam_kernel,
        out_shape=(own_shape, shape(*parts.shape)),
        in_specs=[hbm] * 6,
        out_specs=(hbm, hbm),
        scratch_shapes=[
            pltpu.VMEM((2, PATCH, cols), F32),
            pltpu.VMEM((2, rows - PATCH, PATCH), F32),
            pltpu.VMEM((2, PATCH, cols), F32),
            pltpu.VMEM((2, rows, PATCH), F32),
            pltpu.VMEM((2, PATCH, PATCH), F32),
            pltpu.VMEM(parts.shape, F32),
            pltpu.SemaphoreType.DMA((8,)),
        ],
        input_output_aliases={0: 0},
        compiler_params=small,
        cost_estimate=pl.CostEstimate(flops=10**9, bytes_accessed=2**20, transcendentals=0),
        name="seams",
    )(g_own, above, left_top, left_bottom, from_corner, parts)
    return (object_gradient, probe_gradient.reshape(probe_modes.shape))


def solution(mesh):
    fine = Mesh(mesh.devices.reshape(4, 4, 4, 2, 2), BOTH)
    in_specs = (
        P(None, ROW, COL),
        P(),
        P(ROW, COL, None, None, None),
        P(ROW, COL, None, None),
        P(ROW, COL),
    )
    out_specs = (P(None, ROW, COL), P())
    return jax.shard_map(body, mesh=fine, in_specs=in_specs, out_specs=out_specs, check_vma=False)
```
